256 devices in a mesh: gx: 16 (over z, core), gy: 16 (over x, y).
Axes of the slice: x: 4, y: 4, z: 8, core: 2. Of those that a mesh axis runs over, the one named last changes fastest.
Arguments:
- ensemble: float32 [128, 384, 2048], P('gx', 'gy'), may hold values from -6 to 6
- weights: float32 [4, 128, 12288], P(None, 'gx', 'gy'), may hold values from 0.02 to 0.22
- obs_cell: int32 [3, 512], replicated, may hold values from 0 to 383, as said below
- obs_batch: int32 [512], replicated, may hold values from 0 to 3, as said below
- obs_radius: int32 [512], replicated, may hold values from 24 to 48
- obs_value: float32 [512], replicated, may hold values from -8 to 8
- obs_noise: float32 [64, 512], replicated, may hold values from -6 to 6
- obs_var: float32 [512], replicated, may hold values from 0.25 to 1
Outputs:
- analysis: float32 [128, 384, 2048], P('gx', 'gy')
The draws below stay inside these ranges and needn't reach their ends.
Inputs may be any that keep to these rules, and one draw needn't show every extreme that they name: `obs_cell`: row 0 is an x below 128, row 1 a y below 384, row 2 a level below 32; observations cluster in a few regions. `obs_batch`: each batch number occurs exactly 128 times.
All inputs are finite; a program needn't handle non-finite values.
Results may differ from the reference program's by a relative error of at most 0.0003.
Values sent between devices are 32-bit elements; how exact they have to be, the bound alone decides.
A program may use at most 128 MiB of HBM per device.

```python
import math
import jax
import jax.numpy as jnp
from jax import lax

MEM = 64
LEV = 32
CX = 8
CY = 24
OBS_B = 128
NBATCH = 4
NOBS = 512
NX = 128
NY = 384
N_GX = 16


def draw_ensemble(key, part):
    base = jax.random.fold_in(key, 37)
    keys = jax.random.split(base, 3)
    mode_count = max(2, 3 * MEM // 4)
    decay_rate = 0.03 ** (1.0 / (mode_count - 1))
    amplitudes = 0.7 * jnp.power(jnp.float32(decay_rate), jnp.arange(mode_count).astype(jnp.float32))
    member_coeffs = jax.random.normal(keys[0], (mode_count, MEM), jnp.float32)
    scaled_coeffs = amplitudes[:, None] * member_coeffs
    start_field = 0.05 * jax.random.normal(keys[1], (NX, NY, LEV, MEM), jnp.float32)

    def add_mode(index, total):
        mode_key = jax.random.fold_in(keys[2], index)
        field = jax.random.normal(mode_key, (NX, NY, LEV, 1), jnp.float32)
        row = lax.dynamic_slice_in_dim(scaled_coeffs, index, 1, 0).reshape(1, 1, 1, MEM)
        return total + field * row
    total = lax.fori_loop(0, mode_count, add_mode, start_field)
    return jnp.clip(total, -6.0, 6.0).reshape(NX, NY, LEV * MEM).astype(jnp.float32)


def draw_obs_cell(key, part):
    base = jax.random.fold_in(key, 11)
    keys = jax.random.split(base, 9)
    spread = max(CX, CY)
    drawn_x = jax.random.randint(keys[0], (NOBS,), 0, NX, dtype=jnp.int32)
    drawn_y = jax.random.randint(keys[1], (NOBS,), 0, NY, dtype=jnp.int32)
    centre_x = jax.random.randint(keys[2], (8,), 0, NX, dtype=jnp.int32)
    centre_y = jax.random.randint(keys[3], (8,), 0, NY, dtype=jnp.int32)
    picked = jax.random.randint(keys[4], (NOBS,), 0, 8, dtype=jnp.int32)
    offset_x = jax.random.randint(keys[5], (NOBS,), -spread, spread + 1, dtype=jnp.int32)
    offset_y = jax.random.randint(keys[6], (NOBS,), -spread, spread + 1, dtype=jnp.int32)
    clustered = jax.random.randint(keys[7], (NOBS,), 0, 2, dtype=jnp.int32)
    near_x = jnp.clip(centre_x[picked] + offset_x, 0, NX - 1)
    near_y = jnp.clip(centre_y[picked] + offset_y, 0, NY - 1)
    pos_x = jnp.where(clustered == 1, near_x, drawn_x)
    pos_y = jnp.where(clustered == 1, near_y, drawn_y)
    pos_x = pos_x.at[0].set(NX - 1).at[1].set(0)
    pos_y = pos_y.at[0].set(NY - 1).at[1].set(0)
    pos_l = jax.random.randint(keys[8], (NOBS,), 0, LEV, dtype=jnp.int32)
    return jnp.stack([pos_x, pos_y, pos_l], axis=0).astype(jnp.int32)


def draw_obs_batch(key, part):
    base = jax.random.fold_in(key, 23)
    shuffled = jax.random.permutation(base, NOBS).astype(jnp.int32)
    return (shuffled % NBATCH).astype(jnp.int32)


def with_ends(result, stream_key, low, top_value):
    spot = [jax.random.randint(jax.random.fold_in(stream_key, axis), (), 0, length) for axis, length in enumerate(result.shape)]
    longest = result.shape.index(max(result.shape))
    beside = spot[:longest] + [(spot[longest] + 1) % result.shape[longest]] + spot[longest + 1:]
    return result.at[tuple(spot)].set(low).at[tuple(beside)].set(top_value)


def steps_of(stream_key, shape, pieces, least, high):
    def one(axis_at, parts):
        steps = jax.random.uniform(jax.random.fold_in(jax.random.fold_in(stream_key, 6), axis_at), (parts,), jnp.float32, least / len(pieces), high / len(pieces))
        return jnp.repeat(jnp.exp(steps), shape[axis_at] // parts).reshape((-1,) + (1,) * (len(shape) - axis_at - 1))

    loudness = one(*pieces[0])
    for cut in pieces[1:]:
        loudness = loudness * one(*cut)
    return loudness


def gaussian(rng, dims, scale, limit, held_as=jnp.bfloat16):
    entries = jax.random.normal(rng, dims, jnp.float32) * scale
    return jnp.minimum(jnp.maximum(entries, -limit), limit).astype(held_as)


def setup_inputs(seed: int = 0) -> dict:
    key_list = jax.random.split(jax.random.key(seed), 9)
    ensemble = draw_ensemble(jax.random.fold_in(key_list[8], 71), 0)
    weights = jnp.clip(0.02 + 0.2 * jax.random.uniform(key_list[1], (4, NX, NY * LEV), jnp.float32) ** steps_of(key_list[1], (4, NX, NY * LEV), ((1, 16), (2, 16)), -0.2, 0.2), 0.02, 0.22)
    obs_cell = draw_obs_cell(jax.random.fold_in(key_list[8], 71), 0)
    obs_batch = draw_obs_batch(jax.random.fold_in(key_list[8], 71), 0)
    obs_radius = with_ends(jax.random.randint(key_list[4], (NOBS,), max(CX, CY), 2 * max(CX, CY) + 1), jax.random.fold_in(key_list[4], 1), max(CX, CY), 2 * max(CX, CY)).astype(jnp.int32)
    obs_value = gaussian(key_list[5], (NOBS,), 2.0, 8.0, jnp.float32)
    obs_noise = gaussian(key_list[6], (MEM, NOBS), 1.0, 6.0, jnp.float32)
    obs_var = jnp.clip(jnp.exp(jax.random.uniform(key_list[7], (NOBS,), jnp.float32, math.log(0.25), math.log(1.0))), 0.25, 1.0)
    return {"ensemble": ensemble, "weights": weights, "obs_cell": obs_cell, "obs_batch": obs_batch, "obs_radius": obs_radius, "obs_value": obs_value, "obs_noise": obs_noise, "obs_var": obs_var}


HIGHEST = lax.Precision.HIGHEST
VERTICAL_SCALE = 8.0

def horizontal_taper(delta_x, delta_y, radius):
    distance_ratio = (delta_x * delta_x + delta_y * delta_y) / (radius * radius)
    return jnp.square(jnp.maximum(1.0 - distance_ratio, 0.0))

def level_taper(delta_l):
    return 1.0 / (1.0 + jnp.square(delta_l / VERTICAL_SCALE))

def solve_batch(prior_obs, obs_value, obs_noise, variance):
    anomaly = prior_obs - lax.optimization_barrier(jnp.mean(prior_obs, axis=0, keepdims=True))
    covariance = jnp.dot(anomaly.T, anomaly, precision=HIGHEST) / (MEM - 1) + jnp.diag(variance)
    innovation = obs_value[None, :] + jnp.sqrt(variance)[None, :] * obs_noise - prior_obs
    factor = jnp.linalg.cholesky(covariance)
    solved = jax.scipy.linalg.cho_solve((factor, True), innovation.T)
    return (anomaly, solved.T)

def reference(ensemble, weights, obs_cell, obs_batch, obs_radius, obs_value, obs_noise, obs_var):
    ensemble_grid = ensemble.reshape(NX, NY, LEV, MEM)
    coeffs = weights.reshape(4, NX, NY, LEV, 1)
    padded = jnp.pad(ensemble_grid, ((1, 1), (1, 1), (0, 0), (0, 0)))
    ensemble_grid = ensemble_grid + coeffs[0] * (padded[:-2, 1:-1] - ensemble_grid) + coeffs[1] * (padded[2:, 1:-1] - ensemble_grid) + coeffs[2] * (padded[1:-1, :-2] - ensemble_grid) + coeffs[3] * (padded[1:-1, 2:] - ensemble_grid)
    batch_order = jnp.argsort(obs_batch, stable=True).astype(jnp.int32)
    levels = jnp.arange(LEV).astype(jnp.float32)
    cells_y = jnp.arange(NY).astype(jnp.float32)
    starts = (jnp.arange(N_GX) * CX).astype(jnp.int32)
    for batch_number in range(NBATCH):
        chosen = batch_order[batch_number * OBS_B:(batch_number + 1) * OBS_B]
        obs_x = obs_cell[0][chosen]
        obs_y = obs_cell[1][chosen]
        obs_l = obs_cell[2][chosen]
        prior_obs = ensemble_grid[obs_x, obs_y, obs_l].T
        anomaly, gain_rows = solve_batch(prior_obs, obs_value[chosen], obs_noise[:, chosen], obs_var[chosen])
        radius = obs_radius[chosen].astype(jnp.float32)
        vertical = level_taper(levels[None, :] - obs_l.astype(jnp.float32)[:, None])
        fx = obs_x.astype(jnp.float32)
        fy = obs_y.astype(jnp.float32)

        def update(packed):
            slab_rows, first_row = packed
            cells_x = (first_row + jnp.arange(CX)).astype(jnp.float32)
            across = horizontal_taper(cells_x[None, :, None] - fx[:, None, None], cells_y[None, None, :] - fy[:, None, None], radius[:, None, None])
            loc_taper = across[:, :, :, None] * vertical[:, None, None, :]
            centred = slab_rows - lax.optimization_barrier(jnp.mean(slab_rows, axis=-1, keepdims=True))
            link = jnp.einsum('xylm,mj->jxyl', centred, anomaly, precision=HIGHEST) / (MEM - 1) * loc_taper
            return slab_rows + jnp.einsum('jxyl,mj->xylm', link, gain_rows, precision=HIGHEST)
        blocks = ensemble_grid.reshape(N_GX, CX, NY, LEV, MEM)
        ensemble_grid = lax.map(update, (blocks, starts)).reshape(NX, NY, LEV, MEM)
    return ensemble_grid.reshape(NX, NY, LEV * MEM)
```

```python
import functools
import jax
import jax.numpy as jnp
from jax import lax
from jax.experimental import pallas as pl
from jax.experimental.pallas import tpu as pltpu
from jax.sharding import PartitionSpec as P

MEM = 64
LEV = 32
OBS_B = 128
NBATCH = 4
HIGHEST = lax.Precision.HIGHEST
F32 = jnp.float32
BF16 = jnp.bfloat16


def dot(a, b, precision=None):
    return jnp.dot(a, b, preferred_element_type=F32, precision=precision)


def dot_nt(a, b, precision=None):
    return lax.dot_general(
        a, b, (((1,), (1,)), ((), ())), preferred_element_type=F32, precision=precision
    )


def split(value):
    high = value.astype(BF16)
    return high, (value - high.astype(F32)).astype(BF16)


def eliminate_four(rows, first):
    blocks = len(rows)
    shape = (8, 128)
    columns = [
        [jnp.broadcast_to(rows[v][0][:, first + j : first + j + 1], shape) for v in range(blocks)]
        for j in range(4)
    ]

    def entry(i, j):
        return jnp.broadcast_to(columns[j][0][first + i : first + i + 1, :], shape)

    a00, a01, a11 = entry(0, 0), entry(0, 1), entry(1, 1)
    a20, a21, a30, a31 = entry(2, 0), entry(2, 1), entry(3, 0), entry(3, 1)
    a22, a32, a33 = entry(2, 2), entry(3, 2), entry(3, 3)
    inv = 1.0 / (a00 * a11 - a01 * a01)
    p00, p01, p11 = a11 * inv, -a01 * inv, a00 * inv
    x20, x21 = a20 * p00 + a21 * p01, a20 * p01 + a21 * p11
    x30, x31 = a30 * p00 + a31 * p01, a30 * p01 + a31 * p11
    s22 = a22 - (x20 * a20 + x21 * a21)
    s32 = a32 - (x30 * a20 + x31 * a21)
    s33 = a33 - (x30 * a30 + x31 * a31)
    inv = 1.0 / (s22 * s33 - s32 * s32)
    q22, q32, q33 = s33 * inv, -s32 * inv, s22 * inv
    lane_row = lax.broadcasted_iota(jnp.int32, shape, 0)
    result = [[None] * len(rows[0]) for _ in range(blocks)]
    for col in range(len(rows[0])):
        r0, r1, r2, r3 = (
            jnp.broadcast_to(rows[0][col][first + i : first + i + 1, :], shape) for i in range(4)
        )
        t2 = r2 - (x20 * r0 + x21 * r1)
        t3 = r3 - (x30 * r0 + x31 * r1)
        n2 = q22 * t2 + q32 * t3
        n3 = q32 * t2 + q33 * t3
        n0 = p00 * r0 + p01 * r1 - (x20 * n2 + x30 * n3)
        n1 = p01 * r0 + p11 * r1 - (x21 * n2 + x31 * n3)
        for v in range(blocks):
            value = rows[v][col] - (
                (columns[0][v] * n0 + columns[1][v] * n1)
                + (columns[2][v] * n2 + columns[3][v] * n3)
            )
            if v == 0:
                value = jnp.where(lane_row == first, n0, value)
                value = jnp.where(lane_row == first + 1, n1, value)
                value = jnp.where(lane_row == first + 2, n2, value)
                value = jnp.where(lane_row == first + 3, n3, value)
            result[v][col] = value
    return result


def eliminate_eight(rows):
    rows = eliminate_four(rows, 0)
    rows = eliminate_four(rows, 4)
    rows = [[pltpu.roll(row[0], 120, 1)] + row[1:] for row in rows]
    return rows[1:] + rows[:1]


def flat(rows):
    return tuple(value for row in rows for value in row)


def nested(values, width):
    return [list(values[i : i + width]) for i in range(0, len(values), width)]


def taper_of(dx, dy, dl, radius):
    across = jnp.maximum(1.0 - (dx * dx + dy * dy) / (radius * radius), 0.0)
    return across * across, 1.0 + (dl * 0.125) * (dl * 0.125)


def analysis_kernel(
    axes, f_ref, p_ref, rows_ref, cols_ref, o_ref, state_ref, near_ref, w1_ref, w2_ref, hor_ref, ver_ref
):
    cells = f_ref.shape[0]
    start_x, start_y = axes()
    packed = p_ref[...].T
    state_ref[:, 0:256] = packed[:MEM]
    state_ref[:, 256:512] = packed[MEM:]

    def row_of(index, batch):
        return rows_ref[index : index + 1, batch * OBS_B : (batch + 1) * OBS_B]

    def solve_begin(batch):
        low = batch * OBS_B
        prior = state_ref[:, low : low + OBS_B]
        anomaly = prior - jnp.mean(prior, axis=0, keepdims=True)
        variance = row_of(5, batch)
        deviation = jnp.sqrt(variance)
        inv_dev = 1.0 / deviation
        noise = rows_ref[8:72, low : low + OBS_B]
        innovation = row_of(4, batch) + deviation * noise - prior
        scaled = anomaly * (inv_dev * (1.0 / (MEM - 1) ** 0.5))
        both = jnp.concatenate([scaled, innovation * inv_dev], axis=0)
        right = jnp.concatenate([scaled, jnp.zeros((64, OBS_B), F32)], axis=0)
        product = dot_nt(both, right, HIGHEST)
        eye = lax.broadcasted_iota(jnp.int32, (64, 128), 0) == lax.broadcasted_iota(jnp.int32, (64, 128), 1)
        system = product[:64] + eye.astype(F32)
        rhs = scaled * inv_dev
        rows = [[system[8 * v : 8 * v + 8], rhs[8 * v : 8 * v + 8]] for v in range(8)]
        return anomaly, innovation * variance_inverse(inv_dev), product[64:, :64], rows

    def variance_inverse(inv_dev):
        return inv_dev * inv_dev

    def near(batch, anomaly):
        low, high = batch * OBS_B, (batch + 1) * OBS_B
        if batch == NBATCH - 1:
            return
        links = dot(anomaly.T, state_ref[:, high:], HIGHEST)
        for later in range(batch + 1, NBATCH):
            cut = slice(later * OBS_B, (later + 1) * OBS_B)
            across, down = taper_of(
                cols_ref[low:high, 0:1] - rows_ref[0:1, cut],
                cols_ref[low:high, 1:2] - rows_ref[1:2, cut],
                cols_ref[low:high, 2:3] - rows_ref[2:3, cut],
                cols_ref[low:high, 3:4],
            )
            at = (later - batch - 1) * OBS_B
            near_ref[:, at : at + OBS_B] = links[:, at : at + OBS_B] * (across / (down * (MEM - 1)))

    def tile_begin(batch, anomaly, gain):
        zero = jnp.zeros((64, 128), BF16)
        high, low = split(anomaly)
        high_two = jnp.concatenate(
            [jnp.concatenate([high, zero], axis=1), jnp.concatenate([zero, high], axis=1)], axis=0
        )
        w1_ref[0:128, :] = high_two
        w1_ref[128:256, :] = high_two
        w1_ref[256:384, :] = jnp.concatenate(
            [jnp.concatenate([low, zero], axis=1), jnp.concatenate([zero, low], axis=1)], axis=0
        )
        turned = gain.T
        high, low = split(turned)
        zero = jnp.zeros((128, 64), BF16)
        w2_ref[:, 0:128] = jnp.concatenate(
            [jnp.concatenate([high, zero], axis=1), jnp.concatenate([zero, high], axis=1)], axis=0
        )
        w2_ref[:, 128:256] = jnp.concatenate(
            [jnp.concatenate([low, zero], axis=1), jnp.concatenate([zero, low], axis=1)], axis=0
        )
        cell = lax.broadcasted_iota(jnp.int32, (cells, 1), 0)
        level = lax.broadcasted_iota(jnp.int32, (LEV, 1), 0).astype(F32)
        cell_x = (cell // 24 + start_x).astype(F32)
        cell_y = (cell % 24 + start_y).astype(F32)
        across, down = taper_of(
            cell_x - row_of(0, batch), cell_y - row_of(1, batch), level - row_of(2, batch), row_of(3, batch)
        )
        hor_ref[...] = across
        ver_ref[...] = 1.0 / (down * (MEM - 1))

    def tile_step(src_ref, step):
        lanes = [pl.ds(pl.multiple_of(step * 256 + 128 * h, 128), 128) for h in range(2)]
        state = jnp.concatenate([src_ref[:, lanes[0]], src_ref[:, lanes[1]]], axis=0)
        high, low = split(state)
        link = dot(jnp.concatenate([high, low], axis=1), w1_ref[0:256, :]) + dot(high, w1_ref[256:384, :])
        parts = []
        for h in range(2):
            sides = []
            for p in range(2):
                down = ver_ref[pl.ds(4 * step + 2 * h + p, 1), :]
                sides.append(
                    link[h * cells : (h + 1) * cells, p * 128 : p * 128 + 128] * hor_ref[...] * down
                )
            parts.append(jnp.concatenate(sides, axis=1))
        high, low = split(jnp.concatenate(parts, axis=0))
        wide = dot(high, w2_ref[...])
        state = state + (wide[:, :128] + wide[:, 128:] + dot(low, w2_ref[:, 0:128]))
        for h in range(2):
            o_ref[:, lanes[h]] = state[h * cells : (h + 1) * cells]

    for batch in range(NBATCH + 1):
        if batch < NBATCH:
            anomaly, direct, cross, rows = solve_begin(batch)
            near(batch, anomaly)
            values = flat(rows)
        else:
            values = ()

        def step_body(step, values):
            if batch > 0:
                tile_step(f_ref if batch == 1 else o_ref, step)
            if batch < NBATCH:
                values = flat(eliminate_eight(nested(values, 2)))
            return values

        values = lax.fori_loop(0, 8, step_body, values)
        if batch < NBATCH:
            solved = jnp.concatenate([row[1] for row in nested(values, 2)], axis=0)
            gain = direct - dot(cross, solved, HIGHEST)
            if batch < NBATCH - 1:
                high = (batch + 1) * OBS_B
                state_ref[:, high:] = state_ref[:, high:] + dot(
                    gain, near_ref[:, : NBATCH * OBS_B - high], HIGHEST
                )
            tile_begin(batch, anomaly, gain)


def analyse(axes, forecast, packed, rows, cols):
    cells = forecast.shape[0]
    return pl.pallas_call(
        functools.partial(analysis_kernel, axes),
        out_shape=jax.ShapeDtypeStruct(forecast.shape, F32),
        in_specs=[pl.BlockSpec(memory_space=pltpu.VMEM)] * 4,
        out_specs=pl.BlockSpec(memory_space=pltpu.VMEM),
        scratch_shapes=[
            pltpu.VMEM((MEM, NBATCH * OBS_B), F32),
            pltpu.VMEM((OBS_B, (NBATCH - 1) * OBS_B), F32),
            pltpu.VMEM((384, 256), BF16),
            pltpu.VMEM((256, 256), BF16),
            pltpu.VMEM((cells, OBS_B), F32),
            pltpu.VMEM((LEV, OBS_B), F32),
        ],
        compiler_params=pltpu.CompilerParams(vmem_limit_bytes=48 * 1024 * 1024),
        name="analysis",
    )(forecast, packed, rows, cols)


MESH = pl.DeviceIdType.MESH


def forecast_kernel(
    n_x, n_y,
    ens_ref, w_ref, cell_ref, batch_ref, radius_ref, value_ref, var_ref, noise_ref,
    f_ref, p_ref, rows_ref, cols_ref,
    west_ref, east_ref, south_ref, north_ref, first_ref, last_ref,
    data_ref, spread_ref, pick_ref, found_ref,
    part_ref, got_y_ref, sum_ref, got_x_ref, total_ref, all_ref,
    halo_send, halo_recv, send_1, recv_1, send_2, recv_2, send_3, recv_3,
):
    gx, gy = lax.axis_index("gx"), lax.axis_index("gy")
    rows_x, rows_y = ens_ref.shape[0], ens_ref.shape[1]
    cells = rows_x * rows_y

    def peer(axis, index, count, step):
        return {axis: lax.rem(index + step, count)}

    barrier = pltpu.get_barrier_semaphore()
    for step in range(1, n_x):
        pl.semaphore_signal(barrier, inc=1, device_id=peer("gx", gx, n_x, step), device_id_type=MESH)
    for step in range(1, n_y):
        pl.semaphore_signal(barrier, inc=1, device_id=peer("gy", gy, n_y, step), device_id_type=MESH)

    for x in range(rows_x):
        first_ref[x : x + 1, :] = ens_ref[x, 0:1, :]
        last_ref[x : x + 1, :] = ens_ref[x, rows_y - 1 : rows_y, :]

    pl.semaphore_wait(barrier, n_x + n_y - 2)

    def halo(slot, src, dst, axis, target):
        return pltpu.make_async_remote_copy(
            src_ref=src, dst_ref=dst, send_sem=halo_send.at[slot], recv_sem=halo_recv.at[slot],
            device_id={axis: target}, device_id_type=MESH,
        )

    copies = (
        (halo(0, ens_ref.at[rows_x - 1], west_ref, "gx", lax.rem(gx + 1, n_x)), gx < n_x - 1, gx > 0, west_ref),
        (halo(1, ens_ref.at[0], east_ref, "gx", lax.rem(gx + n_x - 1, n_x)), gx > 0, gx < n_x - 1, east_ref),
        (halo(2, last_ref, south_ref, "gy", lax.rem(gy + 1, n_y)), gy < n_y - 1, gy > 0, south_ref),
        (halo(3, first_ref, north_ref, "gy", lax.rem(gy + n_y - 1, n_y)), gy > 0, gy < n_y - 1, north_ref),
    )
    for copy, sends, _, _ in copies:
        pl.when(sends)(copy.start)

    data_ref[...] = jnp.zeros(data_ref.shape, F32)
    data_ref[0:3, :] = cell_ref[...].astype(F32)
    data_ref[3:4, :] = radius_ref[...].astype(F32)
    data_ref[4:5, :] = value_ref[...]
    data_ref[5:6, :] = var_ref[...]
    data_ref[8:72, :] = noise_ref[...]
    n_obs = batch_ref.shape[1]
    square = (n_obs, n_obs)
    at_row, at_lane = lax.broadcasted_iota(jnp.int32, square, 0), lax.broadcasted_iota(jnp.int32, square, 1)
    before = (at_row < at_lane).astype(F32).astype(BF16)
    kind = lax.broadcasted_iota(jnp.int32, (8, n_obs), 0)
    same = (kind == batch_ref[...]).astype(F32)
    count = dot(same.astype(BF16), before)
    rank = jnp.sum(same * (count + (kind * OBS_B).astype(F32)), axis=0, keepdims=True)
    chosen = (at_row.astype(F32) == rank).astype(F32).astype(BF16)
    data = data_ref[...]
    high = data.astype(BF16)
    rest = data - high.astype(F32)
    middle, low = split(rest)
    thirds = dot_nt(chosen, jnp.concatenate([high, middle, low], axis=0))
    table = (thirds[:, 0:128] + thirds[:, 128:256]) + thirds[:, 256:384]
    cols_ref[...] = table[:, 0:8]
    rows_ref[...] = table.T[0:72]
    obs_x = table[:, 0:1] - (gx * rows_x).astype(F32)
    obs_y = table[:, 1:2] - (gy * rows_y).astype(F32)
    inside = (obs_x >= 0.0) & (obs_x < rows_x) & (obs_y >= 0.0) & (obs_y < rows_y)
    place = jnp.where(inside, obs_x * rows_y + obs_y, -1.0)
    pick_ref[...] = (
        lax.broadcasted_iota(jnp.int32, pick_ref.shape, 1).astype(F32) == place
    ).astype(F32).astype(BF16)
    obs_l = table[:, 2:3]
    pair = jnp.floor(obs_l * 0.5)
    odd = obs_l - 2.0 * pair

    for k in range(4):
        for y in range(rows_y):
            block = w_ref[k, :, 128 * (y // 4) : 128 * (y // 4) + 128]
            if y % 4:
                block = pltpu.roll(block, 128 - 32 * (y % 4), 1)
            spread_ref[pl.ds(k * cells + y, rows_x, stride=rows_y), :] = block
    found_ref[...] = jnp.zeros(found_ref.shape, F32)

    for copy, _, receives, halo_ref in copies:
        pl.when(receives)(copy.wait_recv)

        @pl.when(jnp.logical_not(receives))
        def _():
            halo_ref[...] = jnp.zeros(halo_ref.shape, F32)

    def forecast_step(step, carry):
        lanes = pl.ds(pl.multiple_of(step * 256, 256), 256)
        level = lax.broadcasted_iota(jnp.int32, (128, 256), 0)
        column = lax.broadcasted_iota(jnp.int32, (128, 256), 1) // 64 + 4 * step
        ones = (level == column).astype(F32).astype(BF16)
        high, low = split(spread_ref[...])
        weights = dot(jnp.concatenate([high, low], axis=1), jnp.concatenate([ones, ones], axis=0))
        side = lax.broadcasted_iota(jnp.int32, (rows_y, 256), 0)
        parts = []
        for x in range(rows_x):
            q = ens_ref[x, :, lanes]
            west = west_ref[:, lanes] if x == 0 else ens_ref[x - 1, :, lanes]
            east = east_ref[:, lanes] if x == rows_x - 1 else ens_ref[x + 1, :, lanes]
            south = jnp.where(side == 0, south_ref[x : x + 1, lanes], pltpu.roll(q, 1, 0))
            north = jnp.where(side == rows_y - 1, north_ref[x : x + 1, lanes], pltpu.roll(q, rows_y - 1, 0))
            total = q
            for k, other in enumerate((west, east, south, north)):
                at = k * cells + x * rows_y
                total = total + weights[at : at + rows_y] * (other - q)
            parts.append(total)
        step_rows = jnp.concatenate(parts, axis=0)
        f_ref[:, lanes] = step_rows
        high, low = split(step_rows)
        here = dot(pick_ref[:, 0:cells], high) + dot(pick_ref[:, 0:cells], low)
        found = found_ref[...]
        for h in range(2):
            found = found + jnp.where(
                pair == (2 * step + h).astype(F32), here[:, h * 128 : h * 128 + 128], 0.0
            )
        found_ref[...] = found
        return carry

    lax.fori_loop(0, 8, forecast_step, 0)
    found = found_ref[...]
    turned = pltpu.roll(found, 64, 1)
    left = jnp.where(odd == 0.0, found, turned)
    right = jnp.where(odd == 0.0, turned, found)
    half = n_obs // 2
    lane = lax.broadcasted_iota(jnp.int32, (half, 128), 1)
    part_ref[...] = jnp.where(lane < 64, left[:half], right[half:])

    share = half // n_y

    def send(step, axis, index, count, src, dst, sends, recvs):
        return pltpu.make_async_remote_copy(
            src_ref=src, dst_ref=dst, send_sem=sends.at[step], recv_sem=recvs.at[step],
            device_id=peer(axis, index, count, step), device_id_type=MESH,
        )

    def rows_of(index):
        return pl.ds(pl.multiple_of(index * share, share), share)

    first = [
        send(s, "gy", gy, n_y, part_ref.at[rows_of(lax.rem(gy + s, n_y))], got_y_ref.at[s], send_1, recv_1)
        for s in range(1, n_y)
    ]
    for copy in first:
        copy.start()
    total = part_ref[rows_of(gy), :]
    for s, copy in enumerate(first, 1):
        copy.wait_recv()
        total = total + got_y_ref[s]
    sum_ref[...] = total
    second = [send(s, "gx", gx, n_x, sum_ref, got_x_ref.at[s], send_2, recv_2) for s in range(1, n_x)]
    for copy in second:
        copy.start()
    for s, copy in enumerate(second, 1):
        copy.wait_recv()
        total = total + got_x_ref[s]
    total_ref[...] = total
    third = [
        send(s, "gy", gy, n_y, total_ref, all_ref.at[rows_of(gy)], send_3, recv_3) for s in range(1, n_y)
    ]
    for copy in third:
        copy.start()
    all_ref[rows_of(gy), :] = total
    for copy, sends, _, _ in copies:
        pl.when(sends)(copy.wait_send)
    for copy in first + second:
        copy.wait_send()
    for copy in third:
        copy.wait_recv()
    p_ref[...] = all_ref[...]
    for copy in third:
        copy.wait_send()


def forecast_and_gather(n_x, n_y, ensemble, weights, obs_cell, obs_batch, obs_radius, obs_value, obs_noise, obs_var):
    rows_x, rows_y, width = ensemble.shape
    cells = rows_x * rows_y
    n_obs = obs_batch.shape[0]
    share = n_obs // 2 // n_y
    vmem = pl.BlockSpec(memory_space=pltpu.VMEM)
    dma = pltpu.SemaphoreType.DMA
    return pl.pallas_call(
        functools.partial(forecast_kernel, n_x, n_y),
        out_shape=(
            jax.ShapeDtypeStruct((cells, width), F32),
            jax.ShapeDtypeStruct((n_obs // 2, 128), F32),
            jax.ShapeDtypeStruct((72, n_obs), F32),
            jax.ShapeDtypeStruct((n_obs, 8), F32),
        ),
        in_specs=[vmem] * 8,
        out_specs=(vmem,) * 4,
        scratch_shapes=[
            pltpu.VMEM((rows_y, width), F32),
            pltpu.VMEM((rows_y, width), F32),
            pltpu.VMEM((rows_x, width), F32),
            pltpu.VMEM((rows_x, width), F32),
            pltpu.VMEM((rows_x, width), F32),
            pltpu.VMEM((rows_x, width), F32),
            pltpu.VMEM((128, n_obs), F32),
            pltpu.VMEM((4 * cells, 128), F32),
            pltpu.VMEM((n_obs, 256), BF16),
            pltpu.VMEM((n_obs, 128), F32),
            pltpu.VMEM((n_obs // 2, 128), F32),
            pltpu.VMEM((n_y, share, 128), F32),
            pltpu.VMEM((share, 128), F32),
            pltpu.VMEM((n_x, share, 128), F32),
            pltpu.VMEM((share, 128), F32),
            pltpu.VMEM((n_obs // 2, 128), F32),
            dma((4,)), dma((4,)),
            dma((n_y,)), dma((n_y,)), dma((n_x,)), dma((n_x,)), dma((n_y,)), dma((n_y,)),
        ],
        compiler_params=pltpu.CompilerParams(
            collective_id=0, has_side_effects=True, vmem_limit_bytes=48 * 1024 * 1024
        ),
        name="forecast_and_gather",
    )(
        ensemble, weights, obs_cell, obs_batch.reshape(1, n_obs), obs_radius.reshape(1, n_obs),
        obs_value.reshape(1, n_obs), obs_var.reshape(1, n_obs), obs_noise,
    )


def solution(mesh):
    n_x, n_y = mesh.shape["gx"], mesh.shape["gy"]

    def body(ensemble, *rest):
        rows_x, rows_y, width = ensemble.shape
        forecast, packed, rows, cols = forecast_and_gather(n_x, n_y, ensemble, *rest)
        analysis = analyse(
            lambda: (lax.axis_index("gx") * rows_x, lax.axis_index("gy") * rows_y), forecast, packed, rows, cols
        )
        return analysis.reshape(rows_x, rows_y, width)

    placed = (P("gx", "gy", None), P(None, "gx", "gy"), P(), P(), P(), P(), P(), P())
    return jax.shard_map(
        body, mesh=mesh, in_specs=placed, out_specs=P("gx", "gy", None), check_vma=False
    )
```

```python
import functools
import jax
import jax.numpy as jnp
from jax import lax
from jax.experimental import pallas as pl
from jax.experimental.pallas import tpu as pltpu
from jax.sharding import PartitionSpec as P

MEM = 64
LEV = 32
OBS_B = 128
NBATCH = 4
HIGHEST = lax.Precision.HIGHEST
F32 = jnp.float32
BF16 = jnp.bfloat16


def dot(a, b, precision=None):
    return jnp.dot(a, b, preferred_element_type=F32, precision=precision)


def dot_nt(a, b, precision=None):
    return lax.dot_general(
        a, b, (((1,), (1,)), ((), ())), preferred_element_type=F32, precision=precision
    )


def split(value):
    high = value.astype(BF16)
    return high, (value - high.astype(F32)).astype(BF16)


def eliminate_four(rows, first):
    blocks = len(rows)
    shape = (8, 128)
    columns = [
        [jnp.broadcast_to(rows[v][0][:, first + j : first + j + 1], shape) for v in range(blocks)]
        for j in range(4)
    ]

    def entry(i, j):
        return jnp.broadcast_to(columns[j][0][first + i : first + i + 1, :], shape)

    a00, a01, a11 = entry(0, 0), entry(0, 1), entry(1, 1)
    a20, a21, a30, a31 = entry(2, 0), entry(2, 1), entry(3, 0), entry(3, 1)
    a22, a32, a33 = entry(2, 2), entry(3, 2), entry(3, 3)
    inv = 1.0 / (a00 * a11 - a01 * a01)
    p00, p01, p11 = a11 * inv, -a01 * inv, a00 * inv
    x20, x21 = a20 * p00 + a21 * p01, a20 * p01 + a21 * p11
    x30, x31 = a30 * p00 + a31 * p01, a30 * p01 + a31 * p11
    s22 = a22 - (x20 * a20 + x21 * a21)
    s32 = a32 - (x30 * a20 + x31 * a21)
    s33 = a33 - (x30 * a30 + x31 * a31)
    inv = 1.0 / (s22 * s33 - s32 * s32)
    q22, q32, q33 = s33 * inv, -s32 * inv, s22 * inv
    lane_row = lax.broadcasted_iota(jnp.int32, shape, 0)
    result = [[None] * len(rows[0]) for _ in range(blocks)]
    for col in range(len(rows[0])):
        r0, r1, r2, r3 = (
            jnp.broadcast_to(rows[0][col][first + i : first + i + 1, :], shape) for i in range(4)
        )
        t2 = r2 - (x20 * r0 + x21 * r1)
        t3 = r3 - (x30 * r0 + x31 * r1)
        n2 = q22 * t2 + q32 * t3
        n3 = q32 * t2 + q33 * t3
        n0 = p00 * r0 + p01 * r1 - (x20 * n2 + x30 * n3)
        n1 = p01 * r0 + p11 * r1 - (x21 * n2 + x31 * n3)
        for v in range(blocks):
            value = rows[v][col] - (
                (columns[0][v] * n0 + columns[1][v] * n1)
                + (columns[2][v] * n2 + columns[3][v] * n3)
            )
            if v == 0:
                value = jnp.where(lane_row == first, n0, value)
                value = jnp.where(lane_row == first + 1, n1, value)
                value = jnp.where(lane_row == first + 2, n2, value)
                value = jnp.where(lane_row == first + 3, n3, value)
            result[v][col] = value
    return result


def eliminate_eight(rows):
    rows = eliminate_four(rows, 0)
    rows = eliminate_four(rows, 4)
    rows = [[pltpu.roll(row[0], 120, 1)] + row[1:] for row in rows]
    return rows[1:] + rows[:1]


def flat(rows):
    return tuple(value for row in rows for value in row)


def nested(values, width):
    return [list(values[i : i + width]) for i in range(0, len(values), width)]


def taper_of(dx, dy, dl, radius):
    across = jnp.maximum(1.0 - (dx * dx + dy * dy) / (radius * radius), 0.0)
    return across * across, 1.0 + (dl * 0.125) * (dl * 0.125)


def analysis_kernel(
    axes, f_ref, p_ref, rows_ref, cols_ref, o_ref, state_ref, near_ref, w1_ref, w2_ref, hor_ref, ver_ref
):
    cells = f_ref.shape[0]
    start_x, start_y = axes()
    packed = p_ref[...].T
    state_ref[:, 0:256] = packed[:MEM]
    state_ref[:, 256:512] = packed[MEM:]

    def row_of(index, batch):
        return rows_ref[index : index + 1, batch * OBS_B : (batch + 1) * OBS_B]

    def solve_begin(batch):
        low = batch * OBS_B
        prior = state_ref[:, low : low + OBS_B]
        anomaly = prior - jnp.mean(prior, axis=0, keepdims=True)
        variance = row_of(5, batch)
        deviation = jnp.sqrt(variance)
        inv_dev = 1.0 / deviation
        noise = rows_ref[8:72, low : low + OBS_B]
        innovation = row_of(4, batch) + deviation * noise - prior
        scaled = anomaly * (inv_dev * (1.0 / (MEM - 1) ** 0.5))
        both = jnp.concatenate([scaled, innovation * inv_dev], axis=0)
        right = jnp.concatenate([scaled, jnp.zeros((64, OBS_B), F32)], axis=0)
        product = dot_nt(both, right, HIGHEST)
        eye = lax.broadcasted_iota(jnp.int32, (64, 128), 0) == lax.broadcasted_iota(jnp.int32, (64, 128), 1)
        system = product[:64] + eye.astype(F32)
        rhs = scaled * inv_dev
        rows = [[system[8 * v : 8 * v + 8], rhs[8 * v : 8 * v + 8]] for v in range(8)]
        return anomaly, innovation * variance_inverse(inv_dev), product[64:, :64], rows

    def variance_inverse(inv_dev):
        return inv_dev * inv_dev

    def near(batch, anomaly):
        low, high = batch * OBS_B, (batch + 1) * OBS_B
        if batch == NBATCH - 1:
            return
        links = dot(anomaly.T, state_ref[:, high:], HIGHEST)
        for later in range(batch + 1, NBATCH):
            cut = slice(later * OBS_B, (later + 1) * OBS_B)
            across, down = taper_of(
                cols_ref[low:high, 0:1] - rows_ref[0:1, cut],
                cols_ref[low:high, 1:2] - rows_ref[1:2, cut],
                cols_ref[low:high, 2:3] - rows_ref[2:3, cut],
                cols_ref[low:high, 3:4],
            )
            at = (later - batch - 1) * OBS_B
            near_ref[:, at : at + OBS_B] = links[:, at : at + OBS_B] * (across / (down * (MEM - 1)))

    def tile_begin(batch, anomaly, gain):
        zero = jnp.zeros((64, 128), BF16)
        high, low = split(anomaly)
        high_two = jnp.concatenate(
            [jnp.concatenate([high, zero], axis=1), jnp.concatenate([zero, high], axis=1)], axis=0
        )
        w1_ref[0:128, :] = high_two
        w1_ref[128:256, :] = high_two
        w1_ref[256:384, :] = jnp.concatenate(
            [jnp.concatenate([low, zero], axis=1), jnp.concatenate([zero, low], axis=1)], axis=0
        )
        turned = gain.T
        high, low = split(turned)
        zero = jnp.zeros((128, 64), BF16)
        w2_ref[:, 0:128] = jnp.concatenate(
            [jnp.concatenate([high, zero], axis=1), jnp.concatenate([zero, high], axis=1)], axis=0
        )
        w2_ref[:, 128:256] = jnp.concatenate(
            [jnp.concatenate([low, zero], axis=1), jnp.concatenate([zero, low], axis=1)], axis=0
        )
        cell = lax.broadcasted_iota(jnp.int32, (cells, 1), 0)
        level = lax.broadcasted_iota(jnp.int32, (LEV, 1), 0).astype(F32)
        cell_x = (cell // 24 + start_x).astype(F32)
        cell_y = (cell % 24 + start_y).astype(F32)
        across, down = taper_of(
            cell_x - row_of(0, batch), cell_y - row_of(1, batch), level - row_of(2, batch), row_of(3, batch)
        )
        hor_ref[...] = across
        ver_ref[...] = 1.0 / (down * (MEM - 1))

    def tile_step(src_ref, step):
        lanes = [pl.ds(pl.multiple_of(step * 256 + 128 * h, 128), 128) for h in range(2)]
        state = jnp.concatenate([src_ref[:, lanes[0]], src_ref[:, lanes[1]]], axis=0)
        high, low = split(state)
        link = dot(jnp.concatenate([high, low], axis=1), w1_ref[0:256, :]) + dot(high, w1_ref[256:384, :])
        parts = []
        for h in range(2):
            sides = []
            for p in range(2):
                down = ver_ref[pl.ds(4 * step + 2 * h + p, 1), :]
                sides.append(
                    link[h * cells : (h + 1) * cells, p * 128 : p * 128 + 128] * hor_ref[...] * down
                )
            parts.append(jnp.concatenate(sides, axis=1))
        high, low = split(jnp.concatenate(parts, axis=0))
        wide = dot(high, w2_ref[...])
        state = state + (wide[:, :128] + wide[:, 128:] + dot(low, w2_ref[:, 0:128]))
        for h in range(2):
            o_ref[:, lanes[h]] = state[h * cells : (h + 1) * cells]

    for batch in range(NBATCH + 1):
        if batch < NBATCH:
            anomaly, direct, cross, rows = solve_begin(batch)
            near(batch, anomaly)
            values = flat(rows)
        else:
            values = ()

        def step_body(step, values):
            if batch > 0:
                tile_step(f_ref if batch == 1 else o_ref, step)
            if batch < NBATCH:
                values = flat(eliminate_eight(nested(values, 2)))
            return values

        values = lax.fori_loop(0, 8, step_body, values)
        if batch < NBATCH:
            solved = jnp.concatenate([row[1] for row in nested(values, 2)], axis=0)
            gain = direct - dot(cross, solved, HIGHEST)
            if batch < NBATCH - 1:
                high = (batch + 1) * OBS_B
                state_ref[:, high:] = state_ref[:, high:] + dot(
                    gain, near_ref[:, : NBATCH * OBS_B - high], HIGHEST
                )
            tile_begin(batch, anomaly, gain)


def analyse(axes, forecast, packed, rows, cols):
    cells = forecast.shape[0]
    return pl.pallas_call(
        functools.partial(analysis_kernel, axes),
        out_shape=jax.ShapeDtypeStruct(forecast.shape, F32),
        in_specs=[pl.BlockSpec(memory_space=pltpu.VMEM)] * 4,
        out_specs=pl.BlockSpec(memory_space=pltpu.VMEM),
        scratch_shapes=[
            pltpu.VMEM((MEM, NBATCH * OBS_B), F32),
            pltpu.VMEM((OBS_B, (NBATCH - 1) * OBS_B), F32),
            pltpu.VMEM((384, 256), BF16),
            pltpu.VMEM((256, 256), BF16),
            pltpu.VMEM((cells, OBS_B), F32),
            pltpu.VMEM((LEV, OBS_B), F32),
        ],
        compiler_params=pltpu.CompilerParams(vmem_limit_bytes=48 * 1024 * 1024),
        name="analysis",
    )(forecast, packed, rows, cols)


MESH = pl.DeviceIdType.MESH


def forecast_kernel(
    n_x, n_y,
    ens_hbm, w_hbm, cell_hbm, batch_hbm, radius_hbm, value_hbm, var_hbm, noise_hbm,
    f_ref, p_ref, rows_ref, cols_ref,
    ens_ref, w_ref, cell_ref, batch_ref, ints_ref, floats_ref,
    west_ref, east_ref, south_ref, north_ref, first_ref, last_ref,
    data_ref, spread_ref, point_ref, mix_ref, edge_ref, found_ref,
    part_ref, got_y_ref, sum_ref, got_x_ref, total_ref, all_ref,
    loads, halo_send, halo_recv, send_1, recv_1, send_2, recv_2, send_3, recv_3,
):
    gx, gy = lax.axis_index("gx"), lax.axis_index("gy")
    rows_x, rows_y = ens_ref.shape[0], ens_ref.shape[1]
    cells = rows_x * rows_y
    n_obs = batch_ref.shape[1]

    def peer(axis, index, count, step):
        return {axis: lax.rem(index + step, count)}

    small = [
        pltpu.make_async_copy(src, dst, loads.at[i])
        for i, (src, dst) in enumerate(
            (
                (batch_hbm, batch_ref),
                (cell_hbm, cell_ref),
                (noise_hbm, data_ref.at[8:72]),
                (radius_hbm, ints_ref),
                (value_hbm, floats_ref.at[0]),
                (var_hbm, floats_ref.at[1]),
            )
        )
    ]
    load_weights = pltpu.make_async_copy(w_hbm, w_ref, loads.at[6])
    load_tile = pltpu.make_async_copy(ens_hbm, ens_ref, loads.at[7])
    for copy in small:
        copy.start()
    load_tile.start()
    load_weights.start()

    barrier = pltpu.get_barrier_semaphore()
    for step in range(1, n_x):
        pl.semaphore_signal(barrier, inc=1, device_id=peer("gx", gx, n_x, step), device_id_type=MESH)
    for step in range(1, n_y):
        pl.semaphore_signal(barrier, inc=1, device_id=peer("gy", gy, n_y, step), device_id_type=MESH)

    for copy in small:
        copy.wait()
    data_ref[0:3, :] = cell_ref[...].astype(F32)
    data_ref[3:4, :] = ints_ref[...].astype(F32)
    data_ref[4:5, :] = floats_ref[0]
    data_ref[5:6, :] = floats_ref[1]
    data_ref[6:8, :] = jnp.zeros((2, n_obs), F32)
    data_ref[72:128, :] = jnp.zeros((56, n_obs), F32)
    square = (n_obs, n_obs)
    at_row, at_lane = lax.broadcasted_iota(jnp.int32, square, 0), lax.broadcasted_iota(jnp.int32, square, 1)
    before = (at_row < at_lane).astype(F32).astype(BF16)
    kind = lax.broadcasted_iota(jnp.int32, (8, n_obs), 0)
    same = (kind == batch_ref[...]).astype(F32)
    count = dot(same.astype(BF16), before)
    rank = jnp.sum(same * (count + (kind * OBS_B).astype(F32)), axis=0, keepdims=True)
    chosen = (at_row.astype(F32) == rank).astype(F32).astype(BF16)
    data = data_ref[...]
    high = data.astype(BF16)
    middle, low = split(data - high.astype(F32))
    thirds = dot_nt(chosen, jnp.concatenate([high, middle, low], axis=0))
    table = (thirds[:, 0:128] + thirds[:, 128:256]) + thirds[:, 256:384]
    cols_ref[...] = table[:, 0:8]
    rows_ref[...] = table.T[0:72]

    load_tile.wait()
    for x in range(rows_x):
        first_ref[x : x + 1, :] = ens_ref[x, 0:1, :]
        last_ref[x : x + 1, :] = ens_ref[x, rows_y - 1 : rows_y, :]

    pl.semaphore_wait(barrier, n_x + n_y - 2)

    def halo(slot, src, dst, axis, target):
        return pltpu.make_async_remote_copy(
            src_ref=src, dst_ref=dst, send_sem=halo_send.at[slot], recv_sem=halo_recv.at[slot],
            device_id={axis: target}, device_id_type=MESH,
        )

    copies = (
        (halo(0, ens_ref.at[rows_x - 1], west_ref, "gx", lax.rem(gx + 1, n_x)), gx < n_x - 1, gx > 0, west_ref),
        (halo(1, ens_ref.at[0], east_ref, "gx", lax.rem(gx + n_x - 1, n_x)), gx > 0, gx < n_x - 1, east_ref),
        (halo(2, last_ref, south_ref, "gy", lax.rem(gy + 1, n_y)), gy < n_y - 1, gy > 0, south_ref),
        (halo(3, first_ref, north_ref, "gy", lax.rem(gy + n_y - 1, n_y)), gy > 0, gy < n_y - 1, north_ref),
    )
    for copy, sends, _, _ in copies:
        pl.when(sends)(copy.start)

    load_weights.wait()
    for y in range(rows_y):
        merged = jnp.zeros((rows_x, 128), F32)
        group = lax.broadcasted_iota(jnp.int32, (rows_x, 128), 1) // LEV
        for k in range(4):
            block = w_ref[k, :, 128 * (y // 4) : 128 * (y // 4) + 128]
            low_lanes = pltpu.roll(block, 128 - 32 * (y % 4), 1) if y % 4 else block
            spread_ref[pl.ds(k * cells + y, rows_x, stride=rows_y), :] = low_lanes
            turn = (32 * k - 32 * (y % 4)) % 128
            merged = jnp.where(group == k, pltpu.roll(block, turn, 1) if turn else block, merged)
        point_ref[pl.ds(y, rows_x, stride=rows_y), :] = merged

    obs_x = table[:, 0:1] - (gx * rows_x).astype(F32)
    obs_y = table[:, 1:2] - (gy * rows_y).astype(F32)
    obs_l = table[:, 2:3]
    inside = (obs_x >= 0.0) & (obs_x < rows_x) & (obs_y >= 0.0) & (obs_y < rows_y)

    def place(value):
        return jnp.where(inside, value, -1.0)

    centre = obs_x * rows_y + obs_y
    at_west = place(jnp.where(obs_x > 0.0, centre - rows_y, cells + obs_y))
    at_east = place(jnp.where(obs_x < rows_x - 1.0, centre + rows_y, cells + rows_y + obs_y))
    at_south = place(jnp.where(obs_y > 0.0, centre - 1.0, cells + 2 * rows_y + obs_x))
    at_north = place(jnp.where(obs_y < rows_y - 1.0, centre + 1.0, cells + 2 * rows_y + rows_x + obs_x))
    centre = place(centre)
    lane = lax.broadcasted_iota(jnp.int32, (n_obs, 256), 1).astype(F32)
    is_centre = lane == centre
    high, low = split(point_ref[...])
    both = dot(
        is_centre.astype(F32).astype(BF16)[:, 0:cells], jnp.concatenate([high, low], axis=1)
    )
    mine = both[:, 0:128] + both[:, 128:256]
    lane_level = lax.broadcasted_iota(jnp.int32, (n_obs, 128), 1) % LEV
    mine = jnp.where(lane_level.astype(F32) == obs_l, mine, 0.0)
    high, low = split(mine)
    group = lax.broadcasted_iota(jnp.int32, (128, 512), 0) // LEV == lax.broadcasted_iota(jnp.int32, (128, 512), 1) // 128
    group = group.astype(F32).astype(BF16)
    coeffs = dot(jnp.concatenate([high, low], axis=1), jnp.concatenate([group, group], axis=0))
    coeffs = [jnp.concatenate([coeffs[:, 128 * k : 128 * k + 128]] * 2, axis=1) for k in range(4)]
    mix = jnp.where(is_centre, 1.0 - ((coeffs[0] + coeffs[1]) + (coeffs[2] + coeffs[3])), 0.0)
    for k, at in enumerate((at_west, at_east, at_south, at_north)):
        mix = jnp.where(lane == at, coeffs[k], mix)
    high, low = split(mix)
    mix_ref[:, 0:256] = high
    mix_ref[:, 256:512] = low
    edge_ref[:, 0:64] = high[:, 192:256]
    edge_ref[:, 64:128] = low[:, 192:256]
    edge_ref[:, 128:192] = high[:, 192:256]
    pair = jnp.floor(obs_l * 0.5)
    odd = obs_l - 2.0 * pair
    found_ref[...] = jnp.zeros(found_ref.shape, F32)

    def take(step, here):
        found = found_ref[...]
        for h in range(2):
            found = jnp.where(
                pair == (2 * step + h).astype(F32), found + here[:, h * 128 : h * 128 + 128], found
            )
        found_ref[...] = found

    def lanes_of(step):
        return pl.ds(pl.multiple_of(step * 256, 256), 256)

    def own_cells(step, carry):
        high, low = split(ens_ref[:, :, lanes_of(step)].reshape(cells, 256))
        take(
            step,
            dot(mix_ref[:, 0:cells], high)
            + dot(mix_ref[:, 256 : 256 + cells], high)
            + dot(mix_ref[:, 0:cells], low),
        )
        return carry

    lax.fori_loop(0, 8, own_cells, 0)

    for copy, _, receives, halo_ref in copies:
        pl.when(receives)(copy.wait_recv)

        @pl.when(jnp.logical_not(receives))
        def _():
            halo_ref[...] = jnp.zeros(halo_ref.shape, F32)

    def cells_beside(step, carry):
        lanes = lanes_of(step)
        high, low = split(
            jnp.concatenate([west_ref[:, lanes], east_ref[:, lanes], south_ref[:, lanes], north_ref[:, lanes]], axis=0)
        )
        take(step, dot(edge_ref[...], jnp.concatenate([high, high, low], axis=0)))
        return carry

    lax.fori_loop(0, 8, cells_beside, 0)

    def forecast_step(step, carry):
        lanes = lanes_of(step)
        level = lax.broadcasted_iota(jnp.int32, (128, 256), 0)
        column = lax.broadcasted_iota(jnp.int32, (128, 256), 1) // 64 + 4 * step
        ones = (level == column).astype(F32).astype(BF16)
        high, low = split(spread_ref[...])
        weights = dot(jnp.concatenate([high, low], axis=1), jnp.concatenate([ones, ones], axis=0))
        side = lax.broadcasted_iota(jnp.int32, (rows_y, 256), 0)
        for x in range(rows_x):
            q = ens_ref[x, :, lanes]
            west = west_ref[:, lanes] if x == 0 else ens_ref[x - 1, :, lanes]
            east = east_ref[:, lanes] if x == rows_x - 1 else ens_ref[x + 1, :, lanes]
            south = jnp.where(side == 0, south_ref[x : x + 1, lanes], pltpu.roll(q, 1, 0))
            north = jnp.where(side == rows_y - 1, north_ref[x : x + 1, lanes], pltpu.roll(q, rows_y - 1, 0))
            total = q
            for k, other in enumerate((west, east, south, north)):
                at = k * cells + x * rows_y
                total = total + weights[at : at + rows_y] * (other - q)
            f_ref[x * rows_y : x * rows_y + rows_y, lanes] = total
        return carry

    found = found_ref[...]
    turned = pltpu.roll(found, 64, 1)
    left = jnp.where(odd == 0.0, found, turned)
    right = jnp.where(odd == 0.0, turned, found)
    half = n_obs // 2
    side = lax.broadcasted_iota(jnp.int32, (half, 128), 1)
    part_ref[...] = jnp.where(side < 64, left[:half], right[half:])

    share = half // n_y

    def send(step, axis, index, count, src, dst, sends, recvs):
        return pltpu.make_async_remote_copy(
            src_ref=src, dst_ref=dst, send_sem=sends.at[step], recv_sem=recvs.at[step],
            device_id=peer(axis, index, count, step), device_id_type=MESH,
        )

    def rows_of(index):
        return pl.ds(pl.multiple_of(index * share, share), share)

    first = [
        send(s, "gy", gy, n_y, part_ref.at[rows_of(lax.rem(gy + s, n_y))], got_y_ref.at[s], send_1, recv_1)
        for s in range(1, n_y)
    ]
    for copy in first:
        copy.start()
    lax.fori_loop(0, 3, forecast_step, 0)
    total = part_ref[rows_of(gy), :]
    for s, copy in enumerate(first, 1):
        copy.wait_recv()
        total = total + got_y_ref[s]
    sum_ref[...] = total
    second = [send(s, "gx", gx, n_x, sum_ref, got_x_ref.at[s], send_2, recv_2) for s in range(1, n_x)]
    for copy in second:
        copy.start()
    lax.fori_loop(3, 6, forecast_step, 0)
    for s, copy in enumerate(second, 1):
        copy.wait_recv()
        total = total + got_x_ref[s]
    total_ref[...] = total
    third = [
        send(s, "gy", gy, n_y, total_ref, all_ref.at[rows_of(gy)], send_3, recv_3) for s in range(1, n_y)
    ]
    for copy in third:
        copy.start()
    all_ref[rows_of(gy), :] = total
    lax.fori_loop(6, 8, forecast_step, 0)
    for copy, sends, _, _ in copies:
        pl.when(sends)(copy.wait_send)
    for copy in first + second:
        copy.wait_send()
    for copy in third:
        copy.wait_recv()
    p_ref[...] = all_ref[...]
    for copy in third:
        copy.wait_send()


def forecast_and_gather(n_x, n_y, ensemble, weights, obs_cell, obs_batch, obs_radius, obs_value, obs_noise, obs_var):
    rows_x, rows_y, width = ensemble.shape
    cells = rows_x * rows_y
    n_obs = obs_batch.shape[0]
    share = n_obs // 2 // n_y
    vmem = pl.BlockSpec(memory_space=pltpu.VMEM)
    dma = pltpu.SemaphoreType.DMA
    return pl.pallas_call(
        functools.partial(forecast_kernel, n_x, n_y),
        out_shape=(
            jax.ShapeDtypeStruct((cells, width), F32),
            jax.ShapeDtypeStruct((n_obs // 2, 128), F32),
            jax.ShapeDtypeStruct((72, n_obs), F32),
            jax.ShapeDtypeStruct((n_obs, 8), F32),
        ),
        in_specs=[pl.BlockSpec(memory_space=pltpu.HBM)] * 8,
        out_specs=(vmem,) * 4,
        scratch_shapes=[
            pltpu.VMEM(ensemble.shape, F32),
            pltpu.VMEM(weights.shape, F32),
            pltpu.VMEM(obs_cell.shape, jnp.int32),
            pltpu.VMEM((1, n_obs), jnp.int32),
            pltpu.VMEM((1, n_obs), jnp.int32),
            pltpu.VMEM((2, 1, n_obs), F32),
            pltpu.VMEM((rows_y, width), F32),
            pltpu.VMEM((rows_y, width), F32),
            pltpu.VMEM((rows_x, width), F32),
            pltpu.VMEM((rows_x, width), F32),
            pltpu.VMEM((rows_x, width), F32),
            pltpu.VMEM((rows_x, width), F32),
            pltpu.VMEM((128, n_obs), F32),
            pltpu.VMEM((4 * cells, 128), F32),
            pltpu.VMEM((cells, 128), F32),
            pltpu.VMEM((n_obs, 512), BF16),
            pltpu.VMEM((n_obs, 192), BF16),
            pltpu.VMEM((n_obs, 128), F32),
            pltpu.VMEM((n_obs // 2, 128), F32),
            pltpu.VMEM((n_y, share, 128), F32),
            pltpu.VMEM((share, 128), F32),
            pltpu.VMEM((n_x, share, 128), F32),
            pltpu.VMEM((share, 128), F32),
            pltpu.VMEM((n_obs // 2, 128), F32),
            dma((8,)), dma((4,)), dma((4,)),
            dma((n_y,)), dma((n_y,)), dma((n_x,)), dma((n_x,)), dma((n_y,)), dma((n_y,)),
        ],
        compiler_params=pltpu.CompilerParams(
            collective_id=0, has_side_effects=True, vmem_limit_bytes=48 * 1024 * 1024
        ),
        name="forecast_and_gather",
    )(
        *(
            pltpu.with_memory_space_constraint(value, pltpu.HBM)
            for value in (
                ensemble, weights, obs_cell, obs_batch.reshape(1, n_obs), obs_radius.reshape(1, n_obs),
                obs_value.reshape(1, n_obs), obs_var.reshape(1, n_obs), obs_noise,
            )
        )
    )


def solution(mesh):
    n_x, n_y = mesh.shape["gx"], mesh.shape["gy"]

    def body(ensemble, *rest):
        rows_x, rows_y, width = ensemble.shape
        forecast, packed, rows, cols = forecast_and_gather(n_x, n_y, ensemble, *rest)
        analysis = analyse(
            lambda: (lax.axis_index("gx") * rows_x, lax.axis_index("gy") * rows_y), forecast, packed, rows, cols
        )
        return analysis.reshape(rows_x, rows_y, width)

    placed = (P("gx", "gy", None), P(None, "gx", "gy"), P(), P(), P(), P(), P(), P())
    return jax.shard_map(
        body, mesh=mesh, in_specs=placed, out_specs=P("gx", "gy", None), check_vma=False
    )
```

```python
import functools
import jax
import jax.numpy as jnp
from jax import lax
from jax.experimental import pallas as pl
from jax.experimental.pallas import tpu as pltpu
from jax.sharding import PartitionSpec as P

MEM = 64
LEV = 32
OBS_B = 128
HALF = 64
NBATCH = 4
HIGHEST = lax.Precision.HIGHEST
F32 = jnp.float32
BF16 = jnp.bfloat16


def dot(a, b, precision=None):
    return jnp.dot(a, b, preferred_element_type=F32, precision=precision)


def dot_nt(a, b, precision=None):
    return lax.dot_general(
        a, b, (((1,), (1,)), ((), ())), preferred_element_type=F32, precision=precision
    )


def split(value):
    high = value.astype(BF16)
    return high, (value - high.astype(F32)).astype(BF16)


def invert_two(a, b, d):
    inv = 1.0 / (a * d - b * b)
    return d * inv, -b * inv, a * inv


def invert_four(m):
    p00, p01, p11 = invert_two(m[0][0], m[1][0], m[1][1])
    x20, x21 = m[2][0] * p00 + m[2][1] * p01, m[2][0] * p01 + m[2][1] * p11
    x30, x31 = m[3][0] * p00 + m[3][1] * p01, m[3][0] * p01 + m[3][1] * p11
    s22 = m[2][2] - (x20 * m[2][0] + x21 * m[2][1])
    s32 = m[3][2] - (x30 * m[2][0] + x31 * m[2][1])
    s33 = m[3][3] - (x30 * m[3][0] + x31 * m[3][1])
    q22, q32, q33 = invert_two(s22, s32, s33)
    y20, y21 = q22 * x20 + q32 * x30, q22 * x21 + q32 * x31
    y30, y31 = q32 * x20 + q33 * x30, q32 * x21 + q33 * x31
    low = [
        [p00 + (x20 * y20 + x30 * y30)],
        [p01 + (x20 * y21 + x30 * y31), p11 + (x21 * y21 + x31 * y31)],
        [-y20, -y21, q22],
        [-y30, -y31, q32, q33],
    ]
    return [[low[max(i, j)][min(i, j)] for j in range(4)] for i in range(4)]


def total(terms):
    terms = list(terms)
    while len(terms) > 1:
        terms = [sum(terms[i + 1 : i + 2], terms[i]) for i in range(0, len(terms), 2)]
    return terms[0]


def eliminate_eight(rows):
    blocks = len(rows)
    shape = (8, 128)
    four = range(4)
    columns = [
        [jnp.broadcast_to(rows[v][0][:, j : j + 1], shape) for v in range(blocks)] for j in range(8)
    ]

    def entry(i, j):
        return jnp.broadcast_to(columns[j][0][i : i + 1, :], shape)

    first = [[entry(i, j) for j in range(i + 1)] for i in four]
    cross = [[entry(4 + i, j) for j in four] for i in four]
    second = [[entry(4 + i, 4 + j) for j in range(i + 1)] for i in four]
    p = invert_four(first)
    x = [[total(cross[i][k] * p[k][j] for k in four) for j in four] for i in four]
    q = invert_four(
        [[second[i][j] - total(x[i][k] * cross[j][k] for k in four) for j in range(i + 1)] for i in four]
    )
    at = lax.broadcasted_iota(jnp.int32, shape, 0)
    result = [[None] * len(rows[0]) for _ in range(blocks)]
    for col in range(len(rows[0])):
        r = [jnp.broadcast_to(rows[0][col][i : i + 1, :], shape) for i in range(8)]
        t = [r[4 + i] - total(x[i][k] * r[k] for k in four) for i in four]
        upper = [total(q[i][k] * t[k] for k in four) for i in four]
        lower = [
            total(p[i][k] * r[k] for k in four) - total(x[k][i] * upper[k] for k in four) for i in four
        ]
        solved = lower + upper
        for v in range(1, blocks):
            result[v][col] = rows[v][col] - total(columns[k][v] * solved[k] for k in range(8))
        value = solved[0]
        for k in range(1, 8):
            value = jnp.where(at == k, solved[k], value)
        result[0][col] = value
    result = [[pltpu.roll(row[0], 120, 1)] + row[1:] for row in result]
    return result[1:] + result[:1]


def flat(rows):
    return tuple(value for row in rows for value in row)


def nested(values, width):
    return [list(values[i : i + width]) for i in range(0, len(values), width)]


def taper_of(dx, dy, dl, radius):
    across = jnp.maximum(1.0 - (dx * dx + dy * dy) / (radius * radius), 0.0)
    return across * across, 1.0 + (dl * 0.125) * (dl * 0.125)


def analysis_kernel(
    axes, f_ref, p_ref, rows_ref, cols_ref, select_ref, across_ref, down_ref, most_ref,
    o_ref, state_ref, near_ref, w1_ref, w2_ref, hor_ref, ver_ref,
):
    cells = f_ref.shape[0]
    start_x, start_y = axes()
    packed = p_ref[...].T
    state_ref[:, 0:256] = packed[:MEM]
    state_ref[:, 256:512] = packed[MEM:]

    def row_of(index, batch):
        return rows_ref[index : index + 1, batch * OBS_B : (batch + 1) * OBS_B]

    def solve_begin(batch):
        low = batch * OBS_B
        prior = state_ref[:, low : low + OBS_B]
        anomaly = prior - jnp.mean(prior, axis=0, keepdims=True)
        variance = row_of(5, batch)
        deviation = jnp.sqrt(variance)
        inv_dev = 1.0 / deviation
        noise = rows_ref[8:72, low : low + OBS_B]
        innovation = row_of(4, batch) + deviation * noise - prior
        scaled = anomaly * (inv_dev * (1.0 / (MEM - 1) ** 0.5))
        both = jnp.concatenate([scaled, innovation * inv_dev], axis=0)
        right = jnp.concatenate([scaled, jnp.zeros((64, OBS_B), F32)], axis=0)
        product = dot_nt(both, right, HIGHEST)
        eye = lax.broadcasted_iota(jnp.int32, (64, 128), 0) == lax.broadcasted_iota(jnp.int32, (64, 128), 1)
        system = product[:64] + eye.astype(F32)
        rhs = scaled * inv_dev
        rows = [[system[8 * v : 8 * v + 8], rhs[8 * v : 8 * v + 8]] for v in range(8)]
        return anomaly, innovation * (inv_dev * inv_dev), product[64:, :64], rows

    def near(batch, anomaly):
        low, high = batch * OBS_B, (batch + 1) * OBS_B
        if batch == NBATCH - 1:
            return
        links = dot(anomaly.T, state_ref[:, high:], HIGHEST)
        for later in range(batch + 1, NBATCH):
            cut = slice(later * OBS_B, (later + 1) * OBS_B)
            across, down = taper_of(
                cols_ref[low:high, 0:1] - rows_ref[0:1, cut],
                cols_ref[low:high, 1:2] - rows_ref[1:2, cut],
                cols_ref[low:high, 2:3] - rows_ref[2:3, cut],
                cols_ref[low:high, 3:4],
            )
            at = (later - batch - 1) * OBS_B
            near_ref[:, at : at + OBS_B] = links[:, at : at + OBS_B] * (across / (down * (MEM - 1)))

    def twice(value):
        zero = jnp.zeros(value.shape, value.dtype)
        return jnp.concatenate(
            [jnp.concatenate([value, zero], axis=1), jnp.concatenate([zero, value], axis=1)], axis=0
        )

    def all_begin(batch, anomaly, gain):
        high, low = split(anomaly)
        high_two = twice(high)
        w1_ref[0:128, :] = high_two
        w1_ref[128:256, :] = high_two
        w1_ref[256:384, :] = twice(low)
        high, low = split(gain.T)
        w2_ref[:, 0:128] = twice(high)
        w2_ref[:, 128:256] = twice(low)
        cell = lax.broadcasted_iota(jnp.int32, (cells, 1), 0)
        level = lax.broadcasted_iota(jnp.int32, (LEV, 1), 0).astype(F32)
        cell_x = (cell // 24 + start_x).astype(F32)
        cell_y = (cell % 24 + start_y).astype(F32)
        across, down = taper_of(
            cell_x - row_of(0, batch), cell_y - row_of(1, batch), level - row_of(2, batch), row_of(3, batch)
        )
        hor_ref[...] = across
        ver_ref[...] = 1.0 / (down * (MEM - 1))

    def some_begin(batch, anomaly, gain):
        chosen = select_ref[batch * OBS_B : (batch + 1) * OBS_B, :]
        kept = dot_nt(jnp.concatenate(split(anomaly), axis=0), chosen)
        first = lax.broadcasted_iota(jnp.int32, (MEM, 128), 1) < HALF
        high, low = kept[:MEM], kept[MEM:]
        upper = jnp.concatenate([jnp.where(first, high, 0.0), jnp.where(first, low, 0.0)], axis=1)
        lower = jnp.concatenate([jnp.where(first, 0.0, high), jnp.where(first, 0.0, low)], axis=1)
        both = jnp.concatenate([upper, lower], axis=0).astype(BF16)
        w1_ref[0:128, :] = both
        w1_ref[128:256, :] = both
        high, low = split(gain)
        kept = dot_nt(chosen, jnp.concatenate([high, high, low, low], axis=0))
        slot = lax.broadcasted_iota(jnp.int32, (128, 256), 0) // HALF
        member = (lax.broadcasted_iota(jnp.int32, (128, 256), 1) // MEM) % 2
        both = jnp.where(slot == member, kept, 0.0).astype(BF16)
        w2_ref[0:128, :] = both
        w2_ref[128:256, :] = both

    def lanes_of(step):
        return [pl.ds(pl.multiple_of(step * 256 + 128 * h, 128), 128) for h in range(2)]

    def all_step(batch, src_ref, step):
        lanes = lanes_of(step)
        state = jnp.concatenate([src_ref[:, lanes[0]], src_ref[:, lanes[1]]], axis=0)
        high, low = split(state)
        link = dot(jnp.concatenate([high, low], axis=1), w1_ref[0:256, :]) + dot(high, w1_ref[256:384, :])
        parts = []
        for h in range(2):
            sides = []
            for p in range(2):
                down = ver_ref[pl.ds(4 * step + 2 * h + p, 1), :]
                sides.append(
                    link[h * cells : (h + 1) * cells, p * 128 : p * 128 + 128] * hor_ref[...] * down
                )
            parts.append(jnp.concatenate(sides, axis=1))
        high, low = split(jnp.concatenate(parts, axis=0))
        wide = dot(high, w2_ref[...])
        state = state + (wide[:, :128] + wide[:, 128:] + dot(low, w2_ref[:, 0:128]))
        for h in range(2):
            o_ref[:, lanes[h]] = state[h * cells : (h + 1) * cells]

    def some_step(batch, src_ref, step):
        lanes = lanes_of(step)
        state = jnp.concatenate([src_ref[:, lanes[0]], src_ref[:, lanes[1]]], axis=0)
        link = dot(jnp.concatenate(split(state), axis=1), w1_ref[0:256, :])
        parts = []
        for h in range(2):
            rows = slice(h * cells, (h + 1) * cells)
            down = down_ref[pl.ds(16 * batch + 2 * step + h, 1), :]
            across = across_ref[batch * cells : (batch + 1) * cells, :]
            parts.append((link[rows, :128] + link[rows, 128:]) * (across * down))
        wide = dot(jnp.concatenate(split(jnp.concatenate(parts, axis=0)), axis=1), w2_ref[...])
        state = state + (wide[:, :128] + wide[:, 128:])
        for h in range(2):
            o_ref[:, lanes[h]] = state[h * cells : (h + 1) * cells]

    def process(begin, tile_step):
        anomaly = None
        for batch in range(NBATCH + 1):
            if batch < NBATCH:
                anomaly, direct, cross, rows = solve_begin(batch)
                near(batch, anomaly)
                values = flat(rows)
            else:
                values = ()

            def step_body(step, values):
                if batch > 0:
                    tile_step(batch - 1, f_ref if batch == 1 else o_ref, step)
                if batch < NBATCH:
                    values = flat(eliminate_eight(nested(values, 2)))
                return values

            values = lax.fori_loop(0, 8, step_body, values)
            if batch < NBATCH:
                solved = jnp.concatenate([row[1] for row in nested(values, 2)], axis=0)
                gain = direct - dot(cross, solved, HIGHEST)
                if batch < NBATCH - 1:
                    high = (batch + 1) * OBS_B
                    state_ref[:, high:] = state_ref[:, high:] + dot(
                        gain, near_ref[:, : NBATCH * OBS_B - high], HIGHEST
                    )
                begin(batch, anomaly, gain)

    fits = jnp.max(most_ref[...]) <= HALF

    @pl.when(fits)
    def _():
        process(some_begin, some_step)

    @pl.when(jnp.logical_not(fits))
    def _():
        process(all_begin, all_step)


def analyse(axes, forecast, *rest):
    cells = forecast.shape[0]
    return pl.pallas_call(
        functools.partial(analysis_kernel, axes),
        out_shape=jax.ShapeDtypeStruct(forecast.shape, F32),
        in_specs=[pl.BlockSpec(memory_space=pltpu.VMEM)] * 8,
        out_specs=pl.BlockSpec(memory_space=pltpu.VMEM),
        scratch_shapes=[
            pltpu.VMEM((MEM, NBATCH * OBS_B), F32),
            pltpu.VMEM((OBS_B, (NBATCH - 1) * OBS_B), F32),
            pltpu.VMEM((384, 256), BF16),
            pltpu.VMEM((256, 256), BF16),
            pltpu.VMEM((cells, OBS_B), F32),
            pltpu.VMEM((LEV, OBS_B), F32),
        ],
        compiler_params=pltpu.CompilerParams(vmem_limit_bytes=48 * 1024 * 1024),
        name="analysis",
    )(forecast, *rest)


MESH = pl.DeviceIdType.MESH


def tables(start_x, start_y, rows_ref, select_ref, across_ref, down_ref, most_ref):
    cells = across_ref.shape[0] // NBATCH
    most = jnp.zeros((8, 128), F32)
    square = (128, 128)
    before = (
        lax.broadcasted_iota(jnp.int32, square, 0) < lax.broadcasted_iota(jnp.int32, square, 1)
    ).astype(F32).astype(BF16)
    slot = (lax.broadcasted_iota(jnp.int32, square, 0) % HALF).astype(F32)
    cell = lax.broadcasted_iota(jnp.int32, (cells, 128), 0)
    cell_x, cell_y = (cell // 24).astype(F32), (cell % 24).astype(F32)
    level = 2 * lax.broadcasted_iota(jnp.int32, (LEV // 2, 128), 0)
    level = (level + lax.broadcasted_iota(jnp.int32, (LEV // 2, 128), 1) // HALF).astype(F32)
    kind = lax.broadcasted_iota(jnp.int32, (8, 128), 0)
    for batch in range(NBATCH):
        low = batch * OBS_B
        x, y, l, r = (rows_ref[i : i + 1, low : low + OBS_B] for i in range(4))
        x, y = x - start_x.astype(F32), y - start_y.astype(F32)
        dx = jnp.maximum(jnp.maximum(-x, x - 7.0), 0.0)
        dy = jnp.maximum(jnp.maximum(-y, y - 23.0), 0.0)
        reaches = dx * dx + dy * dy < r * r
        flags = jnp.broadcast_to(reaches.astype(F32), (8, 128))
        position = dot(flags.astype(BF16), before)[0:1]
        most = jnp.maximum(most, jnp.sum(flags, axis=1, keepdims=True))
        chosen = jnp.where((slot == position) & reaches, 1.0, 0.0).astype(BF16)
        select_ref[low : low + OBS_B, :] = chosen
        facts = jnp.where(kind == 0, x, jnp.where(kind == 1, y, jnp.where(kind == 2, l, jnp.where(kind == 3, r, 1.0))))
        kept = dot_nt(facts.astype(BF16), chosen)
        across, down = taper_of(
            cell_x - kept[0:1], cell_y - kept[1:2], level - kept[2:3], kept[3:4] + (1.0 - kept[4:5])
        )
        across_ref[batch * cells : (batch + 1) * cells, :] = across
        down_ref[batch * LEV // 2 : (batch + 1) * LEV // 2, :] = 1.0 / (down * (MEM - 1))
    most_ref[...] = most


def forecast_kernel(
    n_x, n_y,
    ens_hbm, w_hbm, cell_hbm, batch_hbm, radius_hbm, value_hbm, var_hbm, noise_hbm,
    f_ref, p_ref, rows_ref, cols_ref, select_ref, across_ref, down_ref, most_ref,
    ens_ref, w_ref, cell_ref, batch_ref, ints_ref, floats_ref,
    west_ref, east_ref, south_ref, north_ref, first_ref, last_ref,
    data_ref, spread_ref, point_ref, mix_ref, edge_ref, found_ref,
    part_ref, got_y_ref, sum_ref, got_x_ref, total_ref, all_ref,
    loads, halo_send, halo_recv, send_1, recv_1, send_2, recv_2, send_3, recv_3,
):
    gx, gy = lax.axis_index("gx"), lax.axis_index("gy")
    rows_x, rows_y = ens_ref.shape[0], ens_ref.shape[1]
    cells = rows_x * rows_y
    n_obs = batch_ref.shape[1]

    def peer(axis, index, count, step):
        return {axis: lax.rem(index + step, count)}

    small = [
        pltpu.make_async_copy(src, dst, loads.at[i])
        for i, (src, dst) in enumerate(
            (
                (batch_hbm, batch_ref),
                (cell_hbm, cell_ref),
                (noise_hbm, data_ref.at[8:72]),
                (radius_hbm, ints_ref),
                (value_hbm, floats_ref.at[0]),
                (var_hbm, floats_ref.at[1]),
            )
        )
    ]
    load_weights = pltpu.make_async_copy(w_hbm, w_ref, loads.at[6])
    load_tile = pltpu.make_async_copy(ens_hbm, ens_ref, loads.at[7])
    for copy in small:
        copy.start()
    load_tile.start()
    load_weights.start()

    barrier = pltpu.get_barrier_semaphore()
    for step in range(1, n_x):
        pl.semaphore_signal(barrier, inc=1, device_id=peer("gx", gx, n_x, step), device_id_type=MESH)
    for step in range(1, n_y):
        pl.semaphore_signal(barrier, inc=1, device_id=peer("gy", gy, n_y, step), device_id_type=MESH)

    for copy in small:
        copy.wait()
    data_ref[0:3, :] = cell_ref[...].astype(F32)
    data_ref[3:4, :] = ints_ref[...].astype(F32)
    data_ref[4:5, :] = floats_ref[0]
    data_ref[5:6, :] = floats_ref[1]
    data_ref[6:8, :] = jnp.zeros((2, n_obs), F32)
    data_ref[72:128, :] = jnp.zeros((56, n_obs), F32)
    square = (n_obs, n_obs)
    at_row, at_lane = lax.broadcasted_iota(jnp.int32, square, 0), lax.broadcasted_iota(jnp.int32, square, 1)
    before = (at_row < at_lane).astype(F32).astype(BF16)
    kind = lax.broadcasted_iota(jnp.int32, (8, n_obs), 0)
    same = (kind == batch_ref[...]).astype(F32)
    count = dot(same.astype(BF16), before)
    rank = jnp.sum(same * (count + (kind * OBS_B).astype(F32)), axis=0, keepdims=True)
    chosen = (at_row.astype(F32) == rank).astype(F32).astype(BF16)
    data = data_ref[...]
    high = data.astype(BF16)
    middle, low = split(data - high.astype(F32))
    thirds = dot_nt(chosen, jnp.concatenate([high, middle, low], axis=0))
    table = (thirds[:, 0:128] + thirds[:, 128:256]) + thirds[:, 256:384]
    cols_ref[...] = table[:, 0:8]
    rows_ref[...] = table.T[0:72]

    load_tile.wait()
    for x in range(rows_x):
        first_ref[x : x + 1, :] = ens_ref[x, 0:1, :]
        last_ref[x : x + 1, :] = ens_ref[x, rows_y - 1 : rows_y, :]

    pl.semaphore_wait(barrier, n_x + n_y - 2)

    def halo(slot, src, dst, axis, target):
        return pltpu.make_async_remote_copy(
            src_ref=src, dst_ref=dst, send_sem=halo_send.at[slot], recv_sem=halo_recv.at[slot],
            device_id={axis: target}, device_id_type=MESH,
        )

    copies = (
        (halo(0, ens_ref.at[rows_x - 1], west_ref, "gx", lax.rem(gx + 1, n_x)), gx < n_x - 1, gx > 0, west_ref),
        (halo(1, ens_ref.at[0], east_ref, "gx", lax.rem(gx + n_x - 1, n_x)), gx > 0, gx < n_x - 1, east_ref),
        (halo(2, last_ref, south_ref, "gy", lax.rem(gy + 1, n_y)), gy < n_y - 1, gy > 0, south_ref),
        (halo(3, first_ref, north_ref, "gy", lax.rem(gy + n_y - 1, n_y)), gy > 0, gy < n_y - 1, north_ref),
    )
    for copy, sends, _, _ in copies:
        pl.when(sends)(copy.start)

    load_weights.wait()
    for y in range(rows_y):
        merged = jnp.zeros((rows_x, 128), F32)
        group = lax.broadcasted_iota(jnp.int32, (rows_x, 128), 1) // LEV
        for k in range(4):
            block = w_ref[k, :, 128 * (y // 4) : 128 * (y // 4) + 128]
            low_lanes = pltpu.roll(block, 128 - 32 * (y % 4), 1) if y % 4 else block
            spread_ref[pl.ds(k * cells + y, rows_x, stride=rows_y), :] = low_lanes
            turn = (32 * k - 32 * (y % 4)) % 128
            merged = jnp.where(group == k, pltpu.roll(block, turn, 1) if turn else block, merged)
        point_ref[pl.ds(y, rows_x, stride=rows_y), :] = merged

    obs_x = table[:, 0:1] - (gx * rows_x).astype(F32)
    obs_y = table[:, 1:2] - (gy * rows_y).astype(F32)
    obs_l = table[:, 2:3]
    inside = (obs_x >= 0.0) & (obs_x < rows_x) & (obs_y >= 0.0) & (obs_y < rows_y)

    def place(value):
        return jnp.where(inside, value, -1.0)

    centre = obs_x * rows_y + obs_y
    at_west = place(jnp.where(obs_x > 0.0, centre - rows_y, cells + obs_y))
    at_east = place(jnp.where(obs_x < rows_x - 1.0, centre + rows_y, cells + rows_y + obs_y))
    at_south = place(jnp.where(obs_y > 0.0, centre - 1.0, cells + 2 * rows_y + obs_x))
    at_north = place(jnp.where(obs_y < rows_y - 1.0, centre + 1.0, cells + 2 * rows_y + rows_x + obs_x))
    centre = place(centre)
    lane = lax.broadcasted_iota(jnp.int32, (n_obs, 256), 1).astype(F32)
    is_centre = lane == centre
    high, low = split(point_ref[...])
    both = dot(
        is_centre.astype(F32).astype(BF16)[:, 0:cells], jnp.concatenate([high, low], axis=1)
    )
    mine = both[:, 0:128] + both[:, 128:256]
    lane_level = lax.broadcasted_iota(jnp.int32, (n_obs, 128), 1) % LEV
    mine = jnp.where(lane_level.astype(F32) == obs_l, mine, 0.0)
    high, low = split(mine)
    group = lax.broadcasted_iota(jnp.int32, (128, 512), 0) // LEV == lax.broadcasted_iota(jnp.int32, (128, 512), 1) // 128
    group = group.astype(F32).astype(BF16)
    coeffs = dot(jnp.concatenate([high, low], axis=1), jnp.concatenate([group, group], axis=0))
    coeffs = [jnp.concatenate([coeffs[:, 128 * k : 128 * k + 128]] * 2, axis=1) for k in range(4)]
    mix = jnp.where(is_centre, 1.0 - ((coeffs[0] + coeffs[1]) + (coeffs[2] + coeffs[3])), 0.0)
    for k, at in enumerate((at_west, at_east, at_south, at_north)):
        mix = jnp.where(lane == at, coeffs[k], mix)
    high, low = split(mix)
    mix_ref[:, 0:256] = high
    mix_ref[:, 256:512] = low
    edge_ref[:, 0:64] = high[:, 192:256]
    edge_ref[:, 64:128] = low[:, 192:256]
    edge_ref[:, 128:192] = high[:, 192:256]
    pair = jnp.floor(obs_l * 0.5)
    odd = obs_l - 2.0 * pair
    found_ref[...] = jnp.zeros(found_ref.shape, F32)

    def take(step, here):
        found = found_ref[...]
        for h in range(2):
            found = jnp.where(
                pair == (2 * step + h).astype(F32), found + here[:, h * 128 : h * 128 + 128], found
            )
        found_ref[...] = found

    def lanes_of(step):
        return pl.ds(pl.multiple_of(step * 256, 256), 256)

    def own_cells(step, carry):
        high, low = split(ens_ref[:, :, lanes_of(step)].reshape(cells, 256))
        take(
            step,
            dot(mix_ref[:, 0:cells], high)
            + dot(mix_ref[:, 256 : 256 + cells], high)
            + dot(mix_ref[:, 0:cells], low),
        )
        return carry

    lax.fori_loop(0, 8, own_cells, 0)

    for copy, _, receives, halo_ref in copies:
        pl.when(receives)(copy.wait_recv)

        @pl.when(jnp.logical_not(receives))
        def _():
            halo_ref[...] = jnp.zeros(halo_ref.shape, F32)

    def cells_beside(step, carry):
        lanes = lanes_of(step)
        high, low = split(
            jnp.concatenate([west_ref[:, lanes], east_ref[:, lanes], south_ref[:, lanes], north_ref[:, lanes]], axis=0)
        )
        take(step, dot(edge_ref[...], jnp.concatenate([high, high, low], axis=0)))
        return carry

    lax.fori_loop(0, 8, cells_beside, 0)

    def forecast_step(step, carry):
        lanes = lanes_of(step)
        level = lax.broadcasted_iota(jnp.int32, (128, 256), 0)
        column = lax.broadcasted_iota(jnp.int32, (128, 256), 1) // 64 + 4 * step
        ones = (level == column).astype(F32).astype(BF16)
        high, low = split(spread_ref[...])
        weights = dot(jnp.concatenate([high, low], axis=1), jnp.concatenate([ones, ones], axis=0))
        side = lax.broadcasted_iota(jnp.int32, (rows_y, 256), 0)
        for x in range(rows_x):
            q = ens_ref[x, :, lanes]
            west = west_ref[:, lanes] if x == 0 else ens_ref[x - 1, :, lanes]
            east = east_ref[:, lanes] if x == rows_x - 1 else ens_ref[x + 1, :, lanes]
            south = jnp.where(side == 0, south_ref[x : x + 1, lanes], pltpu.roll(q, 1, 0))
            north = jnp.where(side == rows_y - 1, north_ref[x : x + 1, lanes], pltpu.roll(q, rows_y - 1, 0))
            total = q
            for k, other in enumerate((west, east, south, north)):
                at = k * cells + x * rows_y
                total = total + weights[at : at + rows_y] * (other - q)
            f_ref[x * rows_y : x * rows_y + rows_y, lanes] = total
        return carry

    found = found_ref[...]
    turned = pltpu.roll(found, 64, 1)
    left = jnp.where(odd == 0.0, found, turned)
    right = jnp.where(odd == 0.0, turned, found)
    half = n_obs // 2
    side = lax.broadcasted_iota(jnp.int32, (half, 128), 1)
    part_ref[...] = jnp.where(side < 64, left[:half], right[half:])

    share = half // n_y

    def send(step, axis, index, count, src, dst, sends, recvs):
        return pltpu.make_async_remote_copy(
            src_ref=src, dst_ref=dst, send_sem=sends.at[step], recv_sem=recvs.at[step],
            device_id=peer(axis, index, count, step), device_id_type=MESH,
        )

    def rows_of(index):
        return pl.ds(pl.multiple_of(index * share, share), share)

    first = [
        send(s, "gy", gy, n_y, part_ref.at[rows_of(lax.rem(gy + s, n_y))], got_y_ref.at[s], send_1, recv_1)
        for s in range(1, n_y)
    ]
    for copy in first:
        copy.start()
    tables(gx * rows_x, gy * rows_y, rows_ref, select_ref, across_ref, down_ref, most_ref)
    lax.fori_loop(0, 2, forecast_step, 0)
    total = part_ref[rows_of(gy), :]
    for s, copy in enumerate(first, 1):
        copy.wait_recv()
        total = total + got_y_ref[s]
    sum_ref[...] = total
    second = [send(s, "gx", gx, n_x, sum_ref, got_x_ref.at[s], send_2, recv_2) for s in range(1, n_x)]
    for copy in second:
        copy.start()
    lax.fori_loop(2, 5, forecast_step, 0)
    for s, copy in enumerate(second, 1):
        copy.wait_recv()
        total = total + got_x_ref[s]
    total_ref[...] = total
    third = [
        send(s, "gy", gy, n_y, total_ref, all_ref.at[rows_of(gy)], send_3, recv_3) for s in range(1, n_y)
    ]
    for copy in third:
        copy.start()
    all_ref[rows_of(gy), :] = total
    lax.fori_loop(5, 8, forecast_step, 0)
    for copy, sends, _, _ in copies:
        pl.when(sends)(copy.wait_send)
    for copy in first + second:
        copy.wait_send()
    for copy in third:
        copy.wait_recv()
    p_ref[...] = all_ref[...]
    for copy in third:
        copy.wait_send()


def forecast_and_gather(n_x, n_y, ensemble, weights, obs_cell, obs_batch, obs_radius, obs_value, obs_noise, obs_var):
    rows_x, rows_y, width = ensemble.shape
    cells = rows_x * rows_y
    n_obs = obs_batch.shape[0]
    share = n_obs // 2 // n_y
    vmem = pl.BlockSpec(memory_space=pltpu.VMEM)
    dma = pltpu.SemaphoreType.DMA
    return pl.pallas_call(
        functools.partial(forecast_kernel, n_x, n_y),
        out_shape=(
            jax.ShapeDtypeStruct((cells, width), F32),
            jax.ShapeDtypeStruct((n_obs // 2, 128), F32),
            jax.ShapeDtypeStruct((72, n_obs), F32),
            jax.ShapeDtypeStruct((n_obs, 8), F32),
            jax.ShapeDtypeStruct((n_obs, 128), BF16),
            jax.ShapeDtypeStruct((NBATCH * cells, 128), F32),
            jax.ShapeDtypeStruct((NBATCH * LEV // 2, 128), F32),
            jax.ShapeDtypeStruct((8, 128), F32),
        ),
        in_specs=[pl.BlockSpec(memory_space=pltpu.HBM)] * 8,
        out_specs=(vmem,) * 8,
        scratch_shapes=[
            pltpu.VMEM(ensemble.shape, F32),
            pltpu.VMEM(weights.shape, F32),
            pltpu.VMEM(obs_cell.shape, jnp.int32),
            pltpu.VMEM((1, n_obs), jnp.int32),
            pltpu.VMEM((1, n_obs), jnp.int32),
            pltpu.VMEM((2, 1, n_obs), F32),
            pltpu.VMEM((rows_y, width), F32),
            pltpu.VMEM((rows_y, width), F32),
            pltpu.VMEM((rows_x, width), F32),
            pltpu.VMEM((rows_x, width), F32),
            pltpu.VMEM((rows_x, width), F32),
            pltpu.VMEM((rows_x, width), F32),
            pltpu.VMEM((128, n_obs), F32),
            pltpu.VMEM((4 * cells, 128), F32),
            pltpu.VMEM((cells, 128), F32),
            pltpu.VMEM((n_obs, 512), BF16),
            pltpu.VMEM((n_obs, 192), BF16),
            pltpu.VMEM((n_obs, 128), F32),
            pltpu.VMEM((n_obs // 2, 128), F32),
            pltpu.VMEM((n_y, share, 128), F32),
            pltpu.VMEM((share, 128), F32),
            pltpu.VMEM((n_x, share, 128), F32),
            pltpu.VMEM((share, 128), F32),
            pltpu.VMEM((n_obs // 2, 128), F32),
            dma((8,)), dma((4,)), dma((4,)),
            dma((n_y,)), dma((n_y,)), dma((n_x,)), dma((n_x,)), dma((n_y,)), dma((n_y,)),
        ],
        compiler_params=pltpu.CompilerParams(
            collective_id=0, has_side_effects=True, vmem_limit_bytes=48 * 1024 * 1024
        ),
        name="forecast_and_gather",
    )(
        *(
            pltpu.with_memory_space_constraint(value, pltpu.HBM)
            for value in (
                ensemble, weights, obs_cell, obs_batch.reshape(1, n_obs), obs_radius.reshape(1, n_obs),
                obs_value.reshape(1, n_obs), obs_var.reshape(1, n_obs), obs_noise,
            )
        )
    )


def solution(mesh):
    n_x, n_y = mesh.shape["gx"], mesh.shape["gy"]

    def body(ensemble, *rest):
        rows_x, rows_y, width = ensemble.shape
        found = forecast_and_gather(n_x, n_y, ensemble, *rest)
        analysis = analyse(
            lambda: (lax.axis_index("gx") * rows_x, lax.axis_index("gy") * rows_y), *found
        )
        return analysis.reshape(rows_x, rows_y, width)

    placed = (P("gx", "gy", None), P(None, "gx", "gy"), P(), P(), P(), P(), P(), P())
    return jax.shard_map(
        body, mesh=mesh, in_specs=placed, out_specs=P("gx", "gy", None), check_vma=False
    )
```

```python
import functools
import jax
import jax.numpy as jnp
from jax import lax
from jax.experimental import pallas as pl
from jax.experimental.pallas import tpu as pltpu
from jax.sharding import PartitionSpec as P

MEM = 64
LEV = 32
OBS_B = 128
HALF = 64
NBATCH = 4
HIGHEST = lax.Precision.HIGHEST
F32 = jnp.float32
BF16 = jnp.bfloat16


def dot(a, b, precision=None):
    return jnp.dot(a, b, preferred_element_type=F32, precision=precision)


def dot_nt(a, b, precision=None):
    return lax.dot_general(
        a, b, (((1,), (1,)), ((), ())), preferred_element_type=F32, precision=precision
    )


def split(value):
    high = value.astype(BF16)
    return high, (value - high.astype(F32)).astype(BF16)


def invert_two(a, b, d):
    inv = 1.0 / (a * d - b * b)
    return d * inv, -b * inv, a * inv


def invert_four(m):
    p00, p01, p11 = invert_two(m[0][0], m[1][0], m[1][1])
    x20, x21 = m[2][0] * p00 + m[2][1] * p01, m[2][0] * p01 + m[2][1] * p11
    x30, x31 = m[3][0] * p00 + m[3][1] * p01, m[3][0] * p01 + m[3][1] * p11
    s22 = m[2][2] - (x20 * m[2][0] + x21 * m[2][1])
    s32 = m[3][2] - (x30 * m[2][0] + x31 * m[2][1])
    s33 = m[3][3] - (x30 * m[3][0] + x31 * m[3][1])
    q22, q32, q33 = invert_two(s22, s32, s33)
    y20, y21 = q22 * x20 + q32 * x30, q22 * x21 + q32 * x31
    y30, y31 = q32 * x20 + q33 * x30, q32 * x21 + q33 * x31
    low = [
        [p00 + (x20 * y20 + x30 * y30)],
        [p01 + (x20 * y21 + x30 * y31), p11 + (x21 * y21 + x31 * y31)],
        [-y20, -y21, q22],
        [-y30, -y31, q32, q33],
    ]
    return [[low[max(i, j)][min(i, j)] for j in range(4)] for i in range(4)]


def total(terms):
    terms = list(terms)
    while len(terms) > 1:
        terms = [sum(terms[i + 1 : i + 2], terms[i]) for i in range(0, len(terms), 2)]
    return terms[0]


def eliminate_eight(rows, block):
    low = 8 * block
    shape = (8, 128)
    four = range(4)
    columns = [
        [jnp.broadcast_to(rows[v][0][:, low + j : low + j + 1], shape) for v in range(block, len(rows))]
        for j in range(8)
    ]

    def entry(i, j):
        return jnp.broadcast_to(columns[j][0][i : i + 1, :], shape)

    first = [[entry(i, j) for j in range(i + 1)] for i in four]
    cross = [[entry(4 + i, j) for j in four] for i in four]
    second = [[entry(4 + i, 4 + j) for j in range(i + 1)] for i in four]
    p = invert_four(first)
    x = [[total(cross[i][k] * p[k][j] for k in four) for j in four] for i in four]
    q = invert_four(
        [[second[i][j] - total(x[i][k] * cross[j][k] for k in four) for j in range(i + 1)] for i in four]
    )
    at = lax.broadcasted_iota(jnp.int32, shape, 0)
    result = [list(row) for row in rows]
    for col in range(2):
        r = [jnp.broadcast_to(rows[block][col][i : i + 1, :], shape) for i in range(8)]
        t = [r[4 + i] - total(x[i][k] * r[k] for k in four) for i in four]
        upper = [total(q[i][k] * t[k] for k in four) for i in four]
        lower = [
            total(p[i][k] * r[k] for k in four) - total(x[k][i] * upper[k] for k in four) for i in four
        ]
        solved = lower + upper
        for v in range(block + 1, len(rows)):
            result[v][col] = rows[v][col] - total(columns[k][v - block] * solved[k] for k in range(8))
        if col == 1:
            value = solved[0]
            for k in range(1, 8):
                value = jnp.where(at == k, solved[k], value)
            result[block][1] = value
    return result


def taper_of(dx, dy, dl, radius):
    across = jnp.maximum(1.0 - (dx * dx + dy * dy) / (radius * radius), 0.0)
    return across * across, 1.0 + (dl * 0.125) * (dl * 0.125)


def analysis_kernel(
    axes, f_ref, p_ref, rows_ref, cols_ref, select_ref, across_ref, down_ref, most_ref,
    o_ref, state_ref, near_ref, w1_ref, w2_ref, hor_ref, ver_ref,
):
    cells = f_ref.shape[0]
    start_x, start_y = axes()
    packed = p_ref[...].T
    state_ref[:, 0:256] = packed[:MEM]
    state_ref[:, 256:512] = packed[MEM:]

    def row_of(index, batch):
        return rows_ref[index : index + 1, batch * OBS_B : (batch + 1) * OBS_B]

    def solve_begin(batch):
        low = batch * OBS_B
        prior = state_ref[:, low : low + OBS_B]
        anomaly = prior - jnp.mean(prior, axis=0, keepdims=True)
        variance = row_of(5, batch)
        deviation = jnp.sqrt(variance)
        inv_dev = 1.0 / deviation
        noise = rows_ref[8:72, low : low + OBS_B]
        innovation = row_of(4, batch) + deviation * noise - prior
        scaled = anomaly * (inv_dev * (1.0 / (MEM - 1) ** 0.5))
        both = jnp.concatenate([scaled, innovation * inv_dev], axis=0)
        product = dot_nt(scaled, both, HIGHEST)
        eye = lax.broadcasted_iota(jnp.int32, (64, 128), 0) == lax.broadcasted_iota(jnp.int32, (64, 128), 1)
        system = product + eye.astype(F32)
        rhs = scaled * inv_dev
        rows = [[system[8 * v : 8 * v + 8], rhs[8 * v : 8 * v + 8]] for v in range(8)]
        return anomaly, innovation * (inv_dev * inv_dev), rows

    def near(batch, anomaly):
        low, high = batch * OBS_B, (batch + 1) * OBS_B
        if batch == NBATCH - 1:
            return
        links = dot(anomaly.T, state_ref[:, high:], HIGHEST)
        for later in range(batch + 1, NBATCH):
            cut = slice(later * OBS_B, (later + 1) * OBS_B)
            across, down = taper_of(
                cols_ref[low:high, 0:1] - rows_ref[0:1, cut],
                cols_ref[low:high, 1:2] - rows_ref[1:2, cut],
                cols_ref[low:high, 2:3] - rows_ref[2:3, cut],
                cols_ref[low:high, 3:4],
            )
            at = (later - batch - 1) * OBS_B
            near_ref[:, at : at + OBS_B] = links[:, at : at + OBS_B] * (across / (down * (MEM - 1)))

    def twice(value):
        zero = jnp.zeros(value.shape, value.dtype)
        return jnp.concatenate(
            [jnp.concatenate([value, zero], axis=1), jnp.concatenate([zero, value], axis=1)], axis=0
        )

    def all_begin(batch, anomaly, gain):
        high, low = split(anomaly)
        high_two = twice(high)
        w1_ref[0:128, :] = high_two
        w1_ref[128:256, :] = high_two
        w1_ref[256:384, :] = twice(low)
        high, low = split(gain.T)
        w2_ref[:, 0:128] = twice(high)
        w2_ref[:, 128:256] = twice(low)
        cell = lax.broadcasted_iota(jnp.int32, (cells, 1), 0)
        level = lax.broadcasted_iota(jnp.int32, (LEV, 1), 0).astype(F32)
        cell_x = (cell // 24 + start_x).astype(F32)
        cell_y = (cell % 24 + start_y).astype(F32)
        across, down = taper_of(
            cell_x - row_of(0, batch), cell_y - row_of(1, batch), level - row_of(2, batch), row_of(3, batch)
        )
        hor_ref[...] = across
        ver_ref[...] = 1.0 / (down * (MEM - 1))

    def some_begin(batch, anomaly, gain):
        chosen = select_ref[batch * OBS_B : (batch + 1) * OBS_B, :]
        kept = dot_nt(jnp.concatenate(split(anomaly), axis=0), chosen)
        first = lax.broadcasted_iota(jnp.int32, (MEM, 128), 1) < HALF
        high, low = kept[:MEM], kept[MEM:]
        upper = jnp.concatenate([jnp.where(first, high, 0.0), jnp.where(first, low, 0.0)], axis=1)
        lower = jnp.concatenate([jnp.where(first, 0.0, high), jnp.where(first, 0.0, low)], axis=1)
        both = jnp.concatenate([upper, lower], axis=0).astype(BF16)
        w1_ref[0:128, :] = both
        w1_ref[128:256, :] = both
        high, low = split(gain)
        kept = dot_nt(chosen, jnp.concatenate([high, high, low, low], axis=0))
        slot = lax.broadcasted_iota(jnp.int32, (128, 256), 0) // HALF
        member = (lax.broadcasted_iota(jnp.int32, (128, 256), 1) // MEM) % 2
        both = jnp.where(slot == member, kept, 0.0).astype(BF16)
        w2_ref[0:128, :] = both
        w2_ref[128:256, :] = both

    def lanes_of(step):
        return [pl.ds(step * 256 + 128 * h, 128) for h in range(2)]

    def all_step(batch, src_ref, step):
        lanes = lanes_of(step)
        state = jnp.concatenate([src_ref[:, lanes[0]], src_ref[:, lanes[1]]], axis=0)
        high, low = split(state)
        link = dot(jnp.concatenate([high, low], axis=1), w1_ref[0:256, :]) + dot(high, w1_ref[256:384, :])
        parts = []
        for h in range(2):
            sides = []
            for p in range(2):
                down = ver_ref[pl.ds(4 * step + 2 * h + p, 1), :]
                sides.append(
                    link[h * cells : (h + 1) * cells, p * 128 : p * 128 + 128] * hor_ref[...] * down
                )
            parts.append(jnp.concatenate(sides, axis=1))
        high, low = split(jnp.concatenate(parts, axis=0))
        wide = dot(high, w2_ref[...])
        state = state + (wide[:, :128] + wide[:, 128:] + dot(low, w2_ref[:, 0:128]))
        for h in range(2):
            o_ref[:, lanes[h]] = state[h * cells : (h + 1) * cells]

    def some_step(batch, src_ref, step):
        lanes = lanes_of(step)
        state = jnp.concatenate([src_ref[:, lanes[0]], src_ref[:, lanes[1]]], axis=0)
        link = dot(jnp.concatenate(split(state), axis=1), w1_ref[0:256, :])
        parts = []
        for h in range(2):
            rows = slice(h * cells, (h + 1) * cells)
            down = down_ref[pl.ds(16 * batch + 2 * step + h, 1), :]
            across = across_ref[batch * cells : (batch + 1) * cells, :]
            parts.append((link[rows, :128] + link[rows, 128:]) * (across * down))
        wide = dot(jnp.concatenate(split(jnp.concatenate(parts, axis=0)), axis=1), w2_ref[...])
        state = state + (wide[:, :128] + wide[:, 128:])
        for h in range(2):
            o_ref[:, lanes[h]] = state[h * cells : (h + 1) * cells]

    def process(begin, tile_step):
        anomaly = None
        for batch in range(NBATCH + 1):
            if batch < NBATCH:
                anomaly, direct, rows = solve_begin(batch)
                near(batch, anomaly)
            for step in range(8):
                if batch > 0:
                    tile_step(batch - 1, f_ref if batch == 1 else o_ref, step)
                if batch < NBATCH:
                    rows = eliminate_eight(rows, step)
            if batch < NBATCH:
                left = jnp.concatenate([row[0] for row in rows], axis=0).T[64:]
                right = jnp.concatenate([row[1] for row in rows], axis=0)
                gain = direct - dot(left, right, HIGHEST)
                if batch < NBATCH - 1:
                    high = (batch + 1) * OBS_B
                    state_ref[:, high:] = state_ref[:, high:] + dot(
                        gain, near_ref[:, : NBATCH * OBS_B - high], HIGHEST
                    )
                begin(batch, anomaly, gain)

    fits = jnp.max(most_ref[...]) <= HALF

    @pl.when(fits)
    def _():
        process(some_begin, some_step)

    @pl.when(jnp.logical_not(fits))
    def _():
        process(all_begin, all_step)


def analyse(axes, forecast, *rest):
    cells = forecast.shape[0]
    return pl.pallas_call(
        functools.partial(analysis_kernel, axes),
        out_shape=jax.ShapeDtypeStruct(forecast.shape, F32),
        in_specs=[pl.BlockSpec(memory_space=pltpu.VMEM)] * 8,
        out_specs=pl.BlockSpec(memory_space=pltpu.VMEM),
        scratch_shapes=[
            pltpu.VMEM((MEM, NBATCH * OBS_B), F32),
            pltpu.VMEM((OBS_B, (NBATCH - 1) * OBS_B), F32),
            pltpu.VMEM((384, 256), BF16),
            pltpu.VMEM((256, 256), BF16),
            pltpu.VMEM((cells, OBS_B), F32),
            pltpu.VMEM((LEV, OBS_B), F32),
        ],
        compiler_params=pltpu.CompilerParams(vmem_limit_bytes=48 * 1024 * 1024),
        name="analysis",
    )(forecast, *rest)


MESH = pl.DeviceIdType.MESH


def tables(start_x, start_y, rows_ref, select_ref, across_ref, down_ref, most_ref):
    cells = across_ref.shape[0] // NBATCH
    most = jnp.zeros((8, 128), F32)
    square = (128, 128)
    before = (
        lax.broadcasted_iota(jnp.int32, square, 0) < lax.broadcasted_iota(jnp.int32, square, 1)
    ).astype(F32).astype(BF16)
    slot = (lax.broadcasted_iota(jnp.int32, square, 0) % HALF).astype(F32)
    cell = lax.broadcasted_iota(jnp.int32, (cells, 128), 0)
    cell_x, cell_y = (cell // 24).astype(F32), (cell % 24).astype(F32)
    level = 2 * lax.broadcasted_iota(jnp.int32, (LEV // 2, 128), 0)
    level = (level + lax.broadcasted_iota(jnp.int32, (LEV // 2, 128), 1) // HALF).astype(F32)
    kind = lax.broadcasted_iota(jnp.int32, (8, 128), 0)
    for batch in range(NBATCH):
        low = batch * OBS_B
        x, y, l, r = (rows_ref[i : i + 1, low : low + OBS_B] for i in range(4))
        x, y = x - start_x.astype(F32), y - start_y.astype(F32)
        dx = jnp.maximum(jnp.maximum(-x, x - 7.0), 0.0)
        dy = jnp.maximum(jnp.maximum(-y, y - 23.0), 0.0)
        reaches = dx * dx + dy * dy < r * r
        flags = jnp.broadcast_to(reaches.astype(F32), (8, 128))
        position = dot(flags.astype(BF16), before)[0:1]
        most = jnp.maximum(most, jnp.sum(flags, axis=1, keepdims=True))
        chosen = jnp.where((slot == position) & reaches, 1.0, 0.0).astype(BF16)
        select_ref[low : low + OBS_B, :] = chosen
        facts = jnp.where(kind == 0, x, jnp.where(kind == 1, y, jnp.where(kind == 2, l, jnp.where(kind == 3, r, 1.0))))
        kept = dot_nt(facts.astype(BF16), chosen)
        across, down = taper_of(
            cell_x - kept[0:1], cell_y - kept[1:2], level - kept[2:3], kept[3:4] + (1.0 - kept[4:5])
        )
        across_ref[batch * cells : (batch + 1) * cells, :] = across
        down_ref[batch * LEV // 2 : (batch + 1) * LEV // 2, :] = 1.0 / (down * (MEM - 1))
    most_ref[...] = most


def forecast_kernel(
    n_x, n_y,
    ens_hbm, w_hbm, cell_hbm, batch_hbm, radius_hbm, value_hbm, var_hbm, noise_hbm,
    f_ref, p_ref, rows_ref, cols_ref, select_ref, across_ref, down_ref, most_ref,
    ens_ref, w_ref, cell_ref, batch_ref, ints_ref, floats_ref,
    west_ref, east_ref, south_ref, north_ref, first_ref, last_ref,
    data_ref, spread_ref, point_ref, mix_ref, edge_ref, found_ref,
    part_ref, got_y_ref, sum_ref, got_x_ref, total_ref, all_ref,
    loads, halo_send, halo_recv, send_1, recv_1, send_2, recv_2, send_3, recv_3,
):
    gx, gy = lax.axis_index("gx"), lax.axis_index("gy")
    rows_x, rows_y = ens_ref.shape[0], ens_ref.shape[1]
    cells = rows_x * rows_y
    n_obs = batch_ref.shape[1]

    def peer(axis, index, count, step):
        return {axis: lax.rem(index + step, count)}

    small = [
        pltpu.make_async_copy(src, dst, loads.at[i])
        for i, (src, dst) in enumerate(
            (
                (batch_hbm, batch_ref),
                (cell_hbm, cell_ref),
                (noise_hbm, data_ref.at[8:72]),
                (radius_hbm, ints_ref),
                (value_hbm, floats_ref.at[0]),
                (var_hbm, floats_ref.at[1]),
            )
        )
    ]
    load_weights = pltpu.make_async_copy(w_hbm, w_ref, loads.at[6])
    load_tile = pltpu.make_async_copy(ens_hbm, ens_ref, loads.at[7])
    for copy in small:
        copy.start()
    load_tile.start()
    load_weights.start()

    barrier = pltpu.get_barrier_semaphore()
    for step in range(1, n_x):
        pl.semaphore_signal(barrier, inc=1, device_id=peer("gx", gx, n_x, step), device_id_type=MESH)
    for step in range(1, n_y):
        pl.semaphore_signal(barrier, inc=1, device_id=peer("gy", gy, n_y, step), device_id_type=MESH)

    for copy in small:
        copy.wait()
    data_ref[0:3, :] = cell_ref[...].astype(F32)
    data_ref[3:4, :] = ints_ref[...].astype(F32)
    data_ref[4:5, :] = floats_ref[0]
    data_ref[5:6, :] = floats_ref[1]
    data_ref[6:8, :] = jnp.zeros((2, n_obs), F32)
    data_ref[72:128, :] = jnp.zeros((56, n_obs), F32)
    square = (n_obs, n_obs)
    at_row, at_lane = lax.broadcasted_iota(jnp.int32, square, 0), lax.broadcasted_iota(jnp.int32, square, 1)
    before = (at_row < at_lane).astype(F32).astype(BF16)
    kind = lax.broadcasted_iota(jnp.int32, (8, n_obs), 0)
    same = (kind == batch_ref[...]).astype(F32)
    count = dot(same.astype(BF16), before)
    rank = jnp.sum(same * (count + (kind * OBS_B).astype(F32)), axis=0, keepdims=True)
    chosen = (at_row.astype(F32) == rank).astype(F32).astype(BF16)
    data = data_ref[...]
    high = data.astype(BF16)
    middle, low = split(data - high.astype(F32))
    thirds = dot_nt(chosen, jnp.concatenate([high, middle, low], axis=0))
    table = (thirds[:, 0:128] + thirds[:, 128:256]) + thirds[:, 256:384]
    cols_ref[...] = table[:, 0:8]
    rows_ref[...] = table.T[0:72]

    load_tile.wait()
    for x in range(rows_x):
        first_ref[x : x + 1, :] = ens_ref[x, 0:1, :]
        last_ref[x : x + 1, :] = ens_ref[x, rows_y - 1 : rows_y, :]

    pl.semaphore_wait(barrier, n_x + n_y - 2)

    def halo(slot, src, dst, axis, target):
        return pltpu.make_async_remote_copy(
            src_ref=src, dst_ref=dst, send_sem=halo_send.at[slot], recv_sem=halo_recv.at[slot],
            device_id={axis: target}, device_id_type=MESH,
        )

    copies = (
        (halo(0, ens_ref.at[rows_x - 1], west_ref, "gx", lax.rem(gx + 1, n_x)), gx < n_x - 1, gx > 0, west_ref),
        (halo(1, ens_ref.at[0], east_ref, "gx", lax.rem(gx + n_x - 1, n_x)), gx > 0, gx < n_x - 1, east_ref),
        (halo(2, last_ref, south_ref, "gy", lax.rem(gy + 1, n_y)), gy < n_y - 1, gy > 0, south_ref),
        (halo(3, first_ref, north_ref, "gy", lax.rem(gy + n_y - 1, n_y)), gy > 0, gy < n_y - 1, north_ref),
    )
    for copy, sends, _, _ in copies:
        pl.when(sends)(copy.start)

    load_weights.wait()
    for y in range(rows_y):
        merged = jnp.zeros((rows_x, 128), F32)
        group = lax.broadcasted_iota(jnp.int32, (rows_x, 128), 1) // LEV
        for k in range(4):
            block = w_ref[k, :, 128 * (y // 4) : 128 * (y // 4) + 128]
            low_lanes = pltpu.roll(block, 128 - 32 * (y % 4), 1) if y % 4 else block
            spread_ref[pl.ds(k * cells + y, rows_x, stride=rows_y), :] = low_lanes
            turn = (32 * k - 32 * (y % 4)) % 128
            merged = jnp.where(group == k, pltpu.roll(block, turn, 1) if turn else block, merged)
        point_ref[pl.ds(y, rows_x, stride=rows_y), :] = merged

    obs_x = table[:, 0:1] - (gx * rows_x).astype(F32)
    obs_y = table[:, 1:2] - (gy * rows_y).astype(F32)
    obs_l = table[:, 2:3]
    inside = (obs_x >= 0.0) & (obs_x < rows_x) & (obs_y >= 0.0) & (obs_y < rows_y)

    def place(value):
        return jnp.where(inside, value, -1.0)

    centre = obs_x * rows_y + obs_y
    at_west = place(jnp.where(obs_x > 0.0, centre - rows_y, cells + obs_y))
    at_east = place(jnp.where(obs_x < rows_x - 1.0, centre + rows_y, cells + rows_y + obs_y))
    at_south = place(jnp.where(obs_y > 0.0, centre - 1.0, cells + 2 * rows_y + obs_x))
    at_north = place(jnp.where(obs_y < rows_y - 1.0, centre + 1.0, cells + 2 * rows_y + rows_x + obs_x))
    centre = place(centre)
    lane = lax.broadcasted_iota(jnp.int32, (n_obs, 256), 1).astype(F32)
    is_centre = lane == centre
    high, low = split(point_ref[...])
    both = dot(
        is_centre.astype(F32).astype(BF16)[:, 0:cells], jnp.concatenate([high, low], axis=1)
    )
    mine = both[:, 0:128] + both[:, 128:256]
    lane_level = lax.broadcasted_iota(jnp.int32, (n_obs, 128), 1) % LEV
    mine = jnp.where(lane_level.astype(F32) == obs_l, mine, 0.0)
    high, low = split(mine)
    group = lax.broadcasted_iota(jnp.int32, (128, 512), 0) // LEV == lax.broadcasted_iota(jnp.int32, (128, 512), 1) // 128
    group = group.astype(F32).astype(BF16)
    coeffs = dot(jnp.concatenate([high, low], axis=1), jnp.concatenate([group, group], axis=0))
    coeffs = [jnp.concatenate([coeffs[:, 128 * k : 128 * k + 128]] * 2, axis=1) for k in range(4)]
    mix = jnp.where(is_centre, 1.0 - ((coeffs[0] + coeffs[1]) + (coeffs[2] + coeffs[3])), 0.0)
    for k, at in enumerate((at_west, at_east, at_south, at_north)):
        mix = jnp.where(lane == at, coeffs[k], mix)
    high, low = split(mix)
    mix_ref[:, 0:256] = high
    mix_ref[:, 256:512] = low
    edge_ref[:, 0:64] = high[:, 192:256]
    edge_ref[:, 64:128] = low[:, 192:256]
    edge_ref[:, 128:192] = high[:, 192:256]
    pair = jnp.floor(obs_l * 0.5)
    odd = obs_l - 2.0 * pair
    found_ref[...] = jnp.zeros(found_ref.shape, F32)

    def take(step, here):
        found = found_ref[...]
        for h in range(2):
            found = jnp.where(
                pair == (2 * step + h).astype(F32), found + here[:, h * 128 : h * 128 + 128], found
            )
        found_ref[...] = found

    def lanes_of(step):
        return pl.ds(pl.multiple_of(step * 256, 256), 256)

    def own_cells(step, carry):
        high, low = split(ens_ref[:, :, lanes_of(step)].reshape(cells, 256))
        take(
            step,
            dot(mix_ref[:, 0:cells], high)
            + dot(mix_ref[:, 256 : 256 + cells], high)
            + dot(mix_ref[:, 0:cells], low),
        )
        return carry

    lax.fori_loop(0, 8, own_cells, 0)

    for copy, _, receives, halo_ref in copies:
        pl.when(receives)(copy.wait_recv)

        @pl.when(jnp.logical_not(receives))
        def _():
            halo_ref[...] = jnp.zeros(halo_ref.shape, F32)

    def cells_beside(step, carry):
        lanes = lanes_of(step)
        high, low = split(
            jnp.concatenate([west_ref[:, lanes], east_ref[:, lanes], south_ref[:, lanes], north_ref[:, lanes]], axis=0)
        )
        take(step, dot(edge_ref[...], jnp.concatenate([high, high, low], axis=0)))
        return carry

    lax.fori_loop(0, 8, cells_beside, 0)

    def forecast_step(step, carry):
        lanes = lanes_of(step)
        level = lax.broadcasted_iota(jnp.int32, (128, 256), 0)
        column = lax.broadcasted_iota(jnp.int32, (128, 256), 1) // 64 + 4 * step
        ones = (level == column).astype(F32).astype(BF16)
        high, low = split(spread_ref[...])
        weights = dot(jnp.concatenate([high, low], axis=1), jnp.concatenate([ones, ones], axis=0))
        side = lax.broadcasted_iota(jnp.int32, (rows_y, 256), 0)
        for x in range(rows_x):
            q = ens_ref[x, :, lanes]
            west = west_ref[:, lanes] if x == 0 else ens_ref[x - 1, :, lanes]
            east = east_ref[:, lanes] if x == rows_x - 1 else ens_ref[x + 1, :, lanes]
            south = jnp.where(side == 0, south_ref[x : x + 1, lanes], pltpu.roll(q, 1, 0))
            north = jnp.where(side == rows_y - 1, north_ref[x : x + 1, lanes], pltpu.roll(q, rows_y - 1, 0))
            total = q
            for k, other in enumerate((west, east, south, north)):
                at = k * cells + x * rows_y
                total = total + weights[at : at + rows_y] * (other - q)
            f_ref[x * rows_y : x * rows_y + rows_y, lanes] = total
        return carry

    found = found_ref[...]
    turned = pltpu.roll(found, 64, 1)
    left = jnp.where(odd == 0.0, found, turned)
    right = jnp.where(odd == 0.0, turned, found)
    half = n_obs // 2
    side = lax.broadcasted_iota(jnp.int32, (half, 128), 1)
    part_ref[...] = jnp.where(side < 64, left[:half], right[half:])

    share = half // n_y

    def send(step, axis, index, count, src, dst, sends, recvs):
        return pltpu.make_async_remote_copy(
            src_ref=src, dst_ref=dst, send_sem=sends.at[step], recv_sem=recvs.at[step],
            device_id=peer(axis, index, count, step), device_id_type=MESH,
        )

    def rows_of(index):
        return pl.ds(pl.multiple_of(index * share, share), share)

    first = [
        send(s, "gy", gy, n_y, part_ref.at[rows_of(lax.rem(gy + s, n_y))], got_y_ref.at[s], send_1, recv_1)
        for s in range(1, n_y)
    ]
    for copy in first:
        copy.start()
    tables(gx * rows_x, gy * rows_y, rows_ref, select_ref, across_ref, down_ref, most_ref)
    lax.fori_loop(0, 2, forecast_step, 0)
    total = part_ref[rows_of(gy), :]
    for s, copy in enumerate(first, 1):
        copy.wait_recv()
        total = total + got_y_ref[s]
    sum_ref[...] = total
    second = [send(s, "gx", gx, n_x, sum_ref, got_x_ref.at[s], send_2, recv_2) for s in range(1, n_x)]
    for copy in second:
        copy.start()
    lax.fori_loop(2, 5, forecast_step, 0)
    for s, copy in enumerate(second, 1):
        copy.wait_recv()
        total = total + got_x_ref[s]
    total_ref[...] = total
    third = [
        send(s, "gy", gy, n_y, total_ref, all_ref.at[rows_of(gy)], send_3, recv_3) for s in range(1, n_y)
    ]
    for copy in third:
        copy.start()
    all_ref[rows_of(gy), :] = total
    lax.fori_loop(5, 8, forecast_step, 0)
    for copy, sends, _, _ in copies:
        pl.when(sends)(copy.wait_send)
    for copy in first + second:
        copy.wait_send()
    for copy in third:
        copy.wait_recv()
    p_ref[...] = all_ref[...]
    for copy in third:
        copy.wait_send()


def forecast_and_gather(n_x, n_y, ensemble, weights, obs_cell, obs_batch, obs_radius, obs_value, obs_noise, obs_var):
    rows_x, rows_y, width = ensemble.shape
    cells = rows_x * rows_y
    n_obs = obs_batch.shape[0]
    share = n_obs // 2 // n_y
    vmem = pl.BlockSpec(memory_space=pltpu.VMEM)
    dma = pltpu.SemaphoreType.DMA
    return pl.pallas_call(
        functools.partial(forecast_kernel, n_x, n_y),
        out_shape=(
            jax.ShapeDtypeStruct((cells, width), F32),
            jax.ShapeDtypeStruct((n_obs // 2, 128), F32),
            jax.ShapeDtypeStruct((72, n_obs), F32),
            jax.ShapeDtypeStruct((n_obs, 8), F32),
            jax.ShapeDtypeStruct((n_obs, 128), BF16),
            jax.ShapeDtypeStruct((NBATCH * cells, 128), F32),
            jax.ShapeDtypeStruct((NBATCH * LEV // 2, 128), F32),
            jax.ShapeDtypeStruct((8, 128), F32),
        ),
        in_specs=[pl.BlockSpec(memory_space=pltpu.HBM)] * 8,
        out_specs=(vmem,) * 8,
        scratch_shapes=[
            pltpu.VMEM(ensemble.shape, F32),
            pltpu.VMEM(weights.shape, F32),
            pltpu.VMEM(obs_cell.shape, jnp.int32),
            pltpu.VMEM((1, n_obs), jnp.int32),
            pltpu.VMEM((1, n_obs), jnp.int32),
            pltpu.VMEM((2, 1, n_obs), F32),
            pltpu.VMEM((rows_y, width), F32),
            pltpu.VMEM((rows_y, width), F32),
            pltpu.VMEM((rows_x, width), F32),
            pltpu.VMEM((rows_x, width), F32),
            pltpu.VMEM((rows_x, width), F32),
            pltpu.VMEM((rows_x, width), F32),
            pltpu.VMEM((128, n_obs), F32),
            pltpu.VMEM((4 * cells, 128), F32),
            pltpu.VMEM((cells, 128), F32),
            pltpu.VMEM((n_obs, 512), BF16),
            pltpu.VMEM((n_obs, 192), BF16),
            pltpu.VMEM((n_obs, 128), F32),
            pltpu.VMEM((n_obs // 2, 128), F32),
            pltpu.VMEM((n_y, share, 128), F32),
            pltpu.VMEM((share, 128), F32),
            pltpu.VMEM((n_x, share, 128), F32),
            pltpu.VMEM((share, 128), F32),
            pltpu.VMEM((n_obs // 2, 128), F32),
            dma((8,)), dma((4,)), dma((4,)),
            dma((n_y,)), dma((n_y,)), dma((n_x,)), dma((n_x,)), dma((n_y,)), dma((n_y,)),
        ],
        compiler_params=pltpu.CompilerParams(
            collective_id=0, has_side_effects=True, vmem_limit_bytes=48 * 1024 * 1024
        ),
        name="forecast_and_gather",
    )(
        *(
            pltpu.with_memory_space_constraint(value, pltpu.HBM)
            for value in (
                ensemble, weights, obs_cell, obs_batch.reshape(1, n_obs), obs_radius.reshape(1, n_obs),
                obs_value.reshape(1, n_obs), obs_var.reshape(1, n_obs), obs_noise,
            )
        )
    )


def solution(mesh):
    n_x, n_y = mesh.shape["gx"], mesh.shape["gy"]

    def body(ensemble, *rest):
        rows_x, rows_y, width = ensemble.shape
        found = forecast_and_gather(n_x, n_y, ensemble, *rest)
        analysis = analyse(
            lambda: (lax.axis_index("gx") * rows_x, lax.axis_index("gy") * rows_y), *found
        )
        return analysis.reshape(rows_x, rows_y, width)

    placed = (P("gx", "gy", None), P(None, "gx", "gy"), P(), P(), P(), P(), P(), P())
    return jax.shard_map(
        body, mesh=mesh, in_specs=placed, out_specs=P("gx", "gy", None), check_vma=False
    )
```

```python
import functools
import jax
import jax.numpy as jnp
from jax import lax
from jax.experimental import pallas as pl
from jax.experimental.pallas import tpu as pltpu
from jax.sharding import PartitionSpec as P

MEM = 64
LEV = 32
OBS_B = 128
HALF = 64
NBATCH = 4
HIGHEST = lax.Precision.HIGHEST
F32 = jnp.float32
BF16 = jnp.bfloat16


def dot(a, b, precision=None):
    return jnp.dot(a, b, preferred_element_type=F32, precision=precision)


def dot_nt(a, b, precision=None):
    return lax.dot_general(
        a, b, (((1,), (1,)), ((), ())), preferred_element_type=F32, precision=precision
    )


def split(value):
    high = value.astype(BF16)
    return high, (value - high.astype(F32)).astype(BF16)


def invert_two(a, b, d):
    inv = 1.0 / (a * d - b * b)
    return d * inv, -b * inv, a * inv


def invert_four(m):
    p00, p01, p11 = invert_two(m[0][0], m[1][0], m[1][1])
    x20, x21 = m[2][0] * p00 + m[2][1] * p01, m[2][0] * p01 + m[2][1] * p11
    x30, x31 = m[3][0] * p00 + m[3][1] * p01, m[3][0] * p01 + m[3][1] * p11
    s22 = m[2][2] - (x20 * m[2][0] + x21 * m[2][1])
    s32 = m[3][2] - (x30 * m[2][0] + x31 * m[2][1])
    s33 = m[3][3] - (x30 * m[3][0] + x31 * m[3][1])
    q22, q32, q33 = invert_two(s22, s32, s33)
    y20, y21 = q22 * x20 + q32 * x30, q22 * x21 + q32 * x31
    y30, y31 = q32 * x20 + q33 * x30, q32 * x21 + q33 * x31
    low = [
        [p00 + (x20 * y20 + x30 * y30)],
        [p01 + (x20 * y21 + x30 * y31), p11 + (x21 * y21 + x31 * y31)],
        [-y20, -y21, q22],
        [-y30, -y31, q32, q33],
    ]
    return [[low[max(i, j)][min(i, j)] for j in range(4)] for i in range(4)]


def total(terms):
    terms = list(terms)
    while len(terms) > 1:
        terms = [sum(terms[i + 1 : i + 2], terms[i]) for i in range(0, len(terms), 2)]
    return terms[0]


def eliminate_eight(rows, block):
    low = 8 * block
    shape = (8, 128)
    four = range(4)
    columns = [
        [jnp.broadcast_to(rows[v][0][:, low + j : low + j + 1], shape) for v in range(block, len(rows))]
        for j in range(8)
    ]

    def entry(i, j):
        return jnp.broadcast_to(columns[j][0][i : i + 1, :], shape)

    first = [[entry(i, j) for j in range(i + 1)] for i in four]
    cross = [[entry(4 + i, j) for j in four] for i in four]
    second = [[entry(4 + i, 4 + j) for j in range(i + 1)] for i in four]
    p = invert_four(first)
    x = [[total(cross[i][k] * p[k][j] for k in four) for j in four] for i in four]
    q = invert_four(
        [[second[i][j] - total(x[i][k] * cross[j][k] for k in four) for j in range(i + 1)] for i in four]
    )
    at = lax.broadcasted_iota(jnp.int32, shape, 0)
    result = [list(row) for row in rows]
    for col in range(2):
        r = [jnp.broadcast_to(rows[block][col][i : i + 1, :], shape) for i in range(8)]
        t = [r[4 + i] - total(x[i][k] * r[k] for k in four) for i in four]
        upper = [total(q[i][k] * t[k] for k in four) for i in four]
        lower = [
            total(p[i][k] * r[k] for k in four) - total(x[k][i] * upper[k] for k in four) for i in four
        ]
        solved = lower + upper
        for v in range(block + 1, len(rows)):
            result[v][col] = rows[v][col] - total(columns[k][v - block] * solved[k] for k in range(8))
        if col == 1:
            value = solved[0]
            for k in range(1, 8):
                value = jnp.where(at == k, solved[k], value)
            result[block][1] = value
    return result


def taper_of(dx, dy, dl, radius):
    across = jnp.maximum(1.0 - (dx * dx + dy * dy) / (radius * radius), 0.0)
    return across * across, 1.0 + (dl * 0.125) * (dl * 0.125)


def analysis_kernel(
    axes, f_ref, p_ref, rows_ref, cols_ref, select_ref, across_ref, down_ref, most_ref,
    o_ref, state_ref, near_ref, w1_ref, w2_ref, hor_ref, ver_ref,
):
    cells = f_ref.shape[0]
    start_x, start_y = axes()
    packed = p_ref[...].T
    state_ref[:, 0:256] = packed[:MEM]
    state_ref[:, 256:512] = packed[MEM:]

    def row_of(index, batch):
        return rows_ref[index : index + 1, batch * OBS_B : (batch + 1) * OBS_B]

    def solve_begin(batch):
        low = batch * OBS_B
        prior = state_ref[:, low : low + OBS_B]
        anomaly = prior - jnp.mean(prior, axis=0, keepdims=True)
        variance = row_of(5, batch)
        deviation = jnp.sqrt(variance)
        inv_dev = 1.0 / deviation
        noise = rows_ref[8:72, low : low + OBS_B]
        innovation = row_of(4, batch) + deviation * noise - prior
        scaled = anomaly * (inv_dev * (1.0 / (MEM - 1) ** 0.5))
        both = jnp.concatenate([scaled, innovation * inv_dev], axis=0)
        product = dot_nt(scaled, both, HIGHEST)
        eye = lax.broadcasted_iota(jnp.int32, (64, 128), 0) == lax.broadcasted_iota(jnp.int32, (64, 128), 1)
        system = product + eye.astype(F32)
        rhs = scaled * inv_dev
        rows = [[system[8 * v : 8 * v + 8], rhs[8 * v : 8 * v + 8]] for v in range(8)]
        return anomaly, innovation * (inv_dev * inv_dev), rows

    def near(batch, anomaly):
        low, high = batch * OBS_B, (batch + 1) * OBS_B
        if batch == NBATCH - 1:
            return
        links = dot(anomaly.T, state_ref[:, high:], HIGHEST)
        for later in range(batch + 1, NBATCH):
            cut = slice(later * OBS_B, (later + 1) * OBS_B)
            across, down = taper_of(
                cols_ref[low:high, 0:1] - rows_ref[0:1, cut],
                cols_ref[low:high, 1:2] - rows_ref[1:2, cut],
                cols_ref[low:high, 2:3] - rows_ref[2:3, cut],
                cols_ref[low:high, 3:4],
            )
            at = (later - batch - 1) * OBS_B
            near_ref[:, at : at + OBS_B] = links[:, at : at + OBS_B] * (across / (down * (MEM - 1)))

    def twice(value):
        zero = jnp.zeros(value.shape, value.dtype)
        return jnp.concatenate(
            [jnp.concatenate([value, zero], axis=1), jnp.concatenate([zero, value], axis=1)], axis=0
        )

    def all_begin(batch, anomaly, gain):
        high, low = split(anomaly)
        high_two = twice(high)
        w1_ref[0:128, :] = high_two
        w1_ref[128:256, :] = high_two
        w1_ref[256:384, :] = twice(low)
        high, low = split(gain.T)
        w2_ref[:, 0:128] = twice(high)
        w2_ref[:, 128:256] = twice(low)
        cell = lax.broadcasted_iota(jnp.int32, (cells, 1), 0)
        level = lax.broadcasted_iota(jnp.int32, (LEV, 1), 0).astype(F32)
        cell_x = (cell // 24 + start_x).astype(F32)
        cell_y = (cell % 24 + start_y).astype(F32)
        across, down = taper_of(
            cell_x - row_of(0, batch), cell_y - row_of(1, batch), level - row_of(2, batch), row_of(3, batch)
        )
        hor_ref[...] = across
        ver_ref[...] = 1.0 / (down * (MEM - 1))

    def some_begin(batch, anomaly, gain):
        chosen = select_ref[batch * OBS_B : (batch + 1) * OBS_B, :]
        kept = dot_nt(jnp.concatenate(split(anomaly), axis=0), chosen)
        first = lax.broadcasted_iota(jnp.int32, (MEM, 128), 1) < HALF
        high, low = kept[:MEM], kept[MEM:]
        upper = jnp.concatenate([jnp.where(first, high, 0.0), jnp.where(first, low, 0.0)], axis=1)
        lower = jnp.concatenate([jnp.where(first, 0.0, high), jnp.where(first, 0.0, low)], axis=1)
        both = jnp.concatenate([upper, lower], axis=0).astype(BF16)
        w1_ref[0:128, :] = both
        w1_ref[128:256, :] = both
        high, low = split(gain)
        kept = dot_nt(chosen, jnp.concatenate([high, high, low, low], axis=0))
        slot = lax.broadcasted_iota(jnp.int32, (128, 256), 0) // HALF
        member = (lax.broadcasted_iota(jnp.int32, (128, 256), 1) // MEM) % 2
        both = jnp.where(slot == member, kept, 0.0).astype(BF16)
        w2_ref[0:128, :] = both
        w2_ref[128:256, :] = both

    def lanes_of(step):
        return [pl.ds(step * 256 + 128 * h, 128) for h in range(2)]

    def all_step(batch, src_ref, step):
        lanes = lanes_of(step)
        state = jnp.concatenate([src_ref[:, lanes[0]], src_ref[:, lanes[1]]], axis=0)
        high, low = split(state)
        link = dot(jnp.concatenate([high, low], axis=1), w1_ref[0:256, :]) + dot(high, w1_ref[256:384, :])
        parts = []
        for h in range(2):
            sides = []
            for p in range(2):
                down = ver_ref[pl.ds(4 * step + 2 * h + p, 1), :]
                sides.append(
                    link[h * cells : (h + 1) * cells, p * 128 : p * 128 + 128] * hor_ref[...] * down
                )
            parts.append(jnp.concatenate(sides, axis=1))
        high, low = split(jnp.concatenate(parts, axis=0))
        wide = dot(high, w2_ref[...])
        state = state + (wide[:, :128] + wide[:, 128:] + dot(low, w2_ref[:, 0:128]))
        for h in range(2):
            o_ref[:, lanes[h]] = state[h * cells : (h + 1) * cells]

    def some_step(batch, src_ref, step):
        lanes = lanes_of(step)
        state = jnp.concatenate([src_ref[:, lanes[0]], src_ref[:, lanes[1]]], axis=0)
        link = dot(jnp.concatenate(split(state), axis=1), w1_ref[0:256, :])
        parts = []
        for h in range(2):
            rows = slice(h * cells, (h + 1) * cells)
            down = down_ref[pl.ds(16 * batch + 2 * step + h, 1), :]
            across = across_ref[batch * cells : (batch + 1) * cells, :]
            parts.append((link[rows, :128] + link[rows, 128:]) * (across * down))
        wide = dot(jnp.concatenate(split(jnp.concatenate(parts, axis=0)), axis=1), w2_ref[...])
        state = state + (wide[:, :128] + wide[:, 128:])
        for h in range(2):
            o_ref[:, lanes[h]] = state[h * cells : (h + 1) * cells]

    def process(begin, tile_step):
        anomaly = None
        for batch in range(NBATCH + 1):
            if batch < NBATCH:
                anomaly, direct, rows = solve_begin(batch)
                near(batch, anomaly)
            for step in range(8):
                if batch > 0:
                    tile_step(batch - 1, f_ref if batch == 1 else o_ref, step)
                if batch < NBATCH:
                    rows = eliminate_eight(rows, step)
            if batch < NBATCH:
                left = jnp.concatenate([row[0] for row in rows], axis=0).T[64:]
                right = jnp.concatenate([row[1] for row in rows], axis=0)
                gain = direct - dot(left, right, HIGHEST)
                if batch < NBATCH - 1:
                    high = (batch + 1) * OBS_B
                    state_ref[:, high:] = state_ref[:, high:] + dot(
                        gain, near_ref[:, : NBATCH * OBS_B - high], HIGHEST
                    )
                begin(batch, anomaly, gain)

    fits = jnp.max(most_ref[...]) <= HALF

    @pl.when(fits)
    def _():
        process(some_begin, some_step)

    @pl.when(jnp.logical_not(fits))
    def _():
        process(all_begin, all_step)


def analyse(axes, forecast, *rest):
    cells = forecast.shape[0]
    return pl.pallas_call(
        functools.partial(analysis_kernel, axes),
        out_shape=jax.ShapeDtypeStruct(forecast.shape, F32),
        in_specs=[pl.BlockSpec(memory_space=pltpu.VMEM)] * 8,
        out_specs=pl.BlockSpec(memory_space=pltpu.VMEM),
        scratch_shapes=[
            pltpu.VMEM((MEM, NBATCH * OBS_B), F32),
            pltpu.VMEM((OBS_B, (NBATCH - 1) * OBS_B), F32),
            pltpu.VMEM((384, 256), BF16),
            pltpu.VMEM((256, 256), BF16),
            pltpu.VMEM((cells, OBS_B), F32),
            pltpu.VMEM((LEV, OBS_B), F32),
        ],
        compiler_params=pltpu.CompilerParams(vmem_limit_bytes=48 * 1024 * 1024),
        name="analysis",
    )(forecast, *rest)


MESH = pl.DeviceIdType.MESH


def tables(start_x, start_y, rows_ref, select_ref, across_ref, down_ref, most_ref):
    cells = across_ref.shape[0] // NBATCH
    most = jnp.zeros((8, 128), F32)
    square = (128, 128)
    before = (
        lax.broadcasted_iota(jnp.int32, square, 0) < lax.broadcasted_iota(jnp.int32, square, 1)
    ).astype(F32).astype(BF16)
    slot = (lax.broadcasted_iota(jnp.int32, square, 0) % HALF).astype(F32)
    cell = lax.broadcasted_iota(jnp.int32, (cells, 128), 0)
    cell_x, cell_y = (cell // 24).astype(F32), (cell % 24).astype(F32)
    level = 2 * lax.broadcasted_iota(jnp.int32, (LEV // 2, 128), 0)
    level = (level + lax.broadcasted_iota(jnp.int32, (LEV // 2, 128), 1) // HALF).astype(F32)
    kind = lax.broadcasted_iota(jnp.int32, (8, 128), 0)
    for batch in range(NBATCH):
        low = batch * OBS_B
        x, y, l, r = (rows_ref[i : i + 1, low : low + OBS_B] for i in range(4))
        x, y = x - start_x.astype(F32), y - start_y.astype(F32)
        dx = jnp.maximum(jnp.maximum(-x, x - 7.0), 0.0)
        dy = jnp.maximum(jnp.maximum(-y, y - 23.0), 0.0)
        reaches = dx * dx + dy * dy < r * r
        flags = jnp.broadcast_to(reaches.astype(F32), (8, 128))
        position = dot(flags.astype(BF16), before)[0:1]
        most = jnp.maximum(most, jnp.sum(flags, axis=1, keepdims=True))
        chosen = jnp.where((slot == position) & reaches, 1.0, 0.0).astype(BF16)
        select_ref[low : low + OBS_B, :] = chosen
        facts = jnp.where(kind == 0, x, jnp.where(kind == 1, y, jnp.where(kind == 2, l, jnp.where(kind == 3, r, 1.0))))
        kept = dot_nt(facts.astype(BF16), chosen)
        across, down = taper_of(
            cell_x - kept[0:1], cell_y - kept[1:2], level - kept[2:3], kept[3:4] + (1.0 - kept[4:5])
        )
        across_ref[batch * cells : (batch + 1) * cells, :] = across
        down_ref[batch * LEV // 2 : (batch + 1) * LEV // 2, :] = 1.0 / (down * (MEM - 1))
    most_ref[...] = most


def forecast_kernel(
    n_x, n_y,
    ens_hbm, w_hbm, cell_hbm, batch_hbm, radius_hbm, value_hbm, var_hbm, noise_hbm,
    f_ref, p_ref, rows_ref, cols_ref, select_ref, across_ref, down_ref, most_ref,
    ens_ref, w_ref, cell_ref, batch_ref, ints_ref, floats_ref,
    west_ref, east_ref, south_ref, north_ref, first_ref, last_ref,
    data_ref, chosen_ref, spread_ref, point_ref, mix_ref, edge_ref, found_ref,
    part_ref, got_y_ref, sum_ref, got_x_ref, total_ref, all_ref,
    loads, halo_send, halo_recv, send_1, recv_1, send_2, recv_2, send_3, recv_3,
):
    gx, gy = lax.axis_index("gx"), lax.axis_index("gy")
    rows_x, rows_y = ens_ref.shape[0], ens_ref.shape[1]
    cells = rows_x * rows_y
    n_obs = batch_ref.shape[1]

    n_z, n_side = n_x // 2, 4
    z, core, column, line = lax.div(gx, 2), lax.rem(gx, 2), lax.div(gy, n_side), lax.rem(gy, n_side)

    def hops(offset):
        return min(offset[0], n_z - offset[0]) + sum(min(d, n_side - d) for d in offset[2:]) + 0.1 * offset[1]

    layer = [(0, c, x, y) for c in range(2) for x in range(n_y // n_side) for y in range(n_side)][1:]
    layer = sorted(layer, key=hops, reverse=True)
    stack = sorted([(d, 0, 0, 0) for d in range(1, n_z)], key=hops, reverse=True)

    def place_of(offset):
        return (
            2 * lax.rem(z + offset[0], n_z) + lax.rem(core + offset[1], 2),
            n_side * lax.rem(column + offset[2], n_y // n_side) + lax.rem(line + offset[3], n_side),
        )

    small = [
        pltpu.make_async_copy(src, dst, loads.at[i])
        for i, (src, dst) in enumerate(
            (
                (batch_hbm, batch_ref),
                (cell_hbm, cell_ref),
                (noise_hbm, data_ref.at[8:72]),
                (radius_hbm, ints_ref),
                (value_hbm, floats_ref.at[0]),
                (var_hbm, floats_ref.at[1]),
            )
        )
    ]
    load_weights = pltpu.make_async_copy(w_hbm, w_ref, loads.at[6])
    load_tile = pltpu.make_async_copy(ens_hbm, ens_ref, loads.at[7])
    for copy in small:
        copy.start()
    load_tile.start()
    load_weights.start()

    barrier = pltpu.get_barrier_semaphore()
    beside_x = lax.rem(gx + 2 * core - 1 + n_x, n_x)
    for other in [(beside_x, gy)] + [place_of(offset) for offset in layer + stack]:
        pl.semaphore_signal(barrier, inc=1, device_id=other, device_id_type=MESH)

    square = (n_obs, n_obs)
    at_row, at_lane = lax.broadcasted_iota(jnp.int32, square, 0), lax.broadcasted_iota(jnp.int32, square, 1)
    before = (at_row < at_lane).astype(F32).astype(BF16)
    kind = lax.broadcasted_iota(jnp.int32, (8, n_obs), 0)
    for copy in small[:2]:
        copy.wait()
    same = (kind == batch_ref[...]).astype(F32)
    count = dot(same.astype(BF16), before)
    rank = jnp.sum(same * (count + (kind * OBS_B).astype(F32)), axis=0, keepdims=True)
    chosen_ref[...] = (at_row.astype(F32) == rank).astype(F32).astype(BF16)
    cell = cell_ref[...].astype(F32)
    half_y = jnp.floor(cell[1:2] * 0.5)
    facts = jnp.where(kind == 2, cell[1:2] - 2.0 * half_y, jnp.where(kind == 3, cell[2:3], 0.0))
    facts = jnp.where(kind == 0, cell[0:1], jnp.where(kind == 1, half_y, facts))
    where = dot_nt(chosen_ref[...], facts.astype(BF16))

    def order_all():
        for copy in small[2:]:
            copy.wait()
        data_ref[0:3, :] = cell_ref[...].astype(F32)
        data_ref[3:4, :] = ints_ref[...].astype(F32)
        data_ref[4:5, :] = floats_ref[0]
        data_ref[5:6, :] = floats_ref[1]
        data_ref[6:8, :] = jnp.zeros((2, n_obs), F32)
        data_ref[72:128, :] = jnp.zeros((56, n_obs), F32)
        data = data_ref[...]
        high = data.astype(BF16)
        middle, low = split(data - high.astype(F32))
        thirds = dot_nt(chosen_ref[...], jnp.concatenate([high, middle, low], axis=0))
        table = (thirds[:, 0:128] + thirds[:, 128:256]) + thirds[:, 256:384]
        cols_ref[...] = table[:, 0:8]
        rows_ref[...] = table.T[0:72]

    load_tile.wait()
    for x in range(rows_x):
        first_ref[x : x + 1, :] = ens_ref[x, 0:1, :]
        last_ref[x : x + 1, :] = ens_ref[x, rows_y - 1 : rows_y, :]

    pl.semaphore_wait(barrier, len(layer) + len(stack) + 1)

    def halo(slot, src, dst, axis, target):
        return pltpu.make_async_remote_copy(
            src_ref=src, dst_ref=dst, send_sem=halo_send.at[slot], recv_sem=halo_recv.at[slot],
            device_id={axis: target}, device_id_type=MESH,
        )

    copies = (
        (halo(0, ens_ref.at[rows_x - 1], west_ref, "gx", lax.rem(gx + 1, n_x)), gx < n_x - 1, gx > 0, west_ref),
        (halo(1, ens_ref.at[0], east_ref, "gx", lax.rem(gx + n_x - 1, n_x)), gx > 0, gx < n_x - 1, east_ref),
        (halo(2, last_ref, south_ref, "gy", lax.rem(gy + 1, n_y)), gy < n_y - 1, gy > 0, south_ref),
        (halo(3, first_ref, north_ref, "gy", lax.rem(gy + n_y - 1, n_y)), gy > 0, gy < n_y - 1, north_ref),
    )
    for copy, sends, _, _ in copies:
        pl.when(sends)(copy.start)

    load_weights.wait()
    for y in range(rows_y):
        merged = jnp.zeros((rows_x, 128), F32)
        group = lax.broadcasted_iota(jnp.int32, (rows_x, 128), 1) // LEV
        for k in range(4):
            block = w_ref[k, :, 128 * (y // 4) : 128 * (y // 4) + 128]
            low_lanes = pltpu.roll(block, 128 - 32 * (y % 4), 1) if y % 4 else block
            spread_ref[pl.ds(k * cells + y, rows_x, stride=rows_y), :] = low_lanes
            turn = (32 * k - 32 * (y % 4)) % 128
            merged = jnp.where(group == k, pltpu.roll(block, turn, 1) if turn else block, merged)
        point_ref[pl.ds(y, rows_x, stride=rows_y), :] = merged

    obs_x = where[:, 0:1] - (gx * rows_x).astype(F32)
    obs_y = 2.0 * where[:, 1:2] + where[:, 2:3] - (gy * rows_y).astype(F32)
    obs_l = where[:, 3:4]
    inside = (obs_x >= 0.0) & (obs_x < rows_x) & (obs_y >= 0.0) & (obs_y < rows_y)

    def place(value):
        return jnp.where(inside, value, -1.0)

    centre = obs_x * rows_y + obs_y
    at_west = place(jnp.where(obs_x > 0.0, centre - rows_y, cells + obs_y))
    at_east = place(jnp.where(obs_x < rows_x - 1.0, centre + rows_y, cells + rows_y + obs_y))
    at_south = place(jnp.where(obs_y > 0.0, centre - 1.0, cells + 2 * rows_y + obs_x))
    at_north = place(jnp.where(obs_y < rows_y - 1.0, centre + 1.0, cells + 2 * rows_y + rows_x + obs_x))
    centre = place(centre)
    lane = lax.broadcasted_iota(jnp.int32, (n_obs, 256), 1).astype(F32)
    is_centre = lane == centre
    high, low = split(point_ref[...])
    both = dot(
        is_centre.astype(F32).astype(BF16)[:, 0:cells], jnp.concatenate([high, low], axis=1)
    )
    mine = both[:, 0:128] + both[:, 128:256]
    lane_level = lax.broadcasted_iota(jnp.int32, (n_obs, 128), 1) % LEV
    mine = jnp.where(lane_level.astype(F32) == obs_l, mine, 0.0)
    high, low = split(mine)
    group = lax.broadcasted_iota(jnp.int32, (128, 512), 0) // LEV == lax.broadcasted_iota(jnp.int32, (128, 512), 1) // 128
    group = group.astype(F32).astype(BF16)
    coeffs = dot(jnp.concatenate([high, low], axis=1), jnp.concatenate([group, group], axis=0))
    coeffs = [jnp.concatenate([coeffs[:, 128 * k : 128 * k + 128]] * 2, axis=1) for k in range(4)]
    mix = jnp.where(is_centre, 1.0 - ((coeffs[0] + coeffs[1]) + (coeffs[2] + coeffs[3])), 0.0)
    for k, at in enumerate((at_west, at_east, at_south, at_north)):
        mix = jnp.where(lane == at, coeffs[k], mix)
    high, low = split(mix)
    mix_ref[:, 0:256] = high
    mix_ref[:, 256:512] = low
    edge_ref[:, 0:64] = high[:, 192:256]
    edge_ref[:, 64:128] = low[:, 192:256]
    edge_ref[:, 128:192] = high[:, 192:256]
    pair = jnp.floor(obs_l * 0.5)
    odd = obs_l - 2.0 * pair
    found_ref[...] = jnp.zeros(found_ref.shape, F32)

    def take(step, here):
        found = found_ref[...]
        for h in range(2):
            found = jnp.where(
                pair == 2.0 * step + h, found + here[:, h * 128 : h * 128 + 128], found
            )
        found_ref[...] = found

    def lanes_of(step):
        return pl.ds(step * 256, 256)

    def own_cells(step):
        high, low = split(ens_ref[:, :, lanes_of(step)].reshape(cells, 256))
        take(
            step,
            dot(mix_ref[:, 0:cells], high)
            + dot(mix_ref[:, 256 : 256 + cells], high)
            + dot(mix_ref[:, 0:cells], low),
        )

    for step in range(8):
        own_cells(step)

    for copy, _, receives, halo_ref in copies:
        pl.when(receives)(copy.wait_recv)

        @pl.when(jnp.logical_not(receives))
        def _():
            halo_ref[...] = jnp.zeros(halo_ref.shape, F32)

    def cells_beside(step):
        lanes = lanes_of(step)
        high, low = split(
            jnp.concatenate([west_ref[:, lanes], east_ref[:, lanes], south_ref[:, lanes], north_ref[:, lanes]], axis=0)
        )
        take(step, dot(edge_ref[...], jnp.concatenate([high, high, low], axis=0)))

    for step in range(8):
        cells_beside(step)

    def forecast_step(step):
        lanes = lanes_of(step)
        level = lax.broadcasted_iota(jnp.int32, (128, 256), 0)
        column = lax.broadcasted_iota(jnp.int32, (128, 256), 1) // 64 + 4 * step
        ones = (level == column).astype(F32).astype(BF16)
        high, low = split(spread_ref[...])
        weights = dot(jnp.concatenate([high, low], axis=1), jnp.concatenate([ones, ones], axis=0))
        side = lax.broadcasted_iota(jnp.int32, (rows_y, 256), 0)
        for x in range(rows_x):
            q = ens_ref[x, :, lanes]
            west = west_ref[:, lanes] if x == 0 else ens_ref[x - 1, :, lanes]
            east = east_ref[:, lanes] if x == rows_x - 1 else ens_ref[x + 1, :, lanes]
            south = jnp.where(side == 0, south_ref[x : x + 1, lanes], pltpu.roll(q, 1, 0))
            north = jnp.where(side == rows_y - 1, north_ref[x : x + 1, lanes], pltpu.roll(q, rows_y - 1, 0))
            total = q
            for k, other in enumerate((west, east, south, north)):
                at = k * cells + x * rows_y
                total = total + weights[at : at + rows_y] * (other - q)
            f_ref[x * rows_y : x * rows_y + rows_y, lanes] = total

    found = found_ref[...]
    turned = pltpu.roll(found, 64, 1)
    left = jnp.where(odd == 0.0, found, turned)
    right = jnp.where(odd == 0.0, turned, found)
    half = n_obs // 2
    side = lax.broadcasted_iota(jnp.int32, (half, 128), 1)
    part_ref[...] = jnp.where(side < 64, left[:half], right[half:])

    share = half // (len(layer) + 1)

    def rows_of(place):
        return pl.ds(pl.multiple_of((lax.rem(place[0], 2) * n_y + place[1]) * share, share), share)

    def send(slot, offset, src, dst, sends, recvs):
        return pltpu.make_async_remote_copy(
            src_ref=src, dst_ref=dst, send_sem=sends.at[slot], recv_sem=recvs.at[slot],
            device_id=place_of(offset), device_id_type=MESH,
        )

    first = [
        send(s, offset, part_ref.at[rows_of(place_of(offset))], got_y_ref.at[s], send_1, recv_1)
        for s, offset in enumerate(layer)
    ]
    for copy in first:
        copy.start()
    order_all()
    tables(gx * rows_x, gy * rows_y, rows_ref, select_ref, across_ref, down_ref, most_ref)
    mine = rows_of((gx, gy))
    total = part_ref[mine, :]
    for s, copy in enumerate(first):
        copy.wait_recv()
        total = total + got_y_ref[s]
    sum_ref[...] = total
    second = [send(s, offset, sum_ref, got_x_ref.at[s], send_2, recv_2) for s, offset in enumerate(stack)]
    for copy in second:
        copy.start()
    for step in range(0, 5):
        forecast_step(step)
    for s, copy in enumerate(second):
        copy.wait_recv()
        total = total + got_x_ref[s]
    total_ref[...] = total
    third = [send(s, offset, total_ref, all_ref.at[mine], send_3, recv_3) for s, offset in enumerate(layer)]
    for copy in third:
        copy.start()
    all_ref[mine, :] = total
    for step in range(5, 8):
        forecast_step(step)
    for copy, sends, _, _ in copies:
        pl.when(sends)(copy.wait_send)
    for copy in first + second:
        copy.wait_send()
    for copy in third:
        copy.wait_recv()
    p_ref[...] = all_ref[...]
    for copy in third:
        copy.wait_send()


def forecast_and_gather(n_x, n_y, ensemble, weights, obs_cell, obs_batch, obs_radius, obs_value, obs_noise, obs_var):
    rows_x, rows_y, width = ensemble.shape
    cells = rows_x * rows_y
    n_obs = obs_batch.shape[0]
    layer, stack = 2 * n_y, n_x // 2
    share = n_obs // 2 // layer
    vmem = pl.BlockSpec(memory_space=pltpu.VMEM)
    dma = pltpu.SemaphoreType.DMA
    return pl.pallas_call(
        functools.partial(forecast_kernel, n_x, n_y),
        out_shape=(
            jax.ShapeDtypeStruct((cells, width), F32),
            jax.ShapeDtypeStruct((n_obs // 2, 128), F32),
            jax.ShapeDtypeStruct((72, n_obs), F32),
            jax.ShapeDtypeStruct((n_obs, 8), F32),
            jax.ShapeDtypeStruct((n_obs, 128), BF16),
            jax.ShapeDtypeStruct((NBATCH * cells, 128), F32),
            jax.ShapeDtypeStruct((NBATCH * LEV // 2, 128), F32),
            jax.ShapeDtypeStruct((8, 128), F32),
        ),
        in_specs=[pl.BlockSpec(memory_space=pltpu.HBM)] * 8,
        out_specs=(vmem,) * 8,
        scratch_shapes=[
            pltpu.VMEM(ensemble.shape, F32),
            pltpu.VMEM(weights.shape, F32),
            pltpu.VMEM(obs_cell.shape, jnp.int32),
            pltpu.VMEM((1, n_obs), jnp.int32),
            pltpu.VMEM((1, n_obs), jnp.int32),
            pltpu.VMEM((2, 1, n_obs), F32),
            pltpu.VMEM((rows_y, width), F32),
            pltpu.VMEM((rows_y, width), F32),
            pltpu.VMEM((rows_x, width), F32),
            pltpu.VMEM((rows_x, width), F32),
            pltpu.VMEM((rows_x, width), F32),
            pltpu.VMEM((rows_x, width), F32),
            pltpu.VMEM((128, n_obs), F32),
            pltpu.VMEM((n_obs, n_obs), BF16),
            pltpu.VMEM((4 * cells, 128), F32),
            pltpu.VMEM((cells, 128), F32),
            pltpu.VMEM((n_obs, 512), BF16),
            pltpu.VMEM((n_obs, 192), BF16),
            pltpu.VMEM((n_obs, 128), F32),
            pltpu.VMEM((n_obs // 2, 128), F32),
            pltpu.VMEM((layer - 1, share, 128), F32),
            pltpu.VMEM((share, 128), F32),
            pltpu.VMEM((stack - 1, share, 128), F32),
            pltpu.VMEM((share, 128), F32),
            pltpu.VMEM((n_obs // 2, 128), F32),
            dma((8,)), dma((4,)), dma((4,)),
            dma((layer - 1,)), dma((layer - 1,)), dma((stack - 1,)), dma((stack - 1,)),
            dma((layer - 1,)), dma((layer - 1,)),
        ],
        compiler_params=pltpu.CompilerParams(
            collective_id=0, has_side_effects=True, vmem_limit_bytes=48 * 1024 * 1024
        ),
        name="forecast_and_gather",
    )(
        *(
            pltpu.with_memory_space_constraint(value, pltpu.HBM)
            for value in (
                ensemble, weights, obs_cell, obs_batch.reshape(1, n_obs), obs_radius.reshape(1, n_obs),
                obs_value.reshape(1, n_obs), obs_var.reshape(1, n_obs), obs_noise,
            )
        )
    )


def solution(mesh):
    n_x, n_y = mesh.shape["gx"], mesh.shape["gy"]

    def body(ensemble, *rest):
        rows_x, rows_y, width = ensemble.shape
        found = forecast_and_gather(n_x, n_y, ensemble, *rest)
        analysis = analyse(
            lambda: (lax.axis_index("gx") * rows_x, lax.axis_index("gy") * rows_y), *found
        )
        return analysis.reshape(rows_x, rows_y, width)

    placed = (P("gx", "gy", None), P(None, "gx", "gy"), P(), P(), P(), P(), P(), P())
    return jax.shard_map(
        body, mesh=mesh, in_specs=placed, out_specs=P("gx", "gy", None), check_vma=False
    )
```

```python
import functools
import jax
import jax.numpy as jnp
from jax import lax
from jax.experimental import pallas as pl
from jax.experimental.pallas import tpu as pltpu
from jax.sharding import PartitionSpec as P

MEM = 64
LEV = 32
OBS_B = 128
HALF = 64
NBATCH = 4
HIGHEST = lax.Precision.HIGHEST
F32 = jnp.float32
BF16 = jnp.bfloat16


def dot(a, b, precision=None):
    return jnp.dot(a, b, preferred_element_type=F32, precision=precision)


def dot_nt(a, b, precision=None):
    return lax.dot_general(
        a, b, (((1,), (1,)), ((), ())), preferred_element_type=F32, precision=precision
    )


def split(value):
    high = value.astype(BF16)
    return high, (value - high.astype(F32)).astype(BF16)


def invert_two(a, b, d):
    inv = 1.0 / (a * d - b * b)
    return d * inv, -b * inv, a * inv


def invert_four(m):
    p00, p01, p11 = invert_two(m[0][0], m[1][0], m[1][1])
    x20, x21 = m[2][0] * p00 + m[2][1] * p01, m[2][0] * p01 + m[2][1] * p11
    x30, x31 = m[3][0] * p00 + m[3][1] * p01, m[3][0] * p01 + m[3][1] * p11
    s22 = m[2][2] - (x20 * m[2][0] + x21 * m[2][1])
    s32 = m[3][2] - (x30 * m[2][0] + x31 * m[2][1])
    s33 = m[3][3] - (x30 * m[3][0] + x31 * m[3][1])
    q22, q32, q33 = invert_two(s22, s32, s33)
    y20, y21 = q22 * x20 + q32 * x30, q22 * x21 + q32 * x31
    y30, y31 = q32 * x20 + q33 * x30, q32 * x21 + q33 * x31
    low = [
        [p00 + (x20 * y20 + x30 * y30)],
        [p01 + (x20 * y21 + x30 * y31), p11 + (x21 * y21 + x31 * y31)],
        [-y20, -y21, q22],
        [-y30, -y31, q32, q33],
    ]
    return [[low[max(i, j)][min(i, j)] for j in range(4)] for i in range(4)]


def total(terms):
    terms = list(terms)
    while len(terms) > 1:
        terms = [sum(terms[i + 1 : i + 2], terms[i]) for i in range(0, len(terms), 2)]
    return terms[0]


def eliminate_eight(rows, block):
    low = 8 * block
    shape = (8, 128)
    four = range(4)
    columns = [
        [jnp.take_along_axis(rows[v][0], jnp.full(shape, low + j, jnp.int32), axis=1, mode='promise_in_bounds') for v in range(block, len(rows))]
        for j in range(8)
    ]

    def entry(i, j):
        return jnp.broadcast_to(columns[j][0][i : i + 1, :], shape)

    first = [[entry(i, j) for j in range(i + 1)] for i in four]
    cross = [[entry(4 + i, j) for j in four] for i in four]
    second = [[entry(4 + i, 4 + j) for j in range(i + 1)] for i in four]
    p = invert_four(first)
    x = [[total(cross[i][k] * p[k][j] for k in four) for j in four] for i in four]
    q = invert_four(
        [[second[i][j] - total(x[i][k] * cross[j][k] for k in four) for j in range(i + 1)] for i in four]
    )
    at = lax.broadcasted_iota(jnp.int32, shape, 0)
    result = [list(row) for row in rows]
    for col in range(2):
        r = [jnp.broadcast_to(rows[block][col][i : i + 1, :], shape) for i in range(8)]
        t = [r[4 + i] - total(x[i][k] * r[k] for k in four) for i in four]
        upper = [total(q[i][k] * t[k] for k in four) for i in four]
        lower = [
            total(p[i][k] * r[k] for k in four) - total(x[k][i] * upper[k] for k in four) for i in four
        ]
        solved = lower + upper
        for v in range(block + 1, len(rows)):
            result[v][col] = rows[v][col] - total(columns[k][v - block] * solved[k] for k in range(8))
        if col == 1:
            value = solved[0]
            for k in range(1, 8):
                value = jnp.where(at == k, solved[k], value)
            result[block][1] = value
    return result


def taper_of(dx, dy, dl, radius):
    across = jnp.maximum(1.0 - (dx * dx + dy * dy) / (radius * radius), 0.0)
    return across * across, 1.0 + (dl * 0.125) * (dl * 0.125)


def analysis_kernel(
    axes, f_ref, p_ref, rows_ref, cols_ref, select_ref, across_ref, down_ref, most_ref,
    o_ref, state_ref, near_ref, w1_ref, w2_ref, hor_ref, ver_ref,
):
    cells = f_ref.shape[0]
    start_x, start_y = axes()
    packed = p_ref[...].T
    state_ref[:, 0:256] = packed[:MEM]
    state_ref[:, 256:512] = packed[MEM:]

    def row_of(index, batch):
        return rows_ref[index : index + 1, batch * OBS_B : (batch + 1) * OBS_B]

    def solve_begin(batch):
        low = batch * OBS_B
        prior = state_ref[:, low : low + OBS_B]
        anomaly = prior - jnp.mean(prior, axis=0, keepdims=True)
        variance = row_of(5, batch)
        deviation = jnp.sqrt(variance)
        inv_dev = 1.0 / deviation
        noise = rows_ref[8:72, low : low + OBS_B]
        innovation = row_of(4, batch) + deviation * noise - prior
        scaled = anomaly * (inv_dev * (1.0 / (MEM - 1) ** 0.5))
        both = jnp.concatenate([scaled, innovation * inv_dev], axis=0)
        product = dot_nt(scaled, both, HIGHEST)
        eye = lax.broadcasted_iota(jnp.int32, (64, 128), 0) == lax.broadcasted_iota(jnp.int32, (64, 128), 1)
        system = product + eye.astype(F32)
        rhs = scaled * inv_dev
        rows = [[system[8 * v : 8 * v + 8], rhs[8 * v : 8 * v + 8]] for v in range(8)]
        return anomaly, innovation * (inv_dev * inv_dev), rows

    def near(batch, anomaly):
        low, high = batch * OBS_B, (batch + 1) * OBS_B
        if batch == NBATCH - 1:
            return
        links = dot(anomaly.T, state_ref[:, high:], HIGHEST)
        for later in range(batch + 1, NBATCH):
            cut = slice(later * OBS_B, (later + 1) * OBS_B)
            across, down = taper_of(
                cols_ref[low:high, 0:1] - rows_ref[0:1, cut],
                cols_ref[low:high, 1:2] - rows_ref[1:2, cut],
                cols_ref[low:high, 2:3] - rows_ref[2:3, cut],
                cols_ref[low:high, 3:4],
            )
            at = (later - batch - 1) * OBS_B
            near_ref[:, at : at + OBS_B] = links[:, at : at + OBS_B] * (across / (down * (MEM - 1)))

    def twice(value):
        zero = jnp.zeros(value.shape, value.dtype)
        return jnp.concatenate(
            [jnp.concatenate([value, zero], axis=1), jnp.concatenate([zero, value], axis=1)], axis=0
        )

    def all_begin(batch, anomaly, gain):
        high, low = split(anomaly)
        high_two = twice(high)
        w1_ref[0:128, :] = high_two
        w1_ref[128:256, :] = high_two
        w1_ref[256:384, :] = twice(low)
        high, low = split(gain.T)
        w2_ref[:, 0:128] = twice(high)
        w2_ref[:, 128:256] = twice(low)
        cell = lax.broadcasted_iota(jnp.int32, (cells, 1), 0)
        level = lax.broadcasted_iota(jnp.int32, (LEV, 1), 0).astype(F32)
        cell_x = (cell // 24 + start_x).astype(F32)
        cell_y = (cell % 24 + start_y).astype(F32)
        across, down = taper_of(
            cell_x - row_of(0, batch), cell_y - row_of(1, batch), level - row_of(2, batch), row_of(3, batch)
        )
        hor_ref[...] = across
        ver_ref[...] = 1.0 / (down * (MEM - 1))

    def some_begin(batch, anomaly, gain):
        chosen = select_ref[batch * OBS_B : (batch + 1) * OBS_B, :]
        kept = dot_nt(jnp.concatenate(split(anomaly), axis=0), chosen)
        first = lax.broadcasted_iota(jnp.int32, (MEM, 128), 1) < HALF
        high, low = kept[:MEM], kept[MEM:]
        upper = jnp.concatenate([jnp.where(first, high, 0.0), jnp.where(first, low, 0.0)], axis=1)
        lower = jnp.concatenate([jnp.where(first, 0.0, high), jnp.where(first, 0.0, low)], axis=1)
        both = jnp.concatenate([upper, lower], axis=0).astype(BF16)
        w1_ref[0:128, :] = both
        w1_ref[128:256, :] = both
        high, low = split(gain)
        kept = dot_nt(chosen, jnp.concatenate([high, high, low, low], axis=0))
        slot = lax.broadcasted_iota(jnp.int32, (128, 256), 0) // HALF
        member = (lax.broadcasted_iota(jnp.int32, (128, 256), 1) // MEM) % 2
        both = jnp.where(slot == member, kept, 0.0).astype(BF16)
        w2_ref[0:128, :] = both
        w2_ref[128:256, :] = both

    def lanes_of(step):
        return [pl.ds(step * 256 + 128 * h, 128) for h in range(2)]

    def all_step(batch, src_ref, step):
        lanes = lanes_of(step)
        state = jnp.concatenate([src_ref[:, lanes[0]], src_ref[:, lanes[1]]], axis=0)
        high, low = split(state)
        link = dot(jnp.concatenate([high, low], axis=1), w1_ref[0:256, :]) + dot(high, w1_ref[256:384, :])
        parts = []
        for h in range(2):
            sides = []
            for p in range(2):
                down = ver_ref[pl.ds(4 * step + 2 * h + p, 1), :]
                sides.append(
                    link[h * cells : (h + 1) * cells, p * 128 : p * 128 + 128] * hor_ref[...] * down
                )
            parts.append(jnp.concatenate(sides, axis=1))
        high, low = split(jnp.concatenate(parts, axis=0))
        wide = dot(high, w2_ref[...])
        state = state + (wide[:, :128] + wide[:, 128:] + dot(low, w2_ref[:, 0:128]))
        for h in range(2):
            o_ref[:, lanes[h]] = state[h * cells : (h + 1) * cells]

    def some_step(batch, src_ref, step):
        lanes = lanes_of(step)
        state = jnp.concatenate([src_ref[:, lanes[0]], src_ref[:, lanes[1]]], axis=0)
        link = dot(jnp.concatenate(split(state), axis=1), w1_ref[0:256, :])
        parts = []
        for h in range(2):
            rows = slice(h * cells, (h + 1) * cells)
            down = down_ref[pl.ds(16 * batch + 2 * step + h, 1), :]
            across = across_ref[batch * cells : (batch + 1) * cells, :]
            parts.append((link[rows, :128] + link[rows, 128:]) * (across * down))
        wide = dot(jnp.concatenate(split(jnp.concatenate(parts, axis=0)), axis=1), w2_ref[...])
        state = state + (wide[:, :128] + wide[:, 128:])
        for h in range(2):
            o_ref[:, lanes[h]] = state[h * cells : (h + 1) * cells]

    def process(begin, tile_step):
        anomaly = None
        for batch in range(NBATCH + 1):
            if batch < NBATCH:
                anomaly, direct, rows = solve_begin(batch)
                near(batch, anomaly)
            for step in range(8):
                if batch > 0:
                    tile_step(batch - 1, f_ref if batch == 1 else o_ref, step)
                if batch < NBATCH:
                    rows = eliminate_eight(rows, step)
            if batch < NBATCH:
                left = jnp.concatenate([row[0] for row in rows], axis=0).T[64:]
                right = jnp.concatenate([row[1] for row in rows], axis=0)
                gain = direct - dot(left, right, HIGHEST)
                if batch < NBATCH - 1:
                    high = (batch + 1) * OBS_B
                    state_ref[:, high:] = state_ref[:, high:] + dot(
                        gain, near_ref[:, : NBATCH * OBS_B - high], HIGHEST
                    )
                begin(batch, anomaly, gain)

    fits = jnp.max(most_ref[...]) <= HALF

    @pl.when(fits)
    def _():
        process(some_begin, some_step)

    @pl.when(jnp.logical_not(fits))
    def _():
        process(all_begin, all_step)


def analyse(axes, forecast, *rest):
    cells = forecast.shape[0]
    return pl.pallas_call(
        functools.partial(analysis_kernel, axes),
        out_shape=jax.ShapeDtypeStruct(forecast.shape, F32),
        in_specs=[pl.BlockSpec(memory_space=pltpu.VMEM)] * 8,
        out_specs=pl.BlockSpec(memory_space=pltpu.VMEM),
        scratch_shapes=[
            pltpu.VMEM((MEM, NBATCH * OBS_B), F32),
            pltpu.VMEM((OBS_B, (NBATCH - 1) * OBS_B), F32),
            pltpu.VMEM((384, 256), BF16),
            pltpu.VMEM((256, 256), BF16),
            pltpu.VMEM((cells, OBS_B), F32),
            pltpu.VMEM((LEV, OBS_B), F32),
        ],
        compiler_params=pltpu.CompilerParams(vmem_limit_bytes=48 * 1024 * 1024),
        name="analysis",
    )(forecast, *rest)


MESH = pl.DeviceIdType.MESH


def tables(start_x, start_y, rows_ref, select_ref, across_ref, down_ref, most_ref):
    cells = across_ref.shape[0] // NBATCH
    most = jnp.zeros((8, 128), F32)
    square = (128, 128)
    before = (
        lax.broadcasted_iota(jnp.int32, square, 0) < lax.broadcasted_iota(jnp.int32, square, 1)
    ).astype(F32).astype(BF16)
    slot = (lax.broadcasted_iota(jnp.int32, square, 0) % HALF).astype(F32)
    cell = lax.broadcasted_iota(jnp.int32, (cells, 128), 0)
    cell_x, cell_y = (cell // 24).astype(F32), (cell % 24).astype(F32)
    level = 2 * lax.broadcasted_iota(jnp.int32, (LEV // 2, 128), 0)
    level = (level + lax.broadcasted_iota(jnp.int32, (LEV // 2, 128), 1) // HALF).astype(F32)
    kind = lax.broadcasted_iota(jnp.int32, (8, 128), 0)
    for batch in range(NBATCH):
        low = batch * OBS_B
        x, y, l, r = (rows_ref[i : i + 1, low : low + OBS_B] for i in range(4))
        x, y = x - start_x.astype(F32), y - start_y.astype(F32)
        dx = jnp.maximum(jnp.maximum(-x, x - 7.0), 0.0)
        dy = jnp.maximum(jnp.maximum(-y, y - 23.0), 0.0)
        reaches = dx * dx + dy * dy < r * r
        flags = jnp.broadcast_to(reaches.astype(F32), (8, 128))
        position = dot(flags.astype(BF16), before)[0:1]
        most = jnp.maximum(most, jnp.sum(flags, axis=1, keepdims=True))
        chosen = jnp.where((slot == position) & reaches, 1.0, 0.0).astype(BF16)
        select_ref[low : low + OBS_B, :] = chosen
        facts = jnp.where(kind == 0, x, jnp.where(kind == 1, y, jnp.where(kind == 2, l, jnp.where(kind == 3, r, 1.0))))
        kept = dot_nt(facts.astype(BF16), chosen)
        across, down = taper_of(
            cell_x - kept[0:1], cell_y - kept[1:2], level - kept[2:3], kept[3:4] + (1.0 - kept[4:5])
        )
        across_ref[batch * cells : (batch + 1) * cells, :] = across
        down_ref[batch * LEV // 2 : (batch + 1) * LEV // 2, :] = 1.0 / (down * (MEM - 1))
    most_ref[...] = most


def forecast_kernel(
    n_x, n_y,
    ens_hbm, w_hbm, cell_hbm, batch_hbm, radius_hbm, value_hbm, var_hbm, noise_hbm,
    f_ref, p_ref, rows_ref, cols_ref, select_ref, across_ref, down_ref, most_ref,
    ens_ref, w_ref, cell_ref, batch_ref, ints_ref, floats_ref,
    west_ref, east_ref, south_ref, north_ref, first_ref, last_ref,
    data_ref, chosen_ref, spread_ref, point_ref, mix_ref, edge_ref, found_ref,
    part_ref, got_y_ref, sum_ref, got_x_ref, total_ref, all_ref,
    loads, halo_send, halo_recv, send_1, recv_1, send_2, recv_2, send_3, recv_3,
):
    gx, gy = lax.axis_index("gx"), lax.axis_index("gy")
    rows_x, rows_y = ens_ref.shape[0], ens_ref.shape[1]
    cells = rows_x * rows_y
    n_obs = batch_ref.shape[1]

    n_z, n_side = n_x // 2, 4
    z, core, column, line = lax.div(gx, 2), lax.rem(gx, 2), lax.div(gy, n_side), lax.rem(gy, n_side)

    def hops(offset):
        return min(offset[0], n_z - offset[0]) + sum(min(d, n_side - d) for d in offset[2:]) + 0.1 * offset[1]

    layer = [(0, c, x, y) for c in range(2) for x in range(n_y // n_side) for y in range(n_side)][1:]
    layer = sorted(layer, key=hops, reverse=True)
    stack = sorted([(d, 0, 0, 0) for d in range(1, n_z)], key=hops, reverse=True)

    def place_of(offset):
        return (
            2 * lax.rem(z + offset[0], n_z) + lax.rem(core + offset[1], 2),
            n_side * lax.rem(column + offset[2], n_y // n_side) + lax.rem(line + offset[3], n_side),
        )

    small = [
        pltpu.make_async_copy(src, dst, loads.at[i])
        for i, (src, dst) in enumerate(
            (
                (batch_hbm, batch_ref),
                (cell_hbm, cell_ref),
                (noise_hbm, data_ref.at[8:72]),
                (radius_hbm, ints_ref),
                (value_hbm, floats_ref.at[0]),
                (var_hbm, floats_ref.at[1]),
            )
        )
    ]
    load_weights = pltpu.make_async_copy(w_hbm, w_ref, loads.at[6])
    load_tile = pltpu.make_async_copy(ens_hbm, ens_ref, loads.at[7])
    for copy in small:
        copy.start()
    load_tile.start()
    load_weights.start()

    barrier = pltpu.get_barrier_semaphore()
    beside_x = lax.rem(gx + 2 * core - 1 + n_x, n_x)
    for other in [(beside_x, gy)] + [place_of(offset) for offset in layer + stack]:
        pl.semaphore_signal(barrier, inc=1, device_id=other, device_id_type=MESH)

    square = (n_obs, n_obs)
    at_row, at_lane = lax.broadcasted_iota(jnp.int32, square, 0), lax.broadcasted_iota(jnp.int32, square, 1)
    before = (at_row < at_lane).astype(F32).astype(BF16)
    kind = lax.broadcasted_iota(jnp.int32, (8, n_obs), 0)
    for copy in small[:2]:
        copy.wait()
    same = (kind == batch_ref[...]).astype(F32)
    count = dot(same.astype(BF16), before)
    rank = jnp.sum(same * (count + (kind * OBS_B).astype(F32)), axis=0, keepdims=True)
    chosen_ref[...] = (at_row.astype(F32) == rank).astype(F32).astype(BF16)
    cell = cell_ref[...].astype(F32)
    half_y = jnp.floor(cell[1:2] * 0.5)
    facts = jnp.where(kind == 2, cell[1:2] - 2.0 * half_y, jnp.where(kind == 3, cell[2:3], 0.0))
    facts = jnp.where(kind == 0, cell[0:1], jnp.where(kind == 1, half_y, facts))
    where = dot_nt(chosen_ref[...], facts.astype(BF16))

    def order_all():
        for copy in small[2:]:
            copy.wait()
        data_ref[0:3, :] = cell_ref[...].astype(F32)
        data_ref[3:4, :] = ints_ref[...].astype(F32)
        data_ref[4:5, :] = floats_ref[0]
        data_ref[5:6, :] = floats_ref[1]
        data_ref[6:8, :] = jnp.zeros((2, n_obs), F32)
        data_ref[72:128, :] = jnp.zeros((56, n_obs), F32)
        data = data_ref[...]
        high = data.astype(BF16)
        middle, low = split(data - high.astype(F32))
        thirds = dot_nt(chosen_ref[...], jnp.concatenate([high, middle, low], axis=0))
        table = (thirds[:, 0:128] + thirds[:, 128:256]) + thirds[:, 256:384]
        cols_ref[...] = table[:, 0:8]
        rows_ref[...] = table.T[0:72]

    load_tile.wait()
    for x in range(rows_x):
        first_ref[x : x + 1, :] = ens_ref[x, 0:1, :]
        last_ref[x : x + 1, :] = ens_ref[x, rows_y - 1 : rows_y, :]

    pl.semaphore_wait(barrier, len(layer) + len(stack) + 1)

    def halo(slot, src, dst, axis, target):
        return pltpu.make_async_remote_copy(
            src_ref=src, dst_ref=dst, send_sem=halo_send.at[slot], recv_sem=halo_recv.at[slot],
            device_id={axis: target}, device_id_type=MESH,
        )

    copies = (
        (halo(0, ens_ref.at[rows_x - 1], west_ref, "gx", lax.rem(gx + 1, n_x)), gx < n_x - 1, gx > 0, west_ref),
        (halo(1, ens_ref.at[0], east_ref, "gx", lax.rem(gx + n_x - 1, n_x)), gx > 0, gx < n_x - 1, east_ref),
        (halo(2, last_ref, south_ref, "gy", lax.rem(gy + 1, n_y)), gy < n_y - 1, gy > 0, south_ref),
        (halo(3, first_ref, north_ref, "gy", lax.rem(gy + n_y - 1, n_y)), gy > 0, gy < n_y - 1, north_ref),
    )
    for copy, sends, _, _ in copies:
        pl.when(sends)(copy.start)

    load_weights.wait()
    for y in range(rows_y):
        merged = jnp.zeros((rows_x, 128), F32)
        group = lax.broadcasted_iota(jnp.int32, (rows_x, 128), 1) // LEV
        for k in range(4):
            block = w_ref[k, :, 128 * (y // 4) : 128 * (y // 4) + 128]
            low_lanes = pltpu.roll(block, 128 - 32 * (y % 4), 1) if y % 4 else block
            spread_ref[pl.ds(k * cells + y, rows_x, stride=rows_y), :] = low_lanes
            turn = (32 * k - 32 * (y % 4)) % 128
            merged = jnp.where(group == k, pltpu.roll(block, turn, 1) if turn else block, merged)
        point_ref[pl.ds(y, rows_x, stride=rows_y), :] = merged

    obs_x = where[:, 0:1] - (gx * rows_x).astype(F32)
    obs_y = 2.0 * where[:, 1:2] + where[:, 2:3] - (gy * rows_y).astype(F32)
    obs_l = where[:, 3:4]
    inside = (obs_x >= 0.0) & (obs_x < rows_x) & (obs_y >= 0.0) & (obs_y < rows_y)

    def place(value):
        return jnp.where(inside, value, -1.0)

    centre = obs_x * rows_y + obs_y
    at_west = place(jnp.where(obs_x > 0.0, centre - rows_y, cells + obs_y))
    at_east = place(jnp.where(obs_x < rows_x - 1.0, centre + rows_y, cells + rows_y + obs_y))
    at_south = place(jnp.where(obs_y > 0.0, centre - 1.0, cells + 2 * rows_y + obs_x))
    at_north = place(jnp.where(obs_y < rows_y - 1.0, centre + 1.0, cells + 2 * rows_y + rows_x + obs_x))
    centre = place(centre)
    lane = lax.broadcasted_iota(jnp.int32, (n_obs, 256), 1).astype(F32)
    is_centre = lane == centre
    high, low = split(point_ref[...])
    both = dot(
        is_centre.astype(F32).astype(BF16)[:, 0:cells], jnp.concatenate([high, low], axis=1)
    )
    mine = both[:, 0:128] + both[:, 128:256]
    lane_level = lax.broadcasted_iota(jnp.int32, (n_obs, 128), 1) % LEV
    mine = jnp.where(lane_level.astype(F32) == obs_l, mine, 0.0)
    high, low = split(mine)
    group = lax.broadcasted_iota(jnp.int32, (128, 512), 0) // LEV == lax.broadcasted_iota(jnp.int32, (128, 512), 1) // 128
    group = group.astype(F32).astype(BF16)
    coeffs = dot(jnp.concatenate([high, low], axis=1), jnp.concatenate([group, group], axis=0))
    coeffs = [jnp.concatenate([coeffs[:, 128 * k : 128 * k + 128]] * 2, axis=1) for k in range(4)]
    mix = jnp.where(is_centre, 1.0 - ((coeffs[0] + coeffs[1]) + (coeffs[2] + coeffs[3])), 0.0)
    for k, at in enumerate((at_west, at_east, at_south, at_north)):
        mix = jnp.where(lane == at, coeffs[k], mix)
    high, low = split(mix)
    mix_ref[:, 0:256] = high
    mix_ref[:, 256:512] = low
    edge_ref[:, 0:64] = high[:, 192:256]
    edge_ref[:, 64:128] = low[:, 192:256]
    edge_ref[:, 128:192] = high[:, 192:256]
    pair = jnp.floor(obs_l * 0.5)
    odd = obs_l - 2.0 * pair
    found_ref[...] = jnp.zeros(found_ref.shape, F32)

    def take(step, here):
        found = found_ref[...]
        for h in range(2):
            found = jnp.where(
                pair == 2.0 * step + h, found + here[:, h * 128 : h * 128 + 128], found
            )
        found_ref[...] = found

    def lanes_of(step):
        return pl.ds(step * 256, 256)

    def own_cells(step):
        high, low = split(ens_ref[:, :, lanes_of(step)].reshape(cells, 256))
        take(
            step,
            dot(mix_ref[:, 0:cells], high)
            + dot(mix_ref[:, 256 : 256 + cells], high)
            + dot(mix_ref[:, 0:cells], low),
        )

    for step in range(8):
        own_cells(step)

    for copy, _, receives, halo_ref in copies:
        pl.when(receives)(copy.wait_recv)

        @pl.when(jnp.logical_not(receives))
        def _():
            halo_ref[...] = jnp.zeros(halo_ref.shape, F32)

    def cells_beside(step):
        lanes = lanes_of(step)
        high, low = split(
            jnp.concatenate([west_ref[:, lanes], east_ref[:, lanes], south_ref[:, lanes], north_ref[:, lanes]], axis=0)
        )
        take(step, dot(edge_ref[...], jnp.concatenate([high, high, low], axis=0)))

    for step in range(8):
        cells_beside(step)

    def forecast_step(step):
        lanes = lanes_of(step)
        level = lax.broadcasted_iota(jnp.int32, (128, 256), 0)
        column = lax.broadcasted_iota(jnp.int32, (128, 256), 1) // 64 + 4 * step
        ones = (level == column).astype(F32).astype(BF16)
        high, low = split(spread_ref[...])
        weights = dot(jnp.concatenate([high, low], axis=1), jnp.concatenate([ones, ones], axis=0))
        side = lax.broadcasted_iota(jnp.int32, (rows_y, 256), 0)
        for x in range(rows_x):
            q = ens_ref[x, :, lanes]
            west = west_ref[:, lanes] if x == 0 else ens_ref[x - 1, :, lanes]
            east = east_ref[:, lanes] if x == rows_x - 1 else ens_ref[x + 1, :, lanes]
            south = jnp.where(side == 0, south_ref[x : x + 1, lanes], pltpu.roll(q, 1, 0))
            north = jnp.where(side == rows_y - 1, north_ref[x : x + 1, lanes], pltpu.roll(q, rows_y - 1, 0))
            total = q
            for k, other in enumerate((west, east, south, north)):
                at = k * cells + x * rows_y
                total = total + weights[at : at + rows_y] * (other - q)
            f_ref[x * rows_y : x * rows_y + rows_y, lanes] = total

    found = found_ref[...]
    turned = pltpu.roll(found, 64, 1)
    left = jnp.where(odd == 0.0, found, turned)
    right = jnp.where(odd == 0.0, turned, found)
    half = n_obs // 2
    side = lax.broadcasted_iota(jnp.int32, (half, 128), 1)
    part_ref[...] = jnp.where(side < 64, left[:half], right[half:])

    share = half // (len(layer) + 1)

    def rows_of(place):
        return pl.ds(pl.multiple_of((lax.rem(place[0], 2) * n_y + place[1]) * share, share), share)

    def send(slot, offset, src, dst, sends, recvs):
        return pltpu.make_async_remote_copy(
            src_ref=src, dst_ref=dst, send_sem=sends.at[slot], recv_sem=recvs.at[slot],
            device_id=place_of(offset), device_id_type=MESH,
        )

    first = [
        send(s, offset, part_ref.at[rows_of(place_of(offset))], got_y_ref.at[s], send_1, recv_1)
        for s, offset in enumerate(layer)
    ]
    for copy in first:
        copy.start()
    order_all()
    tables(gx * rows_x, gy * rows_y, rows_ref, select_ref, across_ref, down_ref, most_ref)
    mine = rows_of((gx, gy))
    total = part_ref[mine, :]
    for s, copy in enumerate(first):
        copy.wait_recv()
        total = total + got_y_ref[s]
    sum_ref[...] = total
    second = [send(s, offset, sum_ref, got_x_ref.at[s], send_2, recv_2) for s, offset in enumerate(stack)]
    for copy in second:
        copy.start()
    for step in range(0, 5):
        forecast_step(step)
    for s, copy in enumerate(second):
        copy.wait_recv()
        total = total + got_x_ref[s]
    total_ref[...] = total
    third = [send(s, offset, total_ref, all_ref.at[mine], send_3, recv_3) for s, offset in enumerate(layer)]
    for copy in third:
        copy.start()
    all_ref[mine, :] = total
    for step in range(5, 8):
        forecast_step(step)
    for copy, sends, _, _ in copies:
        pl.when(sends)(copy.wait_send)
    for copy in first + second:
        copy.wait_send()
    for copy in third:
        copy.wait_recv()
    p_ref[...] = all_ref[...]
    for copy in third:
        copy.wait_send()


def forecast_and_gather(n_x, n_y, ensemble, weights, obs_cell, obs_batch, obs_radius, obs_value, obs_noise, obs_var):
    rows_x, rows_y, width = ensemble.shape
    cells = rows_x * rows_y
    n_obs = obs_batch.shape[0]
    layer, stack = 2 * n_y, n_x // 2
    share = n_obs // 2 // layer
    vmem = pl.BlockSpec(memory_space=pltpu.VMEM)
    dma = pltpu.SemaphoreType.DMA
    return pl.pallas_call(
        functools.partial(forecast_kernel, n_x, n_y),
        out_shape=(
            jax.ShapeDtypeStruct((cells, width), F32),
            jax.ShapeDtypeStruct((n_obs // 2, 128), F32),
            jax.ShapeDtypeStruct((72, n_obs), F32),
            jax.ShapeDtypeStruct((n_obs, 8), F32),
            jax.ShapeDtypeStruct((n_obs, 128), BF16),
            jax.ShapeDtypeStruct((NBATCH * cells, 128), F32),
            jax.ShapeDtypeStruct((NBATCH * LEV // 2, 128), F32),
            jax.ShapeDtypeStruct((8, 128), F32),
        ),
        in_specs=[pl.BlockSpec(memory_space=pltpu.HBM)] * 8,
        out_specs=(vmem,) * 8,
        scratch_shapes=[
            pltpu.VMEM(ensemble.shape, F32),
            pltpu.VMEM(weights.shape, F32),
            pltpu.VMEM(obs_cell.shape, jnp.int32),
            pltpu.VMEM((1, n_obs), jnp.int32),
            pltpu.VMEM((1, n_obs), jnp.int32),
            pltpu.VMEM((2, 1, n_obs), F32),
            pltpu.VMEM((rows_y, width), F32),
            pltpu.VMEM((rows_y, width), F32),
            pltpu.VMEM((rows_x, width), F32),
            pltpu.VMEM((rows_x, width), F32),
            pltpu.VMEM((rows_x, width), F32),
            pltpu.VMEM((rows_x, width), F32),
            pltpu.VMEM((128, n_obs), F32),
            pltpu.VMEM((n_obs, n_obs), BF16),
            pltpu.VMEM((4 * cells, 128), F32),
            pltpu.VMEM((cells, 128), F32),
            pltpu.VMEM((n_obs, 512), BF16),
            pltpu.VMEM((n_obs, 192), BF16),
            pltpu.VMEM((n_obs, 128), F32),
            pltpu.VMEM((n_obs // 2, 128), F32),
            pltpu.VMEM((layer - 1, share, 128), F32),
            pltpu.VMEM((share, 128), F32),
            pltpu.VMEM((stack - 1, share, 128), F32),
            pltpu.VMEM((share, 128), F32),
            pltpu.VMEM((n_obs // 2, 128), F32),
            dma((8,)), dma((4,)), dma((4,)),
            dma((layer - 1,)), dma((layer - 1,)), dma((stack - 1,)), dma((stack - 1,)),
            dma((layer - 1,)), dma((layer - 1,)),
        ],
        compiler_params=pltpu.CompilerParams(
            collective_id=0, has_side_effects=True, vmem_limit_bytes=48 * 1024 * 1024
        ),
        name="forecast_and_gather",
    )(
        *(
            pltpu.with_memory_space_constraint(value, pltpu.HBM)
            for value in (
                ensemble, weights, obs_cell, obs_batch.reshape(1, n_obs), obs_radius.reshape(1, n_obs),
                obs_value.reshape(1, n_obs), obs_var.reshape(1, n_obs), obs_noise,
            )
        )
    )


def solution(mesh):
    n_x, n_y = mesh.shape["gx"], mesh.shape["gy"]

    def body(ensemble, *rest):
        rows_x, rows_y, width = ensemble.shape
        found = forecast_and_gather(n_x, n_y, ensemble, *rest)
        analysis = analyse(
            lambda: (lax.axis_index("gx") * rows_x, lax.axis_index("gy") * rows_y), *found
        )
        return analysis.reshape(rows_x, rows_y, width)

    placed = (P("gx", "gy", None), P(None, "gx", "gy"), P(), P(), P(), P(), P(), P())
    return jax.shard_map(
        body, mesh=mesh, in_specs=placed, out_specs=P("gx", "gy", None), check_vma=False
    )
```

```python
import functools
import jax
import jax.numpy as jnp
from jax import lax
from jax.experimental import pallas as pl
from jax.experimental.pallas import tpu as pltpu
from jax.sharding import PartitionSpec as P

MEM = 64
LEV = 32
OBS_B = 128
HALF = 64
NBATCH = 4
HIGHEST = lax.Precision.HIGHEST
F32 = jnp.float32
BF16 = jnp.bfloat16


def dot(a, b, precision=None):
    return jnp.dot(a, b, preferred_element_type=F32, precision=precision)


def dot_nt(a, b, precision=None):
    return lax.dot_general(
        a, b, (((1,), (1,)), ((), ())), preferred_element_type=F32, precision=precision
    )


def split(value):
    high = value.astype(BF16)
    return high, (value - high.astype(F32)).astype(BF16)


def invert_two(a, b, d):
    inv = 1.0 / (a * d - b * b)
    return d * inv, -b * inv, a * inv


def invert_four(m):
    p00, p01, p11 = invert_two(m[0][0], m[1][0], m[1][1])
    x20, x21 = m[2][0] * p00 + m[2][1] * p01, m[2][0] * p01 + m[2][1] * p11
    x30, x31 = m[3][0] * p00 + m[3][1] * p01, m[3][0] * p01 + m[3][1] * p11
    s22 = m[2][2] - (x20 * m[2][0] + x21 * m[2][1])
    s32 = m[3][2] - (x30 * m[2][0] + x31 * m[2][1])
    s33 = m[3][3] - (x30 * m[3][0] + x31 * m[3][1])
    q22, q32, q33 = invert_two(s22, s32, s33)
    y20, y21 = q22 * x20 + q32 * x30, q22 * x21 + q32 * x31
    y30, y31 = q32 * x20 + q33 * x30, q32 * x21 + q33 * x31
    low = [
        [p00 + (x20 * y20 + x30 * y30)],
        [p01 + (x20 * y21 + x30 * y31), p11 + (x21 * y21 + x31 * y31)],
        [-y20, -y21, q22],
        [-y30, -y31, q32, q33],
    ]
    return [[low[max(i, j)][min(i, j)] for j in range(4)] for i in range(4)]


def total(terms):
    terms = list(terms)
    while len(terms) > 1:
        terms = [sum(terms[i + 1 : i + 2], terms[i]) for i in range(0, len(terms), 2)]
    return terms[0]


def eliminate_eight(rows, block):
    low = 8 * block
    shape = (8, 128)
    four = range(4)
    columns = [
        [jnp.take_along_axis(rows[v][0], jnp.full(shape, low + j, jnp.int32), axis=1, mode='promise_in_bounds') for v in range(block, len(rows))]
        for j in range(8)
    ]

    pivots = [jnp.broadcast_to(rows[block][0][i : i + 1, :], shape) for i in range(8)]

    def entry(i, j):
        return jnp.take_along_axis(
            pivots[i], jnp.full(shape, low + j, jnp.int32), axis=1, mode='promise_in_bounds'
        )

    first = [[entry(i, j) for j in range(i + 1)] for i in four]
    cross = [[entry(4 + i, j) for j in four] for i in four]
    second = [[entry(4 + i, 4 + j) for j in range(i + 1)] for i in four]
    p = invert_four(first)
    x = [[total(cross[i][k] * p[k][j] for k in four) for j in four] for i in four]
    q = invert_four(
        [[second[i][j] - total(x[i][k] * cross[j][k] for k in four) for j in range(i + 1)] for i in four]
    )
    at = lax.broadcasted_iota(jnp.int32, shape, 0)
    result = [list(row) for row in rows]
    for col in range(2):
        r = [jnp.broadcast_to(rows[block][col][i : i + 1, :], shape) for i in range(8)]
        t = [r[4 + i] - total(x[i][k] * r[k] for k in four) for i in four]
        upper = [total(q[i][k] * t[k] for k in four) for i in four]
        lower = [
            total(p[i][k] * r[k] for k in four) - total(x[k][i] * upper[k] for k in four) for i in four
        ]
        solved = lower + upper
        for v in range(block + 1, len(rows)):
            result[v][col] = rows[v][col] - total(columns[k][v - block] * solved[k] for k in range(8))
        if col == 1:
            value = solved[0]
            for k in range(1, 8):
                value = jnp.where(at == k, solved[k], value)
            result[block][1] = value
    return result


def taper_of(dx, dy, dl, radius):
    across = jnp.maximum(1.0 - (dx * dx + dy * dy) / (radius * radius), 0.0)
    return across * across, 1.0 + (dl * 0.125) * (dl * 0.125)


def analysis_kernel(
    axes, f_ref, p_ref, rows_ref, cols_ref, select_ref, across_ref, down_ref, most_ref,
    o_ref, state_ref, near_ref, w1_ref, w2_ref, hor_ref, ver_ref,
):
    cells = f_ref.shape[0]
    start_x, start_y = axes()
    packed = p_ref[...].T
    state_ref[:, 0:256] = packed[:MEM]
    state_ref[:, 256:512] = packed[MEM:]

    def row_of(index, batch):
        return rows_ref[index : index + 1, batch * OBS_B : (batch + 1) * OBS_B]

    def solve_begin(batch):
        low = batch * OBS_B
        prior = state_ref[:, low : low + OBS_B]
        anomaly = prior - jnp.mean(prior, axis=0, keepdims=True)
        variance = row_of(5, batch)
        deviation = jnp.sqrt(variance)
        inv_dev = 1.0 / deviation
        noise = rows_ref[8:72, low : low + OBS_B]
        innovation = row_of(4, batch) + deviation * noise - prior
        scaled = anomaly * (inv_dev * (1.0 / (MEM - 1) ** 0.5))
        both = jnp.concatenate([scaled, innovation * inv_dev], axis=0)
        product = dot_nt(scaled, both, HIGHEST)
        eye = lax.broadcasted_iota(jnp.int32, (64, 128), 0) == lax.broadcasted_iota(jnp.int32, (64, 128), 1)
        system = product + eye.astype(F32)
        rhs = scaled * inv_dev
        rows = [[system[8 * v : 8 * v + 8], rhs[8 * v : 8 * v + 8]] for v in range(8)]
        return anomaly, innovation * (inv_dev * inv_dev), rows

    def near(batch, anomaly):
        low, high = batch * OBS_B, (batch + 1) * OBS_B
        if batch == NBATCH - 1:
            return
        links = dot(anomaly.T, state_ref[:, high:], HIGHEST)
        for later in range(batch + 1, NBATCH):
            cut = slice(later * OBS_B, (later + 1) * OBS_B)
            across, down = taper_of(
                cols_ref[low:high, 0:1] - rows_ref[0:1, cut],
                cols_ref[low:high, 1:2] - rows_ref[1:2, cut],
                cols_ref[low:high, 2:3] - rows_ref[2:3, cut],
                cols_ref[low:high, 3:4],
            )
            at = (later - batch - 1) * OBS_B
            near_ref[:, at : at + OBS_B] = links[:, at : at + OBS_B] * (across / (down * (MEM - 1)))

    def twice(value):
        zero = jnp.zeros(value.shape, value.dtype)
        return jnp.concatenate(
            [jnp.concatenate([value, zero], axis=1), jnp.concatenate([zero, value], axis=1)], axis=0
        )

    def all_begin(batch, anomaly, gain):
        high, low = split(anomaly)
        high_two = twice(high)
        w1_ref[0:128, :] = high_two
        w1_ref[128:256, :] = high_two
        w1_ref[256:384, :] = twice(low)
        high, low = split(gain.T)
        w2_ref[:, 0:128] = twice(high)
        w2_ref[:, 128:256] = twice(low)
        cell = lax.broadcasted_iota(jnp.int32, (cells, 1), 0)
        level = lax.broadcasted_iota(jnp.int32, (LEV, 1), 0).astype(F32)
        cell_x = (cell // 24 + start_x).astype(F32)
        cell_y = (cell % 24 + start_y).astype(F32)
        across, down = taper_of(
            cell_x - row_of(0, batch), cell_y - row_of(1, batch), level - row_of(2, batch), row_of(3, batch)
        )
        hor_ref[...] = across
        ver_ref[...] = 1.0 / (down * (MEM - 1))

    def some_begin(batch, anomaly, gain):
        chosen = select_ref[batch * OBS_B : (batch + 1) * OBS_B, :]
        kept = dot_nt(jnp.concatenate(split(anomaly), axis=0), chosen)
        first = lax.broadcasted_iota(jnp.int32, (MEM, 128), 1) < HALF
        high, low = kept[:MEM], kept[MEM:]
        upper = jnp.concatenate([jnp.where(first, high, 0.0), jnp.where(first, low, 0.0)], axis=1)
        lower = jnp.concatenate([jnp.where(first, 0.0, high), jnp.where(first, 0.0, low)], axis=1)
        both = jnp.concatenate([upper, lower], axis=0).astype(BF16)
        w1_ref[0:128, :] = both
        w1_ref[128:256, :] = both
        high, low = split(gain)
        kept = dot_nt(chosen, jnp.concatenate([high, high, low, low], axis=0))
        slot = lax.broadcasted_iota(jnp.int32, (128, 256), 0) // HALF
        member = (lax.broadcasted_iota(jnp.int32, (128, 256), 1) // MEM) % 2
        both = jnp.where(slot == member, kept, 0.0).astype(BF16)
        w2_ref[0:128, :] = both
        w2_ref[128:256, :] = both

    def lanes_of(step):
        return [pl.ds(step * 256 + 128 * h, 128) for h in range(2)]

    def all_step(batch, src_ref, step):
        lanes = lanes_of(step)
        state = jnp.concatenate([src_ref[:, lanes[0]], src_ref[:, lanes[1]]], axis=0)
        high, low = split(state)
        link = dot(jnp.concatenate([high, low], axis=1), w1_ref[0:256, :]) + dot(high, w1_ref[256:384, :])
        parts = []
        for h in range(2):
            sides = []
            for p in range(2):
                down = ver_ref[pl.ds(4 * step + 2 * h + p, 1), :]
                sides.append(
                    link[h * cells : (h + 1) * cells, p * 128 : p * 128 + 128] * hor_ref[...] * down
                )
            parts.append(jnp.concatenate(sides, axis=1))
        high, low = split(jnp.concatenate(parts, axis=0))
        wide = dot(high, w2_ref[...])
        state = state + (wide[:, :128] + wide[:, 128:] + dot(low, w2_ref[:, 0:128]))
        for h in range(2):
            o_ref[:, lanes[h]] = state[h * cells : (h + 1) * cells]

    def some_step(batch, src_ref, step):
        lanes = lanes_of(step)
        state = jnp.concatenate([src_ref[:, lanes[0]], src_ref[:, lanes[1]]], axis=0)
        link = dot(jnp.concatenate(split(state), axis=1), w1_ref[0:256, :])
        parts = []
        for h in range(2):
            rows = slice(h * cells, (h + 1) * cells)
            down = down_ref[pl.ds(16 * batch + 2 * step + h, 1), :]
            across = across_ref[batch * cells : (batch + 1) * cells, :]
            parts.append((link[rows, :128] + link[rows, 128:]) * (across * down))
        wide = dot(jnp.concatenate(split(jnp.concatenate(parts, axis=0)), axis=1), w2_ref[...])
        state = state + (wide[:, :128] + wide[:, 128:])
        for h in range(2):
            o_ref[:, lanes[h]] = state[h * cells : (h + 1) * cells]

    def process(begin, tile_step):
        anomaly = None
        for batch in range(NBATCH + 1):
            if batch < NBATCH:
                anomaly, direct, rows = solve_begin(batch)
                near(batch, anomaly)
            for step in range(8):
                if batch > 0:
                    tile_step(batch - 1, f_ref if batch == 1 else o_ref, step)
                if batch < NBATCH:
                    rows = eliminate_eight(rows, step)
            if batch < NBATCH:
                left = jnp.concatenate([row[0] for row in rows], axis=0).T[64:]
                right = jnp.concatenate([row[1] for row in rows], axis=0)
                gain = direct - dot(left, right, HIGHEST)
                if batch < NBATCH - 1:
                    high = (batch + 1) * OBS_B
                    state_ref[:, high:] = state_ref[:, high:] + dot(
                        gain, near_ref[:, : NBATCH * OBS_B - high], HIGHEST
                    )
                begin(batch, anomaly, gain)

    fits = jnp.max(most_ref[...]) <= HALF

    @pl.when(fits)
    def _():
        process(some_begin, some_step)

    @pl.when(jnp.logical_not(fits))
    def _():
        process(all_begin, all_step)


def analyse(axes, forecast, *rest):
    cells = forecast.shape[0]
    return pl.pallas_call(
        functools.partial(analysis_kernel, axes),
        out_shape=jax.ShapeDtypeStruct(forecast.shape, F32),
        in_specs=[pl.BlockSpec(memory_space=pltpu.VMEM)] * 8,
        out_specs=pl.BlockSpec(memory_space=pltpu.VMEM),
        scratch_shapes=[
            pltpu.VMEM((MEM, NBATCH * OBS_B), F32),
            pltpu.VMEM((OBS_B, (NBATCH - 1) * OBS_B), F32),
            pltpu.VMEM((384, 256), BF16),
            pltpu.VMEM((256, 256), BF16),
            pltpu.VMEM((cells, OBS_B), F32),
            pltpu.VMEM((LEV, OBS_B), F32),
        ],
        compiler_params=pltpu.CompilerParams(vmem_limit_bytes=48 * 1024 * 1024),
        name="analysis",
    )(forecast, *rest)


MESH = pl.DeviceIdType.MESH


def tables(start_x, start_y, rows_ref, select_ref, across_ref, down_ref, most_ref):
    cells = across_ref.shape[0] // NBATCH
    most = jnp.zeros((8, 128), F32)
    square = (128, 128)
    before = (
        lax.broadcasted_iota(jnp.int32, square, 0) < lax.broadcasted_iota(jnp.int32, square, 1)
    ).astype(F32).astype(BF16)
    slot = (lax.broadcasted_iota(jnp.int32, square, 0) % HALF).astype(F32)
    cell = lax.broadcasted_iota(jnp.int32, (cells, 128), 0)
    cell_x, cell_y = (cell // 24).astype(F32), (cell % 24).astype(F32)
    level = 2 * lax.broadcasted_iota(jnp.int32, (LEV // 2, 128), 0)
    level = (level + lax.broadcasted_iota(jnp.int32, (LEV // 2, 128), 1) // HALF).astype(F32)
    kind = lax.broadcasted_iota(jnp.int32, (8, 128), 0)
    for batch in range(NBATCH):
        low = batch * OBS_B
        x, y, l, r = (rows_ref[i : i + 1, low : low + OBS_B] for i in range(4))
        x, y = x - start_x.astype(F32), y - start_y.astype(F32)
        dx = jnp.maximum(jnp.maximum(-x, x - 7.0), 0.0)
        dy = jnp.maximum(jnp.maximum(-y, y - 23.0), 0.0)
        reaches = dx * dx + dy * dy < r * r
        flags = jnp.broadcast_to(reaches.astype(F32), (8, 128))
        position = dot(flags.astype(BF16), before)[0:1]
        most = jnp.maximum(most, jnp.sum(flags, axis=1, keepdims=True))
        chosen = jnp.where((slot == position) & reaches, 1.0, 0.0).astype(BF16)
        select_ref[low : low + OBS_B, :] = chosen
        facts = jnp.where(kind == 0, x, jnp.where(kind == 1, y, jnp.where(kind == 2, l, jnp.where(kind == 3, r, 1.0))))
        kept = dot_nt(facts.astype(BF16), chosen)
        across, down = taper_of(
            cell_x - kept[0:1], cell_y - kept[1:2], level - kept[2:3], kept[3:4] + (1.0 - kept[4:5])
        )
        across_ref[batch * cells : (batch + 1) * cells, :] = across
        down_ref[batch * LEV // 2 : (batch + 1) * LEV // 2, :] = 1.0 / (down * (MEM - 1))
    most_ref[...] = most


def forecast_kernel(
    n_x, n_y,
    ens_hbm, w_hbm, cell_hbm, batch_hbm, radius_hbm, value_hbm, var_hbm, noise_hbm,
    f_ref, p_ref, rows_ref, cols_ref, select_ref, across_ref, down_ref, most_ref,
    ens_ref, w_ref, cell_ref, batch_ref, ints_ref, floats_ref,
    west_ref, east_ref, south_ref, north_ref, first_ref, last_ref,
    data_ref, chosen_ref, spread_ref, point_ref, mix_ref, edge_ref, found_ref,
    part_ref, got_y_ref, sum_ref, got_x_ref, total_ref, all_ref,
    loads, halo_send, halo_recv, send_1, recv_1, send_2, recv_2, send_3, recv_3,
):
    gx, gy = lax.axis_index("gx"), lax.axis_index("gy")
    rows_x, rows_y = ens_ref.shape[0], ens_ref.shape[1]
    cells = rows_x * rows_y
    n_obs = batch_ref.shape[1]

    n_z, n_side = n_x // 2, 4
    z, core, column, line = lax.div(gx, 2), lax.rem(gx, 2), lax.div(gy, n_side), lax.rem(gy, n_side)

    def hops(offset):
        return min(offset[0], n_z - offset[0]) + sum(min(d, n_side - d) for d in offset[2:]) + 0.1 * offset[1]

    layer = [(0, c, x, y) for c in range(2) for x in range(n_y // n_side) for y in range(n_side)][1:]
    layer = sorted(layer, key=hops, reverse=True)
    stack = sorted([(d, 0, 0, 0) for d in range(1, n_z)], key=hops, reverse=True)

    def place_of(offset):
        return (
            2 * lax.rem(z + offset[0], n_z) + lax.rem(core + offset[1], 2),
            n_side * lax.rem(column + offset[2], n_y // n_side) + lax.rem(line + offset[3], n_side),
        )

    small = [
        pltpu.make_async_copy(src, dst, loads.at[i])
        for i, (src, dst) in enumerate(
            (
                (batch_hbm, batch_ref),
                (cell_hbm, cell_ref),
                (noise_hbm, data_ref.at[8:72]),
                (radius_hbm, ints_ref),
                (value_hbm, floats_ref.at[0]),
                (var_hbm, floats_ref.at[1]),
            )
        )
    ]
    load_weights = pltpu.make_async_copy(w_hbm, w_ref, loads.at[6])
    load_tile = pltpu.make_async_copy(ens_hbm, ens_ref, loads.at[7])
    for copy in small:
        copy.start()
    load_tile.start()
    load_weights.start()

    barrier = pltpu.get_barrier_semaphore()
    beside_x = lax.rem(gx + 2 * core - 1 + n_x, n_x)
    for other in [(beside_x, gy)] + [place_of(offset) for offset in layer + stack]:
        pl.semaphore_signal(barrier, inc=1, device_id=other, device_id_type=MESH)

    square = (n_obs, n_obs)
    at_row, at_lane = lax.broadcasted_iota(jnp.int32, square, 0), lax.broadcasted_iota(jnp.int32, square, 1)
    before = (at_row < at_lane).astype(F32).astype(BF16)
    kind = lax.broadcasted_iota(jnp.int32, (8, n_obs), 0)
    for copy in small[:2]:
        copy.wait()
    same = (kind == batch_ref[...]).astype(F32)
    count = dot(same.astype(BF16), before)
    rank = jnp.sum(same * (count + (kind * OBS_B).astype(F32)), axis=0, keepdims=True)
    chosen_ref[...] = (at_row.astype(F32) == rank).astype(F32).astype(BF16)
    cell = cell_ref[...].astype(F32)
    half_y = jnp.floor(cell[1:2] * 0.5)
    facts = jnp.where(kind == 2, cell[1:2] - 2.0 * half_y, jnp.where(kind == 3, cell[2:3], 0.0))
    facts = jnp.where(kind == 0, cell[0:1], jnp.where(kind == 1, half_y, facts))
    where = dot_nt(chosen_ref[...], facts.astype(BF16))

    def order_all():
        for copy in small[2:]:
            copy.wait()
        data_ref[0:3, :] = cell_ref[...].astype(F32)
        data_ref[3:4, :] = ints_ref[...].astype(F32)
        data_ref[4:5, :] = floats_ref[0]
        data_ref[5:6, :] = floats_ref[1]
        data_ref[6:8, :] = jnp.zeros((2, n_obs), F32)
        data_ref[72:128, :] = jnp.zeros((56, n_obs), F32)
        data = data_ref[...]
        high = data.astype(BF16)
        middle, low = split(data - high.astype(F32))
        thirds = dot_nt(chosen_ref[...], jnp.concatenate([high, middle, low], axis=0))
        table = (thirds[:, 0:128] + thirds[:, 128:256]) + thirds[:, 256:384]
        cols_ref[...] = table[:, 0:8]
        rows_ref[...] = table.T[0:72]

    load_tile.wait()
    for x in range(rows_x):
        first_ref[x : x + 1, :] = ens_ref[x, 0:1, :]
        last_ref[x : x + 1, :] = ens_ref[x, rows_y - 1 : rows_y, :]

    pl.semaphore_wait(barrier, len(layer) + len(stack) + 1)

    def halo(slot, src, dst, axis, target):
        return pltpu.make_async_remote_copy(
            src_ref=src, dst_ref=dst, send_sem=halo_send.at[slot], recv_sem=halo_recv.at[slot],
            device_id={axis: target}, device_id_type=MESH,
        )

    copies = (
        (halo(0, ens_ref.at[rows_x - 1], west_ref, "gx", lax.rem(gx + 1, n_x)), gx < n_x - 1, gx > 0, west_ref),
        (halo(1, ens_ref.at[0], east_ref, "gx", lax.rem(gx + n_x - 1, n_x)), gx > 0, gx < n_x - 1, east_ref),
        (halo(2, last_ref, south_ref, "gy", lax.rem(gy + 1, n_y)), gy < n_y - 1, gy > 0, south_ref),
        (halo(3, first_ref, north_ref, "gy", lax.rem(gy + n_y - 1, n_y)), gy > 0, gy < n_y - 1, north_ref),
    )
    for copy, sends, _, _ in copies:
        pl.when(sends)(copy.start)

    load_weights.wait()
    for y in range(rows_y):
        merged = jnp.zeros((rows_x, 128), F32)
        group = lax.broadcasted_iota(jnp.int32, (rows_x, 128), 1) // LEV
        for k in range(4):
            block = w_ref[k, :, 128 * (y // 4) : 128 * (y // 4) + 128]
            low_lanes = pltpu.roll(block, 128 - 32 * (y % 4), 1) if y % 4 else block
            spread_ref[pl.ds(k * cells + y, rows_x, stride=rows_y), :] = low_lanes
            turn = (32 * k - 32 * (y % 4)) % 128
            merged = jnp.where(group == k, pltpu.roll(block, turn, 1) if turn else block, merged)
        point_ref[pl.ds(y, rows_x, stride=rows_y), :] = merged

    obs_x = where[:, 0:1] - (gx * rows_x).astype(F32)
    obs_y = 2.0 * where[:, 1:2] + where[:, 2:3] - (gy * rows_y).astype(F32)
    obs_l = where[:, 3:4]
    inside = (obs_x >= 0.0) & (obs_x < rows_x) & (obs_y >= 0.0) & (obs_y < rows_y)

    def place(value):
        return jnp.where(inside, value, -1.0)

    centre = obs_x * rows_y + obs_y
    at_west = place(jnp.where(obs_x > 0.0, centre - rows_y, cells + obs_y))
    at_east = place(jnp.where(obs_x < rows_x - 1.0, centre + rows_y, cells + rows_y + obs_y))
    at_south = place(jnp.where(obs_y > 0.0, centre - 1.0, cells + 2 * rows_y + obs_x))
    at_north = place(jnp.where(obs_y < rows_y - 1.0, centre + 1.0, cells + 2 * rows_y + rows_x + obs_x))
    centre = place(centre)
    lane = lax.broadcasted_iota(jnp.int32, (n_obs, 256), 1).astype(F32)
    is_centre = lane == centre
    high, low = split(point_ref[...])
    both = dot(
        is_centre.astype(F32).astype(BF16)[:, 0:cells], jnp.concatenate([high, low], axis=1)
    )
    mine = both[:, 0:128] + both[:, 128:256]
    lane_level = lax.broadcasted_iota(jnp.int32, (n_obs, 128), 1) % LEV
    mine = jnp.where(lane_level.astype(F32) == obs_l, mine, 0.0)
    high, low = split(mine)
    group = lax.broadcasted_iota(jnp.int32, (128, 512), 0) // LEV == lax.broadcasted_iota(jnp.int32, (128, 512), 1) // 128
    group = group.astype(F32).astype(BF16)
    coeffs = dot(jnp.concatenate([high, low], axis=1), jnp.concatenate([group, group], axis=0))
    coeffs = [jnp.concatenate([coeffs[:, 128 * k : 128 * k + 128]] * 2, axis=1) for k in range(4)]
    mix = jnp.where(is_centre, 1.0 - ((coeffs[0] + coeffs[1]) + (coeffs[2] + coeffs[3])), 0.0)
    for k, at in enumerate((at_west, at_east, at_south, at_north)):
        mix = jnp.where(lane == at, coeffs[k], mix)
    high, low = split(mix)
    mix_ref[:, 0:256] = high
    mix_ref[:, 256:512] = low
    edge_ref[:, 0:64] = high[:, 192:256]
    edge_ref[:, 64:128] = low[:, 192:256]
    edge_ref[:, 128:192] = high[:, 192:256]
    pair = jnp.floor(obs_l * 0.5)
    odd = obs_l - 2.0 * pair
    found_ref[...] = jnp.zeros(found_ref.shape, F32)

    def take(step, here):
        found = found_ref[...]
        for h in range(2):
            found = jnp.where(
                pair == 2.0 * step + h, found + here[:, h * 128 : h * 128 + 128], found
            )
        found_ref[...] = found

    def lanes_of(step):
        return pl.ds(step * 256, 256)

    def own_cells(step):
        high, low = split(ens_ref[:, :, lanes_of(step)].reshape(cells, 256))
        take(
            step,
            dot(mix_ref[:, 0:cells], high)
            + dot(mix_ref[:, 256 : 256 + cells], high)
            + dot(mix_ref[:, 0:cells], low),
        )

    for step in range(8):
        own_cells(step)

    for copy, _, receives, halo_ref in copies:
        pl.when(receives)(copy.wait_recv)

        @pl.when(jnp.logical_not(receives))
        def _():
            halo_ref[...] = jnp.zeros(halo_ref.shape, F32)

    def cells_beside(step):
        lanes = lanes_of(step)
        high, low = split(
            jnp.concatenate([west_ref[:, lanes], east_ref[:, lanes], south_ref[:, lanes], north_ref[:, lanes]], axis=0)
        )
        take(step, dot(edge_ref[...], jnp.concatenate([high, high, low], axis=0)))

    for step in range(8):
        cells_beside(step)

    def forecast_step(step):
        lanes = lanes_of(step)
        level = lax.broadcasted_iota(jnp.int32, (128, 256), 0)
        column = lax.broadcasted_iota(jnp.int32, (128, 256), 1) // 64 + 4 * step
        ones = (level == column).astype(F32).astype(BF16)
        high, low = split(spread_ref[...])
        weights = dot(jnp.concatenate([high, low], axis=1), jnp.concatenate([ones, ones], axis=0))
        side = lax.broadcasted_iota(jnp.int32, (rows_y, 256), 0)
        for x in range(rows_x):
            q = ens_ref[x, :, lanes]
            west = west_ref[:, lanes] if x == 0 else ens_ref[x - 1, :, lanes]
            east = east_ref[:, lanes] if x == rows_x - 1 else ens_ref[x + 1, :, lanes]
            south = jnp.where(side == 0, south_ref[x : x + 1, lanes], pltpu.roll(q, 1, 0))
            north = jnp.where(side == rows_y - 1, north_ref[x : x + 1, lanes], pltpu.roll(q, rows_y - 1, 0))
            total = q
            for k, other in enumerate((west, east, south, north)):
                at = k * cells + x * rows_y
                total = total + weights[at : at + rows_y] * (other - q)
            f_ref[x * rows_y : x * rows_y + rows_y, lanes] = total

    found = found_ref[...]
    turned = pltpu.roll(found, 64, 1)
    left = jnp.where(odd == 0.0, found, turned)
    right = jnp.where(odd == 0.0, turned, found)
    half = n_obs // 2
    side = lax.broadcasted_iota(jnp.int32, (half, 128), 1)
    part_ref[...] = jnp.where(side < 64, left[:half], right[half:])

    share = half // (len(layer) + 1)

    def rows_of(place):
        return pl.ds(pl.multiple_of((lax.rem(place[0], 2) * n_y + place[1]) * share, share), share)

    def send(slot, offset, src, dst, sends, recvs):
        return pltpu.make_async_remote_copy(
            src_ref=src, dst_ref=dst, send_sem=sends.at[slot], recv_sem=recvs.at[slot],
            device_id=place_of(offset), device_id_type=MESH,
        )

    first = [
        send(s, offset, part_ref.at[rows_of(place_of(offset))], got_y_ref.at[s], send_1, recv_1)
        for s, offset in enumerate(layer)
    ]
    for copy in first:
        copy.start()
    order_all()
    tables(gx * rows_x, gy * rows_y, rows_ref, select_ref, across_ref, down_ref, most_ref)
    mine = rows_of((gx, gy))
    total = part_ref[mine, :]
    for s, copy in enumerate(first):
        copy.wait_recv()
        total = total + got_y_ref[s]
    sum_ref[...] = total
    second = [send(s, offset, sum_ref, got_x_ref.at[s], send_2, recv_2) for s, offset in enumerate(stack)]
    for copy in second:
        copy.start()
    for step in range(0, 5):
        forecast_step(step)
    for s, copy in enumerate(second):
        copy.wait_recv()
        total = total + got_x_ref[s]
    total_ref[...] = total
    third = [send(s, offset, total_ref, all_ref.at[mine], send_3, recv_3) for s, offset in enumerate(layer)]
    for copy in third:
        copy.start()
    all_ref[mine, :] = total
    for step in range(5, 8):
        forecast_step(step)
    for copy, sends, _, _ in copies:
        pl.when(sends)(copy.wait_send)
    for copy in first + second:
        copy.wait_send()
    for copy in third:
        copy.wait_recv()
    p_ref[...] = all_ref[...]
    for copy in third:
        copy.wait_send()


def forecast_and_gather(n_x, n_y, ensemble, weights, obs_cell, obs_batch, obs_radius, obs_value, obs_noise, obs_var):
    rows_x, rows_y, width = ensemble.shape
    cells = rows_x * rows_y
    n_obs = obs_batch.shape[0]
    layer, stack = 2 * n_y, n_x // 2
    share = n_obs // 2 // layer
    vmem = pl.BlockSpec(memory_space=pltpu.VMEM)
    dma = pltpu.SemaphoreType.DMA
    return pl.pallas_call(
        functools.partial(forecast_kernel, n_x, n_y),
        out_shape=(
            jax.ShapeDtypeStruct((cells, width), F32),
            jax.ShapeDtypeStruct((n_obs // 2, 128), F32),
            jax.ShapeDtypeStruct((72, n_obs), F32),
            jax.ShapeDtypeStruct((n_obs, 8), F32),
            jax.ShapeDtypeStruct((n_obs, 128), BF16),
            jax.ShapeDtypeStruct((NBATCH * cells, 128), F32),
            jax.ShapeDtypeStruct((NBATCH * LEV // 2, 128), F32),
            jax.ShapeDtypeStruct((8, 128), F32),
        ),
        in_specs=[pl.BlockSpec(memory_space=pltpu.HBM)] * 8,
        out_specs=(vmem,) * 8,
        scratch_shapes=[
            pltpu.VMEM(ensemble.shape, F32),
            pltpu.VMEM(weights.shape, F32),
            pltpu.VMEM(obs_cell.shape, jnp.int32),
            pltpu.VMEM((1, n_obs), jnp.int32),
            pltpu.VMEM((1, n_obs), jnp.int32),
            pltpu.VMEM((2, 1, n_obs), F32),
            pltpu.VMEM((rows_y, width), F32),
            pltpu.VMEM((rows_y, width), F32),
            pltpu.VMEM((rows_x, width), F32),
            pltpu.VMEM((rows_x, width), F32),
            pltpu.VMEM((rows_x, width), F32),
            pltpu.VMEM((rows_x, width), F32),
            pltpu.VMEM((128, n_obs), F32),
            pltpu.VMEM((n_obs, n_obs), BF16),
            pltpu.VMEM((4 * cells, 128), F32),
            pltpu.VMEM((cells, 128), F32),
            pltpu.VMEM((n_obs, 512), BF16),
            pltpu.VMEM((n_obs, 192), BF16),
            pltpu.VMEM((n_obs, 128), F32),
            pltpu.VMEM((n_obs // 2, 128), F32),
            pltpu.VMEM((layer - 1, share, 128), F32),
            pltpu.VMEM((share, 128), F32),
            pltpu.VMEM((stack - 1, share, 128), F32),
            pltpu.VMEM((share, 128), F32),
            pltpu.VMEM((n_obs // 2, 128), F32),
            dma((8,)), dma((4,)), dma((4,)),
            dma((layer - 1,)), dma((layer - 1,)), dma((stack - 1,)), dma((stack - 1,)),
            dma((layer - 1,)), dma((layer - 1,)),
        ],
        compiler_params=pltpu.CompilerParams(
            collective_id=0, has_side_effects=True, vmem_limit_bytes=48 * 1024 * 1024
        ),
        name="forecast_and_gather",
    )(
        *(
            pltpu.with_memory_space_constraint(value, pltpu.HBM)
            for value in (
                ensemble, weights, obs_cell, obs_batch.reshape(1, n_obs), obs_radius.reshape(1, n_obs),
                obs_value.reshape(1, n_obs), obs_var.reshape(1, n_obs), obs_noise,
            )
        )
    )


def solution(mesh):
    n_x, n_y = mesh.shape["gx"], mesh.shape["gy"]

    def body(ensemble, *rest):
        rows_x, rows_y, width = ensemble.shape
        found = forecast_and_gather(n_x, n_y, ensemble, *rest)
        analysis = analyse(
            lambda: (lax.axis_index("gx") * rows_x, lax.axis_index("gy") * rows_y), *found
        )
        return analysis.reshape(rows_x, rows_y, width)

    placed = (P("gx", "gy", None), P(None, "gx", "gy"), P(), P(), P(), P(), P(), P())
    return jax.shard_map(
        body, mesh=mesh, in_specs=placed, out_specs=P("gx", "gy", None), check_vma=False
    )
```
